128 devices in a mesh: ctx: 32 (over z_hi, y, x), ws: 4 (over z_lo, core).
Axes of the slice: x: 4, y: 4, z: 4 (z_hi: 2, z_lo: 2; z = z_hi * 2 + z_lo), core: 2. Of those that a mesh axis runs over, the one named last changes fastest.
Arguments:
- hidden_in: bfloat16 [8192, 2048], P('ctx'), may hold values from -6 to 6
- grad_out: bfloat16 [8192, 2048], P('ctx'), may hold values from -6 to 6
- block_ids: int32 [64], replicated, may hold values from 0 to 63, as said below
- expert_ids: int32 [8192, 6], P('ctx'), may hold values from 0 to 63, all different within a row
- claim_order: int32 [8192], P('ctx'), may hold values from 0 to 255, as said below
- attn_gain: bfloat16 [2048], P(('ctx', 'ws')), may hold values from 0.5 to 1.5
- latent_gain: bfloat16 [512], P(('ctx', 'ws')), may hold values from 0.5 to 1.5
- ffn_gain: bfloat16 [2048], P(('ctx', 'ws')), may hold values from 0.5 to 1.5
- query_weight: bfloat16 [2048, 3072], P('ctx', 'ws'), may hold values from -0.125 to 0.125
- latent_down: bfloat16 [2048, 576], P('ws', 'ctx'), may hold values from -0.125 to 0.125
- latent_up: bfloat16 [512, 4096], P('ctx', 'ws'), may hold values from -0.25 to 0.25
- output_weight: bfloat16 [2048, 2048], P('ws', 'ctx'), may hold values from -1.5 to 1.5
- router_weight: bfloat16 [2048, 64], P('ws', 'ctx'), may hold values from -0.0625 to 0.0625
- expert_gate: bfloat16 [64, 2048, 1408], P('ctx', None, 'ws'), may hold values from -0.125 to 0.125
- expert_up: bfloat16 [64, 2048, 1408], P('ctx', None, 'ws'), may hold values from -0.125 to 0.125
- expert_down: bfloat16 [64, 1408, 2048], P('ctx', 'ws'), may hold values from -6 to 6
- shared_gate: bfloat16 [2048, 2816], P('ctx', 'ws'), may hold values from -0.125 to 0.125
- shared_up: bfloat16 [2048, 2816], P('ctx', 'ws'), may hold values from -0.125 to 0.125
- shared_down: bfloat16 [2816, 2048], P('ws', 'ctx'), may hold values from -0.109375 to 0.109375
Outputs:
- layer_out: bfloat16 [8192, 2048], P('ctx', 'ws')
- grad_in: float32 [8192, 2048], P('ctx', 'ws')
- grad_attn_gain: float32 [2048], P(('ctx', 'ws'))
- grad_latent_gain: float32 [512], P(('ctx', 'ws'))
- grad_ffn_gain: float32 [2048], P(('ctx', 'ws'))
- grad_query: float32 [2048, 3072], P('ctx', 'ws')
- grad_latent_down: float32 [2048, 576], P('ws', 'ctx')
- grad_latent_up: float32 [512, 4096], P('ctx', 'ws')
- grad_output_weight: float32 [2048, 2048], P('ws', 'ctx')
- grad_router: float32 [2048, 64], P('ws', 'ctx')
- grad_expert_gate: float32 [64, 2048, 1408], P('ctx', None, 'ws')
- grad_expert_up: float32 [64, 2048, 1408], P('ctx', None, 'ws')
- grad_expert_down: float32 [64, 1408, 2048], P('ctx', 'ws')
- grad_shared_gate: float32 [2048, 2816], P('ctx', 'ws')
- grad_shared_up: float32 [2048, 2816], P('ctx', 'ws')
- grad_shared_down: float32 [2816, 2048], P('ws', 'ctx')
The draws below stay inside these ranges and needn't reach their ends.
Inputs may be any that keep to these rules, and one draw needn't show every extreme that they name: Stored block j of the stream is global block block_ids[j] = s * 16 + b, block b of sequence s; every block appears once. Stored blocks 2i and 2i + 1 are blocks b and 15 - b of one sequence, in either order. `expert_ids`: each row names 6 different experts. `claim_order`: within the 256 rows of each index of ctx, a permutation of 0 to 255.
All inputs are finite; a program needn't handle non-finite values.
Results may differ from the reference program's by a relative error of at most 0.028.
Values may be sent and summed in bfloat16 or wider, within the bound.
No kernel may reach another device: no remote copies, remote signals or barrier semaphores. Data moves between devices by JAX's collectives and lax.ppermute only.
A program may use at most 320 MiB of HBM per device.

```python
import jax
import jax.numpy as jnp
from jax import lax

D = 2048
H = 16
NOPE = 128
ROPE = 64
VDIM = 128
RANK = 512
FF_EXP = 1408
FF_SH = 2816
TOPK = 6
EXPERTS = 64
TOK_CTX = 256
BLOCK = 128
LENGTH = 2048
TOKENS = 8192
SEQS = 4
BLOCKS = 64
BLOCKS_SEQ = 16
CAP = 30
N_CTX = 32


def draw_block_ids(key, part):
    key = jax.random.fold_in(key, 11)
    pair_total = TOKENS // (2 * BLOCK)
    per_seq = LENGTH // (2 * BLOCK)
    seq_blocks = LENGTH // BLOCK
    seq_total = TOKENS // LENGTH
    key_one, key_two, key_three, key_four = jax.random.split(key, 4)
    chosen_seq = jax.random.randint(key_one, (), 0, seq_total)
    inner_order = jax.random.permutation(key_two, per_seq)
    special = chosen_seq * per_seq + inner_order[:3]
    pair_range = jnp.arange(pair_total)
    is_special = jnp.any(pair_range[:, None] == special[None, :], axis=1).astype(jnp.int32)
    shuffled = jax.random.permutation(key_three, pair_total)
    pair_order = jnp.argsort(is_special * pair_total + shuffled)
    slot_special = ((pair_range == 0) | (pair_range == pair_total // 2) | (pair_range == pair_total - 1)).astype(jnp.int32)
    slot_order = jnp.argsort(slot_special * pair_total + pair_range)
    pair_at_slot = jnp.zeros((pair_total,), jnp.int32).at[slot_order].set(pair_order.astype(jnp.int32))
    sequence = pair_at_slot // per_seq
    within = pair_at_slot % per_seq
    early = sequence * seq_blocks + within
    late = sequence * seq_blocks + seq_blocks - 1 - within
    flipped = jax.random.randint(key_four, (pair_total,), 0, 2)
    first_block = jnp.where(flipped == 1, late, early)
    second_block = jnp.where(flipped == 1, early, late)
    return jnp.stack([first_block, second_block], axis=1).reshape(-1).astype(jnp.int32)


def draw_claim_order(key, part):
    key = jax.random.fold_in(key, 7)
    scores = jax.random.randint(key, (TOKENS // TOK_CTX, TOK_CTX), 0, 131072) * TOK_CTX + jnp.arange(TOK_CTX)[None, :]
    return jnp.argsort(jnp.argsort(scores, axis=1), axis=1).astype(jnp.int32).reshape(-1)


def block_scale(key, shape, cuts, smallest, top_value):
    def one(position, blocks):
        heights = jax.random.uniform(jax.random.fold_in(jax.random.fold_in(key, 6), position), (blocks,), jnp.float32, smallest / len(cuts), top_value / len(cuts))
        return jnp.repeat(jnp.exp(heights), shape[position] // blocks).reshape((-1,) + (1,) * (len(shape) - position - 1))

    factor_of = one(*cuts[0])
    for cut in cuts[1:]:
        factor_of = factor_of * one(*cut)
    return factor_of


def distinct(key, rows, amount, top, lift):
    order = jax.random.permutation(jax.random.fold_in(key, 1), amount)
    pull = order
    for power in range(3):
        pull = pull * pull // amount
    pull = pull * lift // amount
    tickets = jax.random.randint(jax.random.fold_in(key, 2), (rows, amount), 0, 4096) + pull
    sure = jax.random.permutation(jax.random.fold_in(key, 3), rows)[jnp.arange(amount) % rows]
    tickets = jnp.where(jnp.arange(rows)[:, None] == sure[None, :], 1 << 14, tickets)
    merit = tickets * amount + jnp.arange(amount)
    return lax.top_k(merit.astype(jnp.int32), top)[1].astype(jnp.int32)


def bell_draw(rng, dims, width, most, cuts=(), kind=jnp.bfloat16):
    gain = block_scale(rng, dims, cuts, -0.22, 0.18) if cuts else 1.0
    entries = jax.random.normal(rng, dims, jnp.float32) * width * gain
    return jnp.minimum(jnp.maximum(entries, -most), most).astype(kind)


def setup_inputs(seed: int = 0) -> dict:
    seeds = jax.random.split(jax.random.key(seed), 20)
    hidden_in = bell_draw(seeds[0], (TOKENS, D), 1.0, 6.0, ((0, 32),))
    grad_out = bell_draw(seeds[1], (TOKENS, D), 1.0, 6.0, ((0, 32),))
    block_ids = draw_block_ids(jax.random.fold_in(seeds[19], 71), 0)
    expert_ids = distinct(seeds[3], TOKENS, EXPERTS, TOPK, 768)
    claim_order = draw_claim_order(jax.random.fold_in(seeds[19], 71), 0)
    attn_gain = jnp.clip(1.0 + 0.1 * jax.random.normal(seeds[5], (D,), jnp.float32), 0.5, 1.5).astype(jnp.bfloat16)
    latent_gain = jnp.clip(1.0 + 0.1 * jax.random.normal(seeds[6], (RANK,), jnp.float32), 0.5, 1.5).astype(jnp.bfloat16)
    ffn_gain = jnp.clip(1.0 + 0.1 * jax.random.normal(seeds[7], (D,), jnp.float32), 0.5, 1.5).astype(jnp.bfloat16)
    query_weight = bell_draw(seeds[8], (D, H * (NOPE + ROPE)), D ** -0.5, 0.125, ((0, 32), (1, 4)))
    latent_down = bell_draw(seeds[9], (D, RANK + ROPE), D ** -0.5, 0.125, ((0, 4), (1, 32)))
    latent_up = bell_draw(seeds[10], (RANK, H * (NOPE + VDIM)), RANK ** -0.5, 0.25, ((0, 32), (1, 4)))
    output_weight = bell_draw(seeds[11], (H * VDIM, D), (H * VDIM // 128) ** -0.5, 1.5, ((0, 4), (1, 32)))
    router_weight = bell_draw(seeds[12], (D, EXPERTS), (4 * D) ** -0.5, 0.0625, ((0, 4), (1, 32)))
    expert_gate = bell_draw(seeds[13], (EXPERTS, D, FF_EXP), D ** -0.5, 0.125, ((0, 32), (2, 4)))
    expert_up = bell_draw(seeds[14], (EXPERTS, D, FF_EXP), D ** -0.5, 0.125, ((0, 32), (2, 4)))
    expert_down = bell_draw(seeds[15], (EXPERTS, FF_EXP, D), (EXPERTS / (2 * (3 * FF_EXP) ** 0.5)), 6.0, ((0, 32), (1, 4)))
    shared_gate = bell_draw(seeds[16], (D, FF_SH), D ** -0.5, 0.125, ((0, 32), (1, 4)))
    shared_up = bell_draw(seeds[17], (D, FF_SH), D ** -0.5, 0.125, ((0, 32), (1, 4)))
    shared_down = bell_draw(seeds[18], (FF_SH, D), FF_SH ** -0.5, 0.109375, ((0, 4), (1, 32)))
    return dict(hidden_in=hidden_in, grad_out=grad_out, block_ids=block_ids, expert_ids=expert_ids, claim_order=claim_order, attn_gain=attn_gain, latent_gain=latent_gain, ffn_gain=ffn_gain, query_weight=query_weight, latent_down=latent_down, latent_up=latent_up, output_weight=output_weight, router_weight=router_weight, expert_gate=expert_gate, expert_up=expert_up, expert_down=expert_down, shared_gate=shared_gate, shared_up=shared_up, shared_down=shared_down)


EPSILON = 1e-06
ROPE_BASE = 10000.0
HIGHEST = lax.Precision.HIGHEST

@jax.custom_vjp
def low(v):
    return lax.optimization_barrier(v.astype(jnp.bfloat16)).astype(jnp.float32)

@jax.custom_vjp
def low_back(v):
    return v

def low_keep(v):
    return (low(v), None)

def low_pass(kept, grad):
    return (grad,)

def back_keep(v):
    return (v, None)

def back_low(kept, grad):
    return (low(grad),)
low.defvjp(low_keep, low_pass)
low_back.defvjp(back_keep, back_low)

def rotate(values, positions, direction):
    half_width = values.shape[-1] // 2
    frequency = ROPE_BASE ** (-2.0 * jnp.arange(half_width, dtype=jnp.float32) / values.shape[-1])
    angles = positions.astype(jnp.float32)[:, None] * frequency[None, :]
    target_shape = (angles.shape[0],) + (1,) * (values.ndim - 2) + (half_width,)
    cosine = jnp.cos(angles).reshape(target_shape)
    sine_part = direction * jnp.sin(angles).reshape(target_shape)
    first_half = values[..., :half_width]
    second_half = values[..., half_width:]
    return jnp.concatenate([first_half * cosine - second_half * sine_part, second_half * cosine + first_half * sine_part], axis=-1)

def route_table(expert_ids, claim_order):
    picked_one = (expert_ids[:, :, None] == jnp.arange(EXPERTS)[None, None, :]).astype(jnp.float32)
    chosen = lax.optimization_barrier(jnp.sum(picked_one, axis=1)).reshape(N_CTX, TOK_CTX, EXPERTS)
    ordering = claim_order.reshape(N_CTX, TOK_CTX)
    ranking = (ordering[:, None, :] == jnp.arange(TOK_CTX)[None, :, None]).astype(jnp.float32)
    ordered = jnp.einsum('nrt,nte->nre', ranking, chosen, precision=HIGHEST)
    before = jnp.cumsum(ordered, axis=1) - ordered
    earlier = jnp.einsum('nrt,nre->nte', ranking, before, precision=HIGHEST).reshape(TOKENS, EXPERTS)
    slot_index = lax.optimization_barrier(jnp.sum(picked_one * earlier[:, None, :], axis=2)).astype(jnp.int32)
    kept_mask = slot_index < CAP
    source = (jnp.arange(TOKENS) // TOK_CTX).astype(jnp.int32)[:, None]
    target = jnp.where(kept_mask, expert_ids * (N_CTX * CAP) + source * CAP + slot_index, EXPERTS * N_CTX * CAP)
    return (picked_one, kept_mask.astype(jnp.float32), target.astype(jnp.int32))

def attend(operands):
    query_latent, query_rope, latent_keys = operands
    raw_scores = jnp.einsum('thr,kr->htk', query_latent, latent_keys[:, :RANK], precision=HIGHEST)
    raw_scores = raw_scores + jnp.einsum('thp,kp->htk', query_rope, latent_keys[:, RANK:], precision=HIGHEST)
    scores = low_back(raw_scores * (NOPE + ROPE) ** (-0.5))
    block_place = jnp.arange(LENGTH) // BLOCK
    visible = block_place[:, None] >= block_place[None, :]
    scores = jnp.where(visible[None], scores, -1e+30)
    top_score = lax.optimization_barrier(jnp.max(scores, axis=-1, keepdims=True))
    weights = jnp.exp(scores - top_score)
    probabilities = low(weights / lax.optimization_barrier(jnp.sum(weights, axis=-1, keepdims=True)))
    return low(low_back(jnp.einsum('htk,kr->thr', probabilities, latent_keys[:, :RANK], precision=HIGHEST)))

def expert_apply(operands):
    slot_rows, gate_matrix, up_matrix, down_matrix = operands
    gate_pre = low_back(jnp.dot(slot_rows, gate_matrix, precision=HIGHEST))
    up_pre = low_back(jnp.dot(slot_rows, up_matrix, precision=HIGHEST))
    hidden_act = low(jax.nn.silu(gate_pre) * up_pre)
    return low(low_back(jnp.dot(hidden_act, down_matrix, precision=HIGHEST)))

def reference(hidden_in, grad_out, block_ids, expert_ids, claim_order, attn_gain, latent_gain, ffn_gain, query_weight, latent_down, latent_up, output_weight, router_weight, expert_gate, expert_up, expert_down, shared_gate, shared_up, shared_down):
    positions = ((block_ids % BLOCKS_SEQ)[:, None] * BLOCK + jnp.arange(BLOCK)[None, :]).reshape(-1).astype(jnp.int32)
    seq_order = jnp.argsort(block_ids).astype(jnp.int32)
    picked_one, kept_mask, target = route_table(expert_ids, claim_order)
    slot_total = EXPERTS * N_CTX * CAP

    def forward(inputs, gain_one, gain_kv, gain_two, query_matrix, down_matrix, up_matrix, output_matrix, router_matrix, gate_experts, up_experts, down_experts, gate_shared, up_shared, down_shared):
        root_one = lax.rsqrt(lax.optimization_barrier(jnp.mean(inputs * inputs, axis=-1, keepdims=True)) + EPSILON)
        normed_one = low(inputs * root_one * gain_one)
        query_all = low_back(jnp.dot(normed_one, query_matrix, precision=HIGHEST)).reshape(TOKENS, H, NOPE + ROPE)
        query_nope = low(query_all[..., :NOPE])
        query_rope = low(rotate(query_all[..., NOPE:], positions, 1.0))
        compressed = low_back(jnp.dot(normed_one, down_matrix, precision=HIGHEST))
        latent_pre = compressed[:, :RANK]
        root_kv = lax.rsqrt(lax.optimization_barrier(jnp.mean(latent_pre * latent_pre, axis=-1, keepdims=True)) + EPSILON)
        latent_norm = low(latent_pre * root_kv * gain_kv)
        key_rope = low(rotate(compressed[:, RANK:], positions, 1.0))
        up_heads = up_matrix.reshape(RANK, H, NOPE + VDIM)
        query_latent = low(low_back(jnp.einsum('thn,rhn->thr', query_nope, up_heads[..., :NOPE], precision=HIGHEST)))
        latent_all = jnp.concatenate([latent_norm, key_rope], axis=1)
        latent_seq = latent_all.reshape(BLOCKS, BLOCK, RANK + ROPE)[seq_order].reshape(SEQS, LENGTH, RANK + ROPE)
        qlat_seq = query_latent.reshape(BLOCKS, BLOCK, H, RANK)[seq_order].reshape(SEQS, LENGTH, H, RANK)
        qrope_seq = query_rope.reshape(BLOCKS, BLOCK, H, ROPE)[seq_order].reshape(SEQS, LENGTH, H, ROPE)
        value_seq = lax.map(jax.checkpoint(attend), (qlat_seq, qrope_seq, latent_seq))
        value_latent = value_seq.reshape(BLOCKS, BLOCK, H, RANK)[block_ids].reshape(TOKENS, H, RANK)
        head_out = low(low_back(jnp.einsum('thr,rhv->thv', value_latent, up_heads[..., NOPE:], precision=HIGHEST)))
        attn_out = jnp.dot(head_out.reshape(TOKENS, H * VDIM), output_matrix, precision=HIGHEST)
        after_attn = inputs + low_back(attn_out)
        root_two = lax.rsqrt(lax.optimization_barrier(jnp.mean(after_attn * after_attn, axis=-1, keepdims=True)) + EPSILON)
        normed_two = low(after_attn * root_two * gain_two)
        logits = low_back(jnp.dot(normed_two, router_matrix, precision=HIGHEST))
        probabilities = jax.nn.softmax(logits, axis=-1)
        gate_value = lax.optimization_barrier(jnp.sum(probabilities[:, None, :] * picked_one, axis=2))
        gate_sh = low_back(jnp.dot(normed_two, gate_shared, precision=HIGHEST))
        up_sh = low_back(jnp.dot(normed_two, up_shared, precision=HIGHEST))
        hidden_sh = low(jax.nn.silu(gate_sh) * up_sh)
        shared_out = low_back(jnp.dot(hidden_sh, down_shared, precision=HIGHEST))
        slot_buffer = jnp.zeros((slot_total + 1, D), jnp.float32)
        for route in range(TOPK):
            slot_buffer = slot_buffer.at[target[:, route]].add(normed_two * kept_mask[:, route][:, None])
        slot_buffer = low_back(slot_buffer)
        slot_tensor = slot_buffer[:slot_total].reshape(EXPERTS, N_CTX * CAP, D)
        expert_rows = lax.map(jax.checkpoint(expert_apply), (slot_tensor, gate_experts, up_experts, down_experts))
        expert_flat = jnp.concatenate([expert_rows.reshape(slot_total, D), jnp.zeros((1, D), jnp.float32)], axis=0)
        routed = jnp.zeros((TOKENS, D), jnp.float32)
        for route in range(TOPK):
            routed = routed + (gate_value[:, route] * kept_mask[:, route])[:, None] * expert_flat[target[:, route]]
        return after_attn + shared_out + routed
    floats = (hidden_in.astype(jnp.float32), attn_gain.astype(jnp.float32), latent_gain.astype(jnp.float32), ffn_gain.astype(jnp.float32), query_weight.astype(jnp.float32), latent_down.astype(jnp.float32), latent_up.astype(jnp.float32), output_weight.astype(jnp.float32), router_weight.astype(jnp.float32), expert_gate.astype(jnp.float32), expert_up.astype(jnp.float32), expert_down.astype(jnp.float32), shared_gate.astype(jnp.float32), shared_up.astype(jnp.float32), shared_down.astype(jnp.float32))
    layer_value, pullback = jax.vjp(forward, *floats)
    grads = pullback(grad_out.astype(jnp.float32))
    return (layer_value.astype(jnp.bfloat16), grads[0], grads[1], grads[2], grads[3], grads[4], grads[5], grads[6], grads[7], grads[8], grads[9], grads[10], grads[11], grads[12], grads[13], grads[14])
```

```python
import jax
import jax.numpy as jnp
from jax import lax
from jax.experimental import pallas as pl
from jax.experimental.pallas import tpu as pltpu
from jax.sharding import Mesh
from jax.sharding import PartitionSpec as P

WIDTH = 2048
NOPE = 128
ROPE = 64
VDIM = 128
RANK = 512
KEYS = RANK + ROPE
HEADS = 4
EXPERTS = 64
EXP_DEV = 2
CAP = 30
SLOTS = 32
BLOCK = 128
SEQ_BLOCKS = 16
SEQ_PAIRS = 8
TOK = 256
QUARTER = 512
HALF = 1024
FF_SH = 704
N_CTX = 32
CHUNK = 512
EPSILON = 1e-06
ROPE_BASE = 10000.0
SCALE = (NOPE + ROPE) ** (-0.5)
CTX = ("zh", "y", "x")
MIB = 1 << 20

bf16 = jnp.bfloat16
f32 = jnp.float32


def dot(a, b, contract):
    return lax.dot_general(a, b, ((contract[0], contract[1]), ((), ())), preferred_element_type=f32)


def nn(a, b):
    return dot(a, b, ((1,), (0,)))


def nt(a, b):
    return dot(a, b, ((1,), (1,)))


def tn(a, b):
    return dot(a, b, ((0,), (0,)))


def rotate(values, positions, direction):
    half_width = values.shape[-1] // 2
    frequency = ROPE_BASE ** (-2.0 * jnp.arange(half_width, dtype=f32) / values.shape[-1])
    angles = positions.astype(f32)[:, None] * frequency[None, :]
    target_shape = (angles.shape[0],) + (1,) * (values.ndim - 2) + (half_width,)
    cosine = jnp.cos(angles).reshape(target_shape)
    sine_part = direction * jnp.sin(angles).reshape(target_shape)
    first_half = values[..., :half_width]
    second_half = values[..., half_width:]
    return jnp.concatenate(
        [
            first_half * cosine - second_half * sine_part,
            second_half * cosine + first_half * sine_part,
        ],
        axis=-1,
    )


def silu_slope(pre_act):
    sigmoid_val = jax.nn.sigmoid(pre_act)
    return sigmoid_val * (1.0 + pre_act * (1.0 - sigmoid_val))


def norm_back(upstream, source, inverse_root, gain_vec):
    scaled = upstream * gain_vec
    return inverse_root * scaled - source * inverse_root**3 * jnp.mean(
        scaled * source, axis=-1, keepdims=True
    )


def shift(value, axis, size, step):
    return lax.ppermute(value, axis, [(i, (i + step) % size) for i in range(size)])


def swap(value, axis):
    return shift(value, axis, 2, 1)


def pick(value, index, dim):
    return lax.dynamic_index_in_dim(value, index, dim, keepdims=False)


def gather_two(value, axis, dim):
    other = swap(value, axis)
    first = lax.axis_index(axis) == 0
    return jnp.stack(
        [jnp.where(first, value, other), jnp.where(first, other, value)], axis=dim
    )


def gather_four(value, axis, dim):
    here = lax.axis_index(axis)
    pieces = [value] + [shift(value, axis, 4, k) for k in (1, 2, 3)]
    shape = value.shape[:dim] + (4,) + value.shape[dim:]
    result = jnp.zeros(shape, value.dtype)
    for k, piece in enumerate(pieces):
        result = lax.dynamic_update_slice_in_dim(
            result, jnp.expand_dims(piece, dim), (here - k) % 4, dim
        )
    return result


def gather_ctx(value, x_last):
    pair = gather_two(value, "zh", 0)
    if x_last:
        return gather_four(gather_four(pair, "y", 1), "x", 2).reshape((N_CTX,) + value.shape)
    return gather_four(gather_four(pair, "x", 1), "y", 1).reshape((N_CTX,) + value.shape)


def scatter_four(value, axis, dim, kind):
    here = lax.axis_index(axis)
    arrived = [
        shift(pick(value, (here + k) % 4, dim), axis, 4, k).astype(f32) for k in (1, 2, 3)
    ]
    return (pick(value, here, dim).astype(f32) + arrived[0] + arrived[1] + arrived[2]).astype(kind)


def scatter_ctx(value, x_first):
    grid = value.reshape((2, 4, 4) + value.shape[1:])
    if x_first:
        grid = scatter_four(scatter_four(grid, "x", 2, bf16), "y", 1, bf16)
    else:
        grid = scatter_four(scatter_four(grid, "y", 1, bf16), "x", 1, bf16)
    here = lax.axis_index("zh")
    arrived = swap(pick(grid, 1 - here, 0), "zh")
    return pick(grid, here, 0).astype(f32) + arrived.astype(f32)


def exchange_ctx(value):
    return lax.all_to_all(value, CTX, 0, 0, tiled=True)


def half_of(value, core, dim=1):
    return jnp.concatenate(
        [
            lax.dynamic_slice_in_dim(value, core * QUARTER, QUARTER, dim),
            lax.dynamic_slice_in_dim(value, HALF + core * QUARTER, QUARTER, dim),
        ],
        axis=dim,
    )


def whole_of(own, other, core):
    first = jnp.where(core == 0, own, other)
    second = jnp.where(core == 0, other, own)
    return jnp.concatenate(
        [first[:, :QUARTER], second[:, :QUARTER], first[:, QUARTER:], second[:, QUARTER:]], axis=1
    )


def core_half(partial, core):
    arrived = swap(half_of(partial, 1 - core).astype(bf16), "core")
    return half_of(partial, core) + arrived.astype(f32)


def zl_sum(half):
    mine = half.astype(bf16)
    return mine.astype(f32) + swap(mine, "zl").astype(f32)


def zl_quarter(half, zl):
    arrived = swap(
        lax.dynamic_slice_in_dim(half, (1 - zl) * QUARTER, QUARTER, 1).astype(bf16), "zl"
    )
    return lax.dynamic_slice_in_dim(half, zl * QUARTER, QUARTER, 1) + arrived.astype(f32)


def attend_kernel(place_ref, q_ref, k_ref, out_ref, log_ref, top_ref, sum_ref, acc_ref):
    owner, chunk = pl.program_id(0), pl.program_id(1)
    place = place_ref[owner]

    @pl.when(chunk == 0)
    def _():
        top_ref[...] = jnp.full(top_ref.shape, -1e30, f32)
        sum_ref[...] = jnp.zeros(sum_ref.shape, f32)
        acc_ref[...] = jnp.zeros(acc_ref.shape, f32)

    @pl.when(chunk * (CHUNK // BLOCK) <= place)
    def _():
        q = q_ref[...].reshape(HEADS * BLOCK, KEYS)
        k = k_ref[pl.ds(chunk * CHUNK, CHUNK), :]
        scores = nt(q, k) * SCALE
        column = lax.broadcasted_iota(jnp.int32, scores.shape, 1) + chunk * CHUNK
        scores = jnp.where(column < (place + 1) * BLOCK, scores, -1e30)
        top_old = top_ref[...][:, :1]
        top = jnp.maximum(top_old, jnp.max(scores, axis=1, keepdims=True))
        weights = jnp.exp(scores - top)
        fade = jnp.exp(top_old - top)
        total = sum_ref[...][:, :1] * fade + jnp.sum(weights, axis=1, keepdims=True)
        acc_ref[...] = acc_ref[...] * fade + nn(weights.astype(bf16), k[:, :RANK])
        top_ref[...] = jnp.broadcast_to(top, top_ref.shape)
        sum_ref[...] = jnp.broadcast_to(total, sum_ref.shape)

    @pl.when(chunk == pl.num_programs(1) - 1)
    def _():
        total = sum_ref[...][:, :1]
        out_ref[...] = (acc_ref[...] / total).reshape(out_ref.shape)
        log_ref[...] = (top_ref[...] + jnp.log(sum_ref[...])).reshape(log_ref.shape)


def attend(places, query, keys):
    rows = HEADS * BLOCK
    return pl.pallas_call(
        attend_kernel,
        grid_spec=pltpu.PrefetchScalarGridSpec(
            num_scalar_prefetch=1,
            grid=(2, SEQ_BLOCKS * BLOCK // CHUNK),
            in_specs=[
                pl.BlockSpec((HEADS, 1, BLOCK, KEYS), lambda o, c, p: (0, o, 0, 0)),
                pl.BlockSpec((SEQ_BLOCKS * BLOCK, KEYS), lambda o, c, p: (0, 0)),
            ],
            out_specs=[
                pl.BlockSpec((HEADS, 1, BLOCK, RANK), lambda o, c, p: (0, o, 0, 0)),
                pl.BlockSpec((HEADS, 1, BLOCK, BLOCK), lambda o, c, p: (0, o, 0, 0)),
            ],
            scratch_shapes=[
                pltpu.VMEM((rows, 128), f32),
                pltpu.VMEM((rows, 128), f32),
                pltpu.VMEM((rows, RANK), f32),
            ],
        ),
        out_shape=[
            jax.ShapeDtypeStruct((HEADS, 2, BLOCK, RANK), f32),
            jax.ShapeDtypeStruct((HEADS, 2, BLOCK, BLOCK), f32),
        ],
        compiler_params=pltpu.CompilerParams(vmem_limit_bytes=48 * MIB),
        cost_estimate=pl.CostEstimate(
            flops=2 * 2 * rows * 1280 * (KEYS + RANK), bytes_accessed=8 * MIB, transcendentals=0
        ),
        name="attend",
    )(places, query, keys)


def attend_back_kernel(
    place_ref, q_ref, k_ref, out_ref, log_ref, grad_ref, dq_ref, dk_ref, inner_ref
):
    owner, chunk = pl.program_id(0), pl.program_id(1)
    place = place_ref[owner]
    rows = HEADS * BLOCK

    @pl.when((owner == 0) & (chunk == 0))
    def _():
        dk_ref[...] = jnp.zeros(dk_ref.shape, f32)

    @pl.when(chunk == 0)
    def _():
        dq_ref[...] = jnp.zeros(dq_ref.shape, f32)
        inner = jnp.sum(
            grad_ref[...].reshape(rows, RANK).astype(f32) * out_ref[...].reshape(rows, RANK),
            axis=1,
            keepdims=True,
        )
        inner_ref[...] = jnp.broadcast_to(inner, inner_ref.shape)

    @pl.when(chunk * (CHUNK // BLOCK) <= place)
    def _():
        q = q_ref[...].reshape(rows, KEYS)
        grad = grad_ref[...].reshape(rows, RANK)
        part = pl.ds(chunk * CHUNK, CHUNK)
        k = k_ref[part, :]
        scores = nt(q, k) * SCALE
        column = lax.broadcasted_iota(jnp.int32, scores.shape, 1) + chunk * CHUNK
        log_total = log_ref[...].reshape(rows, BLOCK)[:, :1]
        probs = jnp.where(column < (place + 1) * BLOCK, jnp.exp(scores - log_total), 0.0)
        prob_back = nt(grad, k[:, :RANK])
        score_grad = (probs * (prob_back - inner_ref[...][:, :1])).astype(bf16)
        dq_ref[...] += (nn(score_grad, k) * SCALE).reshape(dq_ref.shape)
        dk_ref[part, :] += tn(score_grad, q) * SCALE
        dk_ref[part, :RANK] += tn(probs.astype(bf16), grad)


def attend_back(places, query, keys, value, log_total, grad):
    rows = HEADS * BLOCK

    def per_owner(width):
        return pl.BlockSpec((HEADS, 1, BLOCK, width), lambda o, c, p: (0, o, 0, 0))

    whole = pl.BlockSpec((SEQ_BLOCKS * BLOCK, KEYS), lambda o, c, p: (0, 0))
    return pl.pallas_call(
        attend_back_kernel,
        grid_spec=pltpu.PrefetchScalarGridSpec(
            num_scalar_prefetch=1,
            grid=(2, SEQ_BLOCKS * BLOCK // CHUNK),
            in_specs=[
                per_owner(KEYS),
                whole,
                per_owner(RANK),
                per_owner(BLOCK),
                per_owner(RANK),
            ],
            out_specs=[per_owner(KEYS), whole],
            scratch_shapes=[pltpu.VMEM((rows, 128), f32)],
        ),
        out_shape=[
            jax.ShapeDtypeStruct((HEADS, 2, BLOCK, KEYS), f32),
            jax.ShapeDtypeStruct((SEQ_BLOCKS * BLOCK, KEYS), f32),
        ],
        compiler_params=pltpu.CompilerParams(vmem_limit_bytes=48 * MIB),
        cost_estimate=pl.CostEstimate(
            flops=2 * 2 * rows * 1280 * 5 * KEYS, bytes_accessed=14 * MIB, transcendentals=0
        ),
        name="attend_back",
    )(places, query, keys, value, log_total, grad)


def on_device(
    hidden_in,
    grad_out,
    block_ids,
    expert_ids,
    claim_order,
    attn_gain,
    latent_gain,
    ffn_gain,
    query_weight,
    latent_down,
    latent_up,
    output_weight,
    router_weight,
    expert_gate,
    expert_up,
    expert_down,
    shared_gate,
    shared_up,
    shared_down,
):
    ctx = lax.axis_index(CTX)
    zl = lax.axis_index("zl")
    core = lax.axis_index("core")
    ws = zl * 2 + core
    column_start = ws * QUARTER

    gains = jnp.concatenate([attn_gain, latent_gain, ffn_gain])
    small = jnp.concatenate(
        [
            latent_down.T,
            router_weight.T,
            jnp.pad(gains, (0, QUARTER - gains.shape[0]))[None],
            jnp.zeros((3, QUARTER), bf16),
        ],
        axis=0,
    )
    small_all = gather_ctx(small, True)
    down_t = small_all[:, :18].reshape(KEYS, QUARTER)
    side = gather_two(gather_two(small_all[:, 18:21], "zl", 0), "core", 1).reshape(
        4, N_CTX, 3, QUARTER
    )
    router_t = side[:, :, :2].transpose(1, 2, 0, 3).reshape(EXPERTS, WIDTH)
    gain_one = side[:, :, 2, :16].transpose(1, 0, 2).reshape(-1).astype(f32)
    gain_kv = side[:, :, 2, 16:20].transpose(1, 0, 2).reshape(-1).astype(f32)
    gain_two = side[:, :, 2, 20:36].transpose(1, 0, 2).reshape(-1).astype(f32)

    up_mine = latent_up.reshape(16, HEADS, NOPE + VDIM).transpose(1, 0, 2).reshape(64, NOPE + VDIM)
    out_up = jnp.concatenate([output_weight.T, up_mine], axis=1)
    query_full = gather_ctx(query_weight, True).reshape(WIDTH, HEADS * (NOPE + ROPE))
    out_up_all = gather_ctx(out_up, False)
    output_t = out_up_all[..., :QUARTER].reshape(WIDTH, QUARTER)
    up_heads = (
        out_up_all[..., QUARTER:]
        .reshape(N_CTX, HEADS, 16, NOPE + VDIM)
        .transpose(1, 0, 2, 3)
        .reshape(HEADS, RANK, NOPE + VDIM)
    )
    key_up = up_heads[..., :NOPE]
    value_up = up_heads[..., NOPE:]

    local_ids = lax.dynamic_slice_in_dim(block_ids, ctx * 2, 2)
    places = local_ids % SEQ_BLOCKS
    sequence = local_ids[0] // SEQ_BLOCKS
    positions = (places[:, None] * BLOCK + jnp.arange(BLOCK)[None, :]).reshape(-1)
    pair_ids = block_ids.reshape(N_CTX, 2)
    in_seq = (pair_ids[:, 0] // SEQ_BLOCKS) == sequence
    rank = jnp.cumsum(in_seq.astype(jnp.int32)) - 1
    is_pair = in_seq[None, :] & (rank[None, :] == jnp.arange(SEQ_PAIRS)[:, None])
    pairs = jnp.sum(jnp.where(is_pair, jnp.arange(N_CTX)[None, :], 0), axis=1)
    pair_places = pair_ids[pairs] % SEQ_BLOCKS
    place_of = pair_places.T.reshape(-1)
    slot_of = jnp.sum(
        jnp.where(
            place_of[None, :] == jnp.arange(SEQ_BLOCKS)[:, None],
            jnp.arange(SEQ_BLOCKS)[None, :],
            0,
        ),
        axis=1,
    )

    inputs = hidden_in.astype(f32)
    root_one = lax.rsqrt(jnp.mean(inputs * inputs, axis=-1, keepdims=True) + EPSILON)
    normed_one = (inputs * root_one * gain_one).astype(bf16)
    normed_quarter = lax.dynamic_slice_in_dim(normed_one, column_start, QUARTER, 1)
    compressed_part = nt(normed_quarter, down_t).reshape(2, 2, 64, KEYS)
    compressed_half = pick(compressed_part, core, 1) + swap(
        pick(compressed_part, 1 - core, 1), "core"
    )
    compressed = pick(compressed_half, zl, 0) + swap(pick(compressed_half, 1 - zl, 0), "zl")
    row_start = ws * 64
    my_positions = lax.dynamic_slice_in_dim(positions, row_start, 64)
    latent_pre = compressed[:, :RANK]
    root_kv = lax.rsqrt(jnp.mean(latent_pre * latent_pre, axis=-1, keepdims=True) + EPSILON)
    latent_rows = jnp.concatenate(
        [
            (latent_pre * root_kv * gain_kv).astype(bf16),
            rotate(compressed[:, RANK:], my_positions, 1.0).astype(bf16),
        ],
        axis=1,
    )
    latent_ctx = gather_ctx(latent_rows, True)
    latent_mine = latent_ctx[pairs]
    latent_seq = gather_two(gather_two(latent_mine, "zl", 0), "core", 2).reshape(
        SEQ_BLOCKS, BLOCK, KEYS
    )
    keys = latent_seq[slot_of].reshape(SEQ_BLOCKS * BLOCK, KEYS)

    query_all = nn(normed_one, query_full).reshape(TOK, HEADS, NOPE + ROPE)
    query_nope = query_all[..., :NOPE].astype(bf16)
    query_rope = rotate(query_all[..., NOPE:], positions, 1.0).astype(bf16)
    query_latent = jnp.einsum(
        "thn,hrn->htr", query_nope, key_up, preferred_element_type=f32
    ).astype(bf16)
    query = jnp.concatenate([query_latent, query_rope.transpose(1, 0, 2)], axis=2)
    query = query.reshape(HEADS, 2, BLOCK, KEYS)
    value, log_total = attend(places, query, keys)
    value_parts = value.reshape(HEADS, TOK, RANK).astype(bf16)
    head_out = jnp.einsum("htr,hrv->thv", value_parts, value_up, preferred_element_type=f32)
    head_flat = head_out.astype(bf16).reshape(TOK, HEADS * VDIM)
    attn_part = nt(head_flat, output_t)
    attn_half = zl_sum(core_half(attn_part, core))
    after_half = half_of(inputs, core) + attn_half
    after_attn = whole_of(after_half, swap(after_half, "core"), core)
    root_two = lax.rsqrt(jnp.mean(after_attn * after_attn, axis=-1, keepdims=True) + EPSILON)
    normed_two = (after_attn * root_two * gain_two).astype(bf16)

    gate_up_mine, shared_down_mine, _ = lax.optimization_barrier(
        (jnp.concatenate([shared_gate, shared_up], axis=1), shared_down.T, keys)
    )
    gate_up = gather_ctx(gate_up_mine, True).reshape(WIDTH, 2 * FF_SH)
    shared_down_t = gather_ctx(shared_down_mine, False).reshape(WIDTH, FF_SH)

    chosen = jnp.sum(
        (expert_ids[:, :, None] == jnp.arange(EXPERTS)[None, None, :]).astype(f32), axis=1
    )
    before = (claim_order[None, :] < claim_order[:, None]).astype(bf16)
    earlier = nn(before, chosen.astype(bf16))
    slot_by = jnp.where(chosen > 0, earlier, float(CAP))
    slot_by = jnp.where(slot_by < CAP, slot_by, 99.0).T.reshape(N_CTX, EXP_DEV, TOK)
    slot_by = slot_by.transpose(1, 0, 2)
    places_hot = (
        slot_by[:, :, None, :] == jnp.arange(SLOTS, dtype=f32)[None, None, :, None]
    ).astype(bf16)
    flat_hot = places_hot.reshape(EXP_DEV, N_CTX * SLOTS, TOK)

    grad_half, _ = lax.optimization_barrier((half_of(grad_out, core), keys))
    grad_rows = []
    for e in range(EXP_DEV):
        sent = nn(flat_hot[e], grad_half).astype(bf16).reshape(N_CTX, SLOTS, HALF)
        own = exchange_ctx(sent).reshape(N_CTX * SLOTS, HALF)
        grad_rows.append(whole_of(own, swap(own, "core"), core))

    logits = nt(normed_two, router_t)
    probs_router = jax.nn.softmax(logits, axis=-1)
    probs_by = probs_router.T.reshape(N_CTX, EXP_DEV, TOK).transpose(1, 0, 2)
    gate_slots = jnp.sum(places_hot.astype(f32) * probs_by[:, :, None, :], axis=3)

    normed_half = half_of(normed_two, core)
    rows_in, gate_in = [], []
    for e in range(EXP_DEV):
        sent = nn(flat_hot[e], normed_half).astype(bf16).reshape(N_CTX, SLOTS, HALF)
        gate_row = jnp.pad(gate_slots[e].astype(bf16), ((0, 0), (0, HALF - SLOTS)))
        sent = lax.dynamic_update_slice_in_dim(sent, gate_row[:, None, :], CAP, 1)
        own = exchange_ctx(sent)
        gate_in.append(own[:, CAP, :SLOTS].astype(f32).reshape(N_CTX * SLOTS, 1))
        own = own.reshape(N_CTX * SLOTS, HALF)
        rows_in.append(whole_of(own, swap(own, "core"), core))

    gate_up_pre = nn(normed_two, gate_up)
    gate_sh, up_sh = gate_up_pre[:, :FF_SH], gate_up_pre[:, FF_SH:]
    hidden_sh = (jax.nn.silu(gate_sh) * up_sh).astype(bf16)
    grad_hidden_sh = nn(grad_out, shared_down_t)
    grad_gate_up = jnp.concatenate(
        [
            (grad_hidden_sh * up_sh * silu_slope(gate_sh)).astype(bf16),
            (grad_hidden_sh * jax.nn.silu(gate_sh)).astype(bf16),
        ],
        axis=1,
    )
    shared_in_half = core_half(nt(grad_gate_up, gate_up), core)
    shared_part = nt(hidden_sh, shared_down_t)
    shared_half = core_half(shared_part, core)
    grad_gate_up_part = tn(normed_two, grad_gate_up).astype(bf16)
    grad_shared_down_part = tn(grad_out, hidden_sh).astype(bf16)

    grads_gate, grads_up, grads_down = [], [], []
    rows_back, outs_back = [], []
    later = []
    for e in range(EXP_DEV):
        rows, grads = rows_in[e], grad_rows[e]
        gate_ex = nn(rows, expert_gate[e])
        up_ex = nn(rows, expert_up[e])
        hidden_ex = (jax.nn.silu(gate_ex) * up_ex).astype(bf16)
        plain = nt(grads, expert_down[e])
        gate_dot = jnp.sum(hidden_ex.astype(f32) * plain, axis=1)
        grad_hidden = plain * gate_in[e]
        grad_gate_ex = (grad_hidden * up_ex * silu_slope(gate_ex)).astype(bf16)
        grad_up_ex = (grad_hidden * jax.nn.silu(gate_ex)).astype(bf16)
        halves = []
        for which in (1 - core, core):
            halves.append(
                nt(grad_gate_ex, half_of(expert_gate[e], which, 0))
                + nt(grad_up_ex, half_of(expert_up[e], which, 0))
            )
        summed = halves[1] + swap(halves[0].astype(bf16), "core").astype(f32)
        gate_dot = (gate_dot + swap(gate_dot, "core")).astype(bf16).reshape(N_CTX, SLOTS)
        sent = summed.astype(bf16).reshape(N_CTX, SLOTS, HALF)
        gate_row = jnp.pad(gate_dot, ((0, 0), (0, HALF - SLOTS)))
        sent = lax.dynamic_update_slice_in_dim(sent, gate_row[:, None, :], CAP, 1)
        rows_back.append(exchange_ctx(sent))
        later.append((rows, grads, hidden_ex, grad_gate_ex, grad_up_ex))
    for e in range(EXP_DEV):
        rows, grads, hidden_ex, grad_gate_ex, grad_up_ex = later[e]
        halves = [nn(hidden_ex, half_of(expert_down[e], which, 1)) for which in (1 - core, core)]
        summed = halves[1] + swap(halves[0].astype(bf16), "core").astype(f32)
        outs_back.append(exchange_ctx(summed.astype(bf16).reshape(N_CTX, SLOTS, HALF)))
        scaled_hidden = (hidden_ex.astype(f32) * gate_in[e]).astype(bf16)
        grads_down.append(tn(scaled_hidden, grads))
        grads_gate.append(tn(rows, grad_gate_ex))
        grads_up.append(tn(rows, grad_up_ex))
    grad_expert_gate = jnp.stack(grads_gate)
    grad_expert_up = jnp.stack(grads_up)
    grad_expert_down = jnp.stack(grads_down)

    routed_in_half = shared_in_half
    prob_grad = []
    for e in range(EXP_DEV):
        routed_in_half = routed_in_half + tn(
            flat_hot[e], rows_back[e].reshape(N_CTX * SLOTS, HALF)
        )
        dots = rows_back[e][:, CAP, :SLOTS].astype(f32)
        prob_grad.append(jnp.sum(places_hot[e].astype(f32) * dots[:, :, None], axis=1))
    prob_grad = jnp.stack(prob_grad, axis=1).reshape(EXPERTS, TOK).T
    prob_grad = prob_grad + swap(prob_grad, "zl")
    normed_half_grad = zl_sum(routed_in_half)
    normed_two_grad = whole_of(normed_half_grad, swap(normed_half_grad, "core"), core)
    logit_grad = (
        probs_router * (prob_grad - jnp.sum(probs_router * prob_grad, axis=-1, keepdims=True))
    ).astype(bf16)
    normed_two_grad = normed_two_grad + nn(logit_grad, router_t)
    normed_two_quarter = lax.dynamic_slice_in_dim(normed_two, column_start, QUARTER, 1)
    router_part = tn(logit_grad, normed_two_quarter).reshape(N_CTX, EXP_DEV, QUARTER)
    upstream = grad_out.astype(f32)
    after_grad = upstream + norm_back(normed_two_grad, after_attn, root_two, gain_two)
    gain_two_part = jnp.sum(normed_two_grad * after_attn * root_two, axis=0)
    gain_two_mine = pick(gain_two_part.reshape(N_CTX, 4, 16), ws, 1)

    attn_grad = after_grad.astype(bf16)
    head_grad = nn(attn_grad, output_t).astype(bf16).reshape(TOK, HEADS, VDIM)
    latent_grad = jnp.einsum(
        "thv,hrv->htr", head_grad, value_up, preferred_element_type=f32
    ).astype(bf16)
    grad_query_lat, grad_keys = attend_back(
        places,
        query,
        keys,
        value,
        log_total,
        latent_grad.reshape(HEADS, 2, BLOCK, RANK),
    )
    grad_query_lat = grad_query_lat.reshape(HEADS, TOK, KEYS)

    grad_keys = grad_keys.astype(bf16).reshape(SEQ_BLOCKS, 2, 64, KEYS)
    keys_half = pick(grad_keys, core, 1).astype(f32) + swap(
        pick(grad_keys, 1 - core, 1), "core"
    ).astype(f32)
    keys_half = keys_half.astype(bf16)[place_of].reshape(2, SEQ_PAIRS, 64, KEYS)
    keys_mine = pick(keys_half, zl, 0).astype(f32) + swap(pick(keys_half, 1 - zl, 0), "zl").astype(
        f32
    )
    keys_sent = jnp.where(
        in_seq[:, None, None], keys_mine.astype(bf16)[jnp.clip(rank, 0, SEQ_PAIRS - 1)], 0
    )
    latent_sum = jnp.sum(exchange_ctx(keys_sent).astype(f32), axis=0)

    query_lat_grad = grad_query_lat[..., :RANK].astype(bf16)
    nope_grad = jnp.einsum("htr,hrn->thn", query_lat_grad, key_up, preferred_element_type=f32)
    rope_grad = rotate(grad_query_lat[..., RANK:].transpose(1, 0, 2), positions, -1.0)
    query_grad = (
        jnp.concatenate([nope_grad, rope_grad], axis=-1)
        .astype(bf16)
        .reshape(TOK, HEADS * (NOPE + ROPE))
    )
    grad_query_part = tn(normed_one, query_grad).astype(bf16)
    normed_one_part = nt(query_grad, query_full)
    grad_key_up = jnp.einsum(
        "thn,htr->hrn", query_nope, query_lat_grad, preferred_element_type=f32
    )
    grad_value_up = jnp.einsum("htr,thv->hrv", value_parts, head_grad, preferred_element_type=f32)
    grad_up_part = (
        jnp.concatenate([grad_key_up, grad_value_up], axis=-1)
        .astype(bf16)
        .reshape(HEADS, N_CTX, 16, NOPE + VDIM)
        .transpose(1, 0, 2, 3)
        .reshape(N_CTX, 64, NOPE + VDIM)
    )
    grad_output_part = tn(attn_grad, head_flat).astype(bf16).reshape(N_CTX, 64, QUARTER)

    latent_norm_grad = latent_sum[:, :RANK]
    latent_pre_grad = norm_back(latent_norm_grad, latent_pre, root_kv, gain_kv)
    gain_kv_part = jnp.sum(latent_norm_grad * latent_pre * root_kv, axis=0)
    rope_pre_grad = rotate(latent_sum[:, RANK:], my_positions, -1.0)
    compressed_grad = jnp.concatenate([latent_pre_grad, rope_pre_grad], axis=1).astype(bf16)
    compressed_grad = gather_two(gather_two(compressed_grad, "core", 0), "zl", 0).reshape(TOK, KEYS)
    grad_down_part = tn(compressed_grad, normed_quarter).reshape(N_CTX, 18, QUARTER)
    rows_grad = nn(compressed_grad, down_t)
    mine = lax.dynamic_slice_in_dim(normed_one_part, column_start, QUARTER, 1)
    normed_one_part = lax.dynamic_update_slice_in_dim(
        normed_one_part, mine + rows_grad, column_start, 1
    )
    input_part = norm_back(normed_one_part, inputs, root_one, gain_one)
    gain_one_part = jnp.sum(normed_one_part * inputs * root_one, axis=0)
    input_quarter = zl_quarter(core_half(input_part, core), zl)
    grad_in = lax.dynamic_slice_in_dim(after_grad, column_start, QUARTER, 1) + input_quarter
    gain_parts = jnp.concatenate(
        [gain_one_part.reshape(N_CTX, 2, 2, 16), gain_kv_part.reshape(N_CTX, 2, 2, 4)], axis=-1
    )
    gain_core = pick(gain_parts, core, 2) + swap(pick(gain_parts, 1 - core, 2), "core")
    gain_mine = pick(gain_core, zl, 1) + swap(pick(gain_core, 1 - zl, 1), "zl")

    routed_half = shared_half
    for e in range(EXP_DEV):
        weighted = (flat_hot[e].astype(f32) * gate_slots[e].reshape(N_CTX * SLOTS, 1)).astype(bf16)
        routed_half = routed_half + tn(weighted, outs_back[e].reshape(N_CTX * SLOTS, HALF))
    layer_out = (
        lax.dynamic_slice_in_dim(after_attn, column_start, QUARTER, 1)
        + zl_quarter(routed_half, zl)
    ).astype(bf16)

    gate_up_sum = scatter_ctx(grad_gate_up_part.reshape(N_CTX, 64, 2 * FF_SH), True)
    shared_down_sum = scatter_ctx(grad_shared_down_part.reshape(N_CTX, 64, FF_SH), False)
    query_sum = scatter_ctx(grad_query_part.reshape(N_CTX, 64, HEADS * (NOPE + ROPE)), True)
    out_up_sum = scatter_ctx(jnp.concatenate([grad_output_part, grad_up_part], axis=2), False)
    gain_row = jnp.concatenate([gain_mine, gain_two_mine], axis=1)
    gain_row = jnp.pad(gain_row, ((0, 0), (0, QUARTER - 36)))[:, None, :]
    small_parts = jnp.concatenate(
        [
            grad_down_part.astype(bf16),
            router_part.astype(bf16),
            gain_row.astype(bf16),
            jnp.zeros((N_CTX, 3, QUARTER), bf16),
        ],
        axis=1,
    )
    small_sum = scatter_ctx(small_parts, True)
    up_sum = (
        out_up_sum[:, QUARTER:]
        .reshape(HEADS, 16, NOPE + VDIM)
        .transpose(1, 0, 2)
        .reshape(16, HEADS * (NOPE + VDIM))
    )
    return (
        layer_out,
        grad_in,
        small_sum[20, :16],
        small_sum[20, 16:20],
        small_sum[20, 20:36],
        query_sum,
        small_sum[:18].T,
        up_sum,
        out_up_sum[:, :QUARTER].T,
        small_sum[18:20].T,
        grad_expert_gate,
        grad_expert_up,
        grad_expert_down,
        gate_up_sum[:, :FF_SH],
        gate_up_sum[:, FF_SH:],
        shared_down_sum.T,
    )


def solution(mesh):
    grid = Mesh(mesh.devices.reshape(2, 4, 4, 2, 2), CTX + ("zl", "core"))
    ctx, ws, both = CTX, ("zl", "core"), CTX + ("zl", "core")
    placed = (
        P(ctx, None),
        P(ctx, None),
        P(),
        P(ctx, None),
        P(ctx),
        P(both),
        P(both),
        P(both),
        P(ctx, ws),
        P(ws, ctx),
        P(ctx, ws),
        P(ws, ctx),
        P(ws, ctx),
        P(ctx, None, ws),
        P(ctx, None, ws),
        P(ctx, ws, None),
        P(ctx, ws),
        P(ctx, ws),
        P(ws, ctx),
    )
    return jax.shard_map(
        on_device,
        mesh=grid,
        in_specs=placed,
        out_specs=(
            P(ctx, ws),
            P(ctx, ws),
            P(both),
            P(both),
            P(both),
            P(ctx, ws),
            P(ws, ctx),
            P(ctx, ws),
            P(ws, ctx),
            P(ws, ctx),
            P(ctx, None, ws),
            P(ctx, None, ws),
            P(ctx, ws, None),
            P(ctx, ws),
            P(ctx, ws),
            P(ws, ctx),
        ),
        check_vma=False,
    )
```

```python
import jax
import jax.numpy as jnp
from jax import lax
from jax.experimental import pallas as pl
from jax.experimental.pallas import tpu as pltpu
from jax.sharding import Mesh
from jax.sharding import PartitionSpec as P

WIDTH = 2048
NOPE = 128
ROPE = 64
VDIM = 128
RANK = 512
KEYS = RANK + ROPE
HEADS = 4
EXPERTS = 64
EXP_DEV = 2
CAP = 30
TOPK = 6
SLOTS = 32
BLOCK = 128
SEQ_BLOCKS = 16
SEQ_PAIRS = 8
TOK = 256
QUARTER = 512
HALF = 1024
FF_SH = 704
N_CTX = 32
CHUNK = 512
EPSILON = 1e-06
ROPE_BASE = 10000.0
SCALE = (NOPE + ROPE) ** (-0.5)
CTX = ("zh", "y", "x")
MIB = 1 << 20

bf16 = jnp.bfloat16
f32 = jnp.float32


def dot(a, b, contract):
    return lax.dot_general(a, b, ((contract[0], contract[1]), ((), ())), preferred_element_type=f32)


def nn(a, b):
    return dot(a, b, ((1,), (0,)))


def nt(a, b):
    return dot(a, b, ((1,), (1,)))


def tn(a, b):
    return dot(a, b, ((0,), (0,)))


def rotate(values, positions, direction):
    half_width = values.shape[-1] // 2
    frequency = ROPE_BASE ** (-2.0 * jnp.arange(half_width, dtype=f32) / values.shape[-1])
    angles = positions.astype(f32)[:, None] * frequency[None, :]
    target_shape = (angles.shape[0],) + (1,) * (values.ndim - 2) + (half_width,)
    cosine = jnp.cos(angles).reshape(target_shape)
    sine_part = direction * jnp.sin(angles).reshape(target_shape)
    first_half = values[..., :half_width]
    second_half = values[..., half_width:]
    return jnp.concatenate(
        [
            first_half * cosine - second_half * sine_part,
            second_half * cosine + first_half * sine_part,
        ],
        axis=-1,
    )


def silu_slope(pre_act):
    sigmoid_val = jax.nn.sigmoid(pre_act)
    return sigmoid_val * (1.0 + pre_act * (1.0 - sigmoid_val))


def norm_back(upstream, source, inverse_root, gain_vec):
    scaled = upstream * gain_vec
    return inverse_root * scaled - source * inverse_root**3 * jnp.mean(
        scaled * source, axis=-1, keepdims=True
    )


def shift(value, axis, size, step):
    return lax.ppermute(value, axis, [(i, (i + step) % size) for i in range(size)])


def swap(value, axis):
    return shift(value, axis, 2, 1)


def pick(value, index, dim):
    return lax.dynamic_index_in_dim(value, index, dim, keepdims=False)


def gather_two(value, axis, dim):
    other = swap(value, axis)
    first = lax.axis_index(axis) == 0
    return jnp.stack(
        [jnp.where(first, value, other), jnp.where(first, other, value)], axis=dim
    )


def gather_ctx(value, name):
    with jax.named_scope(name):
        gathered = lax.all_gather(value, CTX, axis=0, tiled=False)
        return gathered.reshape((2, 16) + value.shape)


def scatter_yx(value, name):
    with jax.named_scope(name):
        pair = lax.psum_scatter(value, ("y", "x"), scatter_dimension=0, tiled=True)
        return pair.reshape(2, -1, pair.shape[1])


def scatter_zh(pair, name):
    with jax.named_scope(name):
        here = lax.axis_index("zh")
        arrived = swap(pick(pair, 1 - here, 0), "zh")
        return pick(pair, here, 0).astype(f32) + arrived.astype(f32)


def after(value, earlier):
    return lax.optimization_barrier((value, earlier))[0]


def exchange_ctx(value, name, earlier=None):
    with jax.named_scope(name):
        if earlier is not None:
            value = after(value, earlier)
        return lax.all_to_all(value, CTX, 0, 0, tiled=True)


def share_ctx(value, name):
    return exchange_ctx(jnp.broadcast_to(value[None], (N_CTX,) + value.shape), name)


def half_of(value, core, dim=1):
    return jnp.concatenate(
        [
            lax.dynamic_slice_in_dim(value, core * QUARTER, QUARTER, dim),
            lax.dynamic_slice_in_dim(value, HALF + core * QUARTER, QUARTER, dim),
        ],
        axis=dim,
    )


def whole_of(own, other, core):
    first = jnp.where(core == 0, own, other)
    second = jnp.where(core == 0, other, own)
    return jnp.concatenate(
        [first[:, :QUARTER], second[:, :QUARTER], first[:, QUARTER:], second[:, QUARTER:]], axis=1
    )


def core_half(partial, core):
    arrived = swap(half_of(partial, 1 - core).astype(bf16), "core")
    return half_of(partial, core) + arrived.astype(f32)


def zl_sum(half):
    mine = half.astype(bf16)
    return mine.astype(f32) + swap(mine, "zl").astype(f32)


def zl_quarter(half, zl):
    arrived = swap(
        lax.dynamic_slice_in_dim(half, (1 - zl) * QUARTER, QUARTER, 1).astype(bf16), "zl"
    )
    return lax.dynamic_slice_in_dim(half, zl * QUARTER, QUARTER, 1) + arrived.astype(f32)


def call(body, outs, name, flops, scratch=(), limit=56):
    def run(scalars, *arrays):
        spec = pl.BlockSpec(memory_space=pltpu.VMEM)
        moved = sum(a.size * a.dtype.itemsize for a in arrays)
        moved += sum(o.size * o.dtype.itemsize for o in outs)
        return pl.pallas_call(
            body,
            in_specs=[pl.BlockSpec(memory_space=pltpu.SMEM)] + [spec] * len(arrays),
            out_specs=[spec] * len(outs),
            out_shape=outs,
            scratch_shapes=scratch,
            compiler_params=pltpu.CompilerParams(vmem_limit_bytes=limit * MIB),
            cost_estimate=pl.CostEstimate(
                flops=int(flops), bytes_accessed=int(moved), transcendentals=0
            ),
            name=name,
        )(scalars, *arrays)

    return run


def out(shape, kind):
    return jax.ShapeDtypeStruct(shape, kind)


def quarter_at(zl, core):
    return pl.ds(pl.multiple_of(zl * HALF + core * QUARTER, QUARTER), QUARTER)


def whole_value(own, other, core):
    first = jnp.where(core == 0, own, other)
    second = jnp.where(core == 0, other, own)
    return jnp.concatenate(
        [first[:, :QUARTER], second[:, :QUARTER], first[:, QUARTER:], second[:, QUARTER:]], axis=1
    )


def one_hot(slots):
    number = lax.broadcasted_iota(jnp.int32, (N_CTX, SLOTS, TOK), 1).astype(f32)
    hot = jnp.where(slots[:, None, :] == number, 1.0, 0.0)
    return hot.reshape(N_CTX * SLOTS, TOK)


def cotangents_kernel(core_ref, ids_ref, row_ref, col_ref, grad_ref, slot_ref, sent_ref):
    core = core_ref[0]
    row = lax.broadcasted_iota(jnp.int32, (EXPERTS, TOK), 0)
    expert = (row & (N_CTX - 1)) * 2 + (row >> 5)
    chosen = jnp.zeros((EXPERTS, TOK), f32)
    for k in range(TOPK):
        chosen = chosen + jnp.where(ids_ref[k : k + 1, :] == expert, 1.0, 0.0)
    before = jnp.where(col_ref[...] < row_ref[...], 1.0, 0.0).astype(bf16)
    earlier = nn(chosen.astype(bf16), before)
    slots = jnp.where((chosen > 0.5) & (earlier < CAP - 0.5), earlier, 99.0)
    slot_ref[...] = slots
    grad = jnp.concatenate([grad_ref[:, quarter_at(0, core)], grad_ref[:, quarter_at(1, core)]], 1)
    for e in range(EXP_DEV):
        hot = one_hot(slots[e * N_CTX : (e + 1) * N_CTX]).astype(bf16)
        sent_ref[:, e] = nn(hot, grad).astype(bf16).reshape(N_CTX, SLOTS, HALF)


def middle_kernel(
    core_ref, own_ref, other_ref, input_ref, gain_ref, router_ref, slot_ref,
    normed_ref, root_ref, probs_ref, sent_one_ref, sent_two_ref,
):
    core = core_ref[0]
    after = input_ref[...].astype(f32) + whole_value(own_ref[...], other_ref[...], core)
    root = lax.rsqrt(jnp.sum(after * after, axis=1, keepdims=True) * (1.0 / WIDTH) + EPSILON)
    normed = (after * root * gain_ref[...]).astype(bf16)
    normed_ref[...] = normed
    root_ref[...] = jnp.broadcast_to(root, root_ref.shape)
    logits = nt(router_ref[...], normed)
    weights = jnp.exp(logits - jnp.max(logits, axis=0, keepdims=True))
    probs = weights / jnp.sum(weights, axis=0, keepdims=True)
    probs_ref[...] = probs
    half = jnp.concatenate(
        [normed_ref[:, quarter_at(0, core)], normed_ref[:, quarter_at(1, core)]], axis=1
    )
    slot_row = lax.broadcasted_iota(jnp.int32, (N_CTX, SLOTS, HALF), 1)
    for e, sent_ref in enumerate((sent_one_ref, sent_two_ref)):
        part = slice(e * N_CTX, (e + 1) * N_CTX)
        hot = one_hot(slot_ref[part])
        gated = (hot.reshape(N_CTX, SLOTS, TOK) * probs[part][:, None, :]).astype(bf16)
        gate_row = nt(jnp.ones((8, TOK), bf16), gated.reshape(N_CTX * SLOTS, TOK))[:1]
        rows = nn(hot.astype(bf16), half).reshape(N_CTX, SLOTS, HALF)
        sent_ref[...] = jnp.where(slot_row == CAP, gate_row[None], rows).astype(bf16)


def column_of(row, ctx):
    groups = row.shape[0]
    lane = lax.broadcasted_iota(jnp.int32, (HALF, SLOTS), 0) - ctx * SLOTS
    picked = jnp.where(lane == lax.broadcasted_iota(jnp.int32, (HALF, SLOTS), 1), 1.0, 0.0)
    mine = nn(row.astype(bf16), picked.astype(bf16))
    square = (groups, SLOTS, SLOTS)
    same = lax.broadcasted_iota(jnp.int32, square, 1) == lax.broadcasted_iota(jnp.int32, square, 2)
    spread = jnp.where(same, mine[:, None, :], 0.0).reshape(groups * SLOTS, SLOTS)
    return jnp.sum(spread, axis=1, keepdims=True)


def shared_kernel(
    core_ref, normed_ref, grad_ref, weight_ref,
    own_ref, send_ref, in_own_ref, in_send_ref, grads_ref, pre_ref, back_ref,
):
    core = core_ref[0]

    def block(step):
        z, group = step // 4, lax.rem(step, 4)
        place = pl.ds(pl.multiple_of(step * 256, 256), 256)
        return z, group, place, weight_ref[pl.ds(group * 4, 4), z].reshape(256, 3 * FF_SH)

    pre_ref[...] = jnp.zeros(pre_ref.shape, f32)
    back_ref[...] = jnp.zeros(back_ref.shape, f32)

    def forward(step, carry):
        _, _, place, weight = block(step)
        pre_ref[...] += nn(normed_ref[:, place], weight[:, : 2 * FF_SH])
        back_ref[...] += nn(grad_ref[:, place], weight[:, 2 * FF_SH :])
        return carry

    lax.fori_loop(0, 8, forward, 0)
    gate, up, back = pre_ref[:, :FF_SH], pre_ref[:, FF_SH:], back_ref[...]
    sigmoid = 1.0 / (1.0 + jnp.exp(-gate))
    act = gate * sigmoid
    hidden = (act * up).astype(bf16)
    grad_gate = back * up * (sigmoid * (1.0 + gate * (1.0 - sigmoid)))
    grad_pre = jnp.concatenate([grad_gate, back * act], axis=1).astype(bf16)

    def backward(step, carry):
        z, group, place, weight = block(step)
        grads_ref[pl.ds(group * 4, 4), z, :, : 2 * FF_SH] = (
            tn(normed_ref[:, place], grad_pre).astype(bf16).reshape(4, 64, 2 * FF_SH)
        )
        grads_ref[pl.ds(group * 4, 4), z, :, 2 * FF_SH :] = (
            tn(grad_ref[:, place], hidden).astype(bf16).reshape(4, 64, FF_SH)
        )
        shared = nt(hidden, weight[:, 2 * FF_SH :])
        inner = nt(grad_pre, weight[:, : 2 * FF_SH])
        column = pl.ds(pl.multiple_of(z * QUARTER + lax.rem(group, 2) * 256, 256), 256)

        @pl.when(group // 2 == core)
        def _():
            own_ref[:, column] = shared
            in_own_ref[:, column] = inner

        @pl.when(group // 2 != core)
        def _():
            send_ref[:, column] = shared.astype(bf16)
            in_send_ref[:, column] = inner.astype(bf16)

        return carry

    lax.fori_loop(0, 8, backward, 0)


def shared(core, normed_two, grad_out, weights):
    run = pl.pallas_call(
        shared_kernel,
        in_specs=[pl.BlockSpec(memory_space=pltpu.SMEM)]
        + [pl.BlockSpec(memory_space=pltpu.VMEM)] * 3,
        out_specs=[pl.BlockSpec(memory_space=pltpu.VMEM)] * 5,
        out_shape=[
            out((TOK, HALF), f32),
            out((TOK, HALF), bf16),
            out((TOK, HALF), f32),
            out((TOK, HALF), bf16),
            out((16, 2, 64, 3 * FF_SH), bf16),
        ],
        scratch_shapes=[pltpu.VMEM((TOK, 2 * FF_SH), f32), pltpu.VMEM((TOK, FF_SH), f32)],
        compiler_params=pltpu.CompilerParams(vmem_limit_bytes=56 * MIB),
        cost_estimate=pl.CostEstimate(
            flops=18 * TOK * WIDTH * FF_SH, bytes_accessed=24 * MIB, transcendentals=0
        ),
        name="shared_experts",
    )
    return run(core, normed_two, grad_out, weights)


def expert_kernel(
    core_ref, own_ref, other_ref, grad_own_ref, grad_other_ref, wg_ref, wu_ref, wd_ref,
    back_own_ref, back_send_ref, y_own_ref, y_send_ref, dot_ref, scaled_ref, dg_ref, du_ref,
):
    core = core_ref[0]
    groups = own_ref.shape[0]
    rows = groups * SLOTS
    gate = jnp.zeros((rows, 352), f32)
    up = jnp.zeros((rows, 352), f32)
    plain = jnp.zeros((rows, 352), f32)
    for z in range(2):
        mine = slice(z * QUARTER, (z + 1) * QUARTER)
        for x_ref, g_ref, which in (
            (own_ref, grad_own_ref, core), (other_ref, grad_other_ref, 1 - core),
        ):
            place = quarter_at(z, which)
            x = x_ref[:, :, mine].reshape(rows, QUARTER)
            gate = gate + nt(x, wg_ref[0, :, place])
            up = up + nt(x, wu_ref[0, :, place])
            plain = plain + nt(g_ref[:, 0, :, mine].reshape(rows, QUARTER), wd_ref[0, :, place])
    sigmoid = 1.0 / (1.0 + jnp.exp(-gate))
    act = gate * sigmoid
    hidden = (act * up).astype(bf16)
    weight = column_of(own_ref[:, CAP, :], core_ref[1])
    scaled_ref[...] = (hidden.astype(f32) * weight).astype(bf16)
    dot_ref[...] = nt(jnp.ones((8, 352), bf16), (hidden.astype(f32) * plain).astype(bf16))
    back = plain * weight
    dg = (back * up * (sigmoid * (1.0 + gate * (1.0 - sigmoid)))).astype(bf16)
    du = (back * act).astype(bf16)
    dg_ref[...] = dg
    du_ref[...] = du
    for z in range(2):
        mine = slice(z * QUARTER, (z + 1) * QUARTER)
        for back_ref, y_ref, which in (
            (back_own_ref, y_own_ref, core), (back_send_ref, y_send_ref, 1 - core),
        ):
            place = quarter_at(z, which)
            part = nn(dg, wg_ref[0, :, place]) + nn(du, wu_ref[0, :, place])
            back_ref[:, :, mine] = part.astype(bf16).reshape(groups, SLOTS, QUARTER)
            part = nn(hidden, wd_ref[0, :, place])
            y_ref[:, :, mine] = part.astype(bf16).reshape(groups, SLOTS, QUARTER)


def expert(e, core, own, other, grad_own, grad_other, wg, wu, wd):
    total, step = N_CTX * SLOTS, 512
    rows = pl.BlockSpec((step // SLOTS, SLOTS, HALF), lambda i: (i, 0, 0))
    grads = pl.BlockSpec((step // SLOTS, 1, SLOTS, HALF), lambda i: (i, e, 0, 0))
    weight = pl.BlockSpec((1, 352, WIDTH), lambda i: (e, 0, 0))
    units = pl.BlockSpec((step, 352), lambda i: (i, 0))
    return pl.pallas_call(
        expert_kernel,
        grid=(total // step,),
        in_specs=[pl.BlockSpec(memory_space=pltpu.SMEM), rows, rows, grads, grads]
        + [weight] * 3,
        out_specs=[rows] * 4 + [pl.BlockSpec((8, step), lambda i: (0, i))] + [units] * 3,
        out_shape=[out((N_CTX, SLOTS, HALF), bf16)] * 4
        + [out((8, total), f32)] + [out((total, 352), bf16)] * 3,
        compiler_params=pltpu.CompilerParams(vmem_limit_bytes=56 * MIB),
        cost_estimate=pl.CostEstimate(
            flops=12 * total * WIDTH * 352, bytes_accessed=24 * MIB, transcendentals=0
        ),
        name="expert",
    )(core, own, other, grad_own, grad_other, wg, wu, wd)


def finish_rows_kernel(core_ref, own_ref, arrived_ref, dot_ref, dot_arrived_ref, sent_ref):
    slot_row = lax.broadcasted_iota(jnp.int32, (N_CTX, SLOTS, HALF), 1)
    rows = own_ref[...].astype(f32) + arrived_ref[...].astype(f32)
    dots = (dot_ref[:1] + dot_arrived_ref[:1]).reshape(1, 1, HALF)
    sent_ref[...] = jnp.where(slot_row == CAP, dots, rows).astype(bf16)


def add_kernel(core_ref, own_ref, arrived_ref, sum_ref):
    sum_ref[...] = (own_ref[...].astype(f32) + arrived_ref[...].astype(f32)).astype(bf16)


def keys_kernel(slot_ref, own_ref, zl_ref, core_ref, keys_ref):
    zl, core = slot_ref[SEQ_BLOCKS], slot_ref[SEQ_BLOCKS + 1]

    def block(place, carry):
        slot = slot_ref[place]
        half, pair = slot // SEQ_PAIRS, lax.rem(slot, SEQ_PAIRS)
        mine = jnp.where(half == zl, own_ref[pair], zl_ref[pair])
        other = core_ref[jnp.where(half == zl, 0, 1), pair]
        start = pl.multiple_of(place * BLOCK, BLOCK)
        here = pl.multiple_of(start + core * 64, 64)
        there = pl.multiple_of(start + (1 - core) * 64, 64)
        keys_ref[pl.ds(here, 64), :] = mine
        keys_ref[pl.ds(there, 64), :] = other
        return carry

    lax.fori_loop(0, SEQ_BLOCKS, block, 0)


def key_split_kernel(place_ref, own_ref, arrived_ref, mine_ref, sent_ref):
    zl = place_ref[SEQ_BLOCKS]

    def pair(i, carry):
        here, there = place_ref[zl * SEQ_PAIRS + i], place_ref[(1 - zl) * SEQ_PAIRS + i]
        mine_ref[i] = own_ref[here].astype(f32) + arrived_ref[here].astype(f32)
        sent_ref[i] = (own_ref[there].astype(f32) + arrived_ref[there].astype(f32)).astype(bf16)
        return carry

    lax.fori_loop(0, SEQ_PAIRS, pair, 0)


def key_spread_kernel(pair_ref, mine_ref, arrived_ref, sent_ref):
    sent_ref[...] = jnp.zeros(sent_ref.shape, bf16)

    def pair(i, carry):
        sent_ref[pair_ref[i]] = (mine_ref[i] + arrived_ref[i].astype(f32)).astype(bf16)
        return carry

    lax.fori_loop(0, SEQ_PAIRS, pair, 0)


def latent_back_kernel(
    core_ref, back_ref, pre_ref, root_ref, gain_ref, cos_ref, sin_ref, grad_ref, gain_grad_ref
):
    total = jnp.zeros((64, KEYS), f32)
    for i in range(N_CTX):
        total = total + back_ref[i].astype(f32)
    normed_grad, pre, root = total[:, :RANK], pre_ref[...], root_ref[...]
    gain_grad_ref[...] = jnp.sum(normed_grad * pre * root, axis=0, keepdims=True)
    scaled = normed_grad * gain_ref[...]
    mean = jnp.sum(scaled * pre, axis=1, keepdims=True) * (1.0 / RANK)
    grad_ref[:, :RANK] = (root * scaled - pre * (root * root * root * mean)).astype(bf16)
    grad_ref[:, RANK:] = turned(total[:, RANK:], cos_ref[...], -sin_ref[...]).astype(bf16)


def input_back_kernel(
    core_ref, compressed_ref, down_ref, normed_ref, part_ref, input_ref, root_ref, gain_ref,
    own_ref, send_ref, gain_grad_ref, down_grad_ref, total_ref,
):
    core, zl = core_ref[0], core_ref[1]
    quarter = quarter_at(zl, core)
    compressed = compressed_ref[...]
    down_grad_ref[...] = tn(compressed, normed_ref[:, quarter]).astype(bf16)
    total_ref[...] = part_ref[...]
    total_ref[:, quarter] += nn(compressed, down_ref[...])
    grad, source, root = total_ref[...], input_ref[...].astype(f32), root_ref[...]
    gain_grad_ref[...] = jnp.sum(grad * source * root, axis=0, keepdims=True)
    scaled = grad * gain_ref[...]
    mean = jnp.sum(scaled * source, axis=1, keepdims=True) * (1.0 / WIDTH)
    total_ref[...] = root * scaled - source * (root * root * root * mean)
    for z in range(2):
        mine = slice(z * QUARTER, (z + 1) * QUARTER)
        own_ref[:, mine] = total_ref[:, quarter_at(z, core)]
        send_ref[:, mine] = total_ref[:, quarter_at(z, 1 - core)].astype(bf16)


def expert_grads_kernel(
    core_ref, one_ref, one_other_ref, two_ref, two_other_ref, ga_ref, gb_ref,
    scaled_one_ref, dg_one_ref, du_one_ref, scaled_two_ref, dg_two_ref, du_two_ref,
    wg_ref, wu_ref, wd_ref,
):
    mine = lax.rem(pl.program_id(1), 2) == core_ref[0]
    rows = N_CTX * SLOTS
    grad = jnp.where(mine, ga_ref[...], gb_ref[...]).reshape(rows, QUARTER)
    for e, (own_ref, other_ref, scaled_ref, dg_ref, du_ref) in enumerate(
        (
            (one_ref, one_other_ref, scaled_one_ref, dg_one_ref, du_one_ref),
            (two_ref, two_other_ref, scaled_two_ref, dg_two_ref, du_two_ref),
        )
    ):

        @pl.when(pl.program_id(0) == e)
        def _(own_ref=own_ref, other_ref=other_ref, scaled_ref=scaled_ref, dg_ref=dg_ref,
              du_ref=du_ref):
            x = jnp.where(mine, own_ref[...], other_ref[...]).reshape(rows, QUARTER)
            wg_ref[0] = tn(dg_ref[...], x)
            wu_ref[0] = tn(du_ref[...], x)
            wd_ref[0] = tn(scaled_ref[...], grad)


def expert_grads(core, rows, grads, units):
    total = N_CTX * SLOTS
    first = pl.BlockSpec(
        (N_CTX, SLOTS, QUARTER), lambda e, q: (0, 0, jnp.where(e == 0, q // 2, 1))
    )
    second = pl.BlockSpec(
        (N_CTX, SLOTS, QUARTER), lambda e, q: (0, 0, jnp.where(e == 0, 0, q // 2))
    )
    grad = pl.BlockSpec((N_CTX, 1, SLOTS, QUARTER), lambda e, q: (0, e, 0, q // 2))
    unit = pl.BlockSpec((total, 352), lambda e, q: (0, 0))
    result = pl.BlockSpec((1, 352, QUARTER), lambda e, q: (e, 0, q))
    return pl.pallas_call(
        expert_grads_kernel,
        grid=(EXP_DEV, 4),
        in_specs=[pl.BlockSpec(memory_space=pltpu.SMEM), first, first, second, second, grad, grad]
        + [unit] * 6,
        out_specs=[result] * 3,
        out_shape=[out((EXP_DEV, 352, WIDTH), f32)] * 3,
        compiler_params=pltpu.CompilerParams(vmem_limit_bytes=56 * MIB),
        cost_estimate=pl.CostEstimate(
            flops=12 * total * WIDTH * 352, bytes_accessed=36 * MIB, transcendentals=0
        ),
        name="expert_grads",
    )(core, *rows, *grads, *units)


def combine_kernel(
    core_ref, one_ref, two_ref, slot_ref, own_ref, arrived_ref, half_ref, prob_ref
):
    half = own_ref[...] + arrived_ref[...].astype(f32)
    for e, back_ref in enumerate((one_ref, two_ref)):
        part = slice(e * N_CTX, (e + 1) * N_CTX)
        hot = one_hot(slot_ref[part])
        half = half + tn(hot.astype(bf16), back_ref[...].reshape(N_CTX * SLOTS, HALF))
        dots = column_of(back_ref[:, CAP, :], core_ref[1])
        prob_ref[part] = jnp.sum((hot * dots).reshape(N_CTX, SLOTS, TOK), axis=1)
    half_ref[...] = half.astype(bf16)


def outputs_kernel(core_ref, back_ref, slot_ref, probs_ref, own_ref, arrived_ref, half_ref):
    hot = one_hot(slot_ref[...]).reshape(N_CTX, SLOTS, TOK) * probs_ref[...][:, None, :]
    half = own_ref[...] + arrived_ref[...].astype(f32)
    half_ref[...] = half + tn(
        hot.reshape(N_CTX * SLOTS, TOK).astype(bf16), back_ref[...].reshape(N_CTX * SLOTS, HALF)
    )


def weight_rows(attn_ref, z, group, first, last):
    return attn_ref[z, group * 4 : group * 4 + 4, :, first:last].reshape(256, last - first)


def up_rows(attn_ref, z, head, first):
    rows = attn_ref[z, :, head * 16 : head * 16 + 16, first : first + 128]
    return rows.reshape(256, 128)


def turned(values, cos, sin):
    flipped = jnp.concatenate([values[:, ROPE // 2 :], values[:, : ROPE // 2]], axis=1)
    return values * cos + flipped * sin


def query_kernel(core_ref, normed_ref, attn_ref, cos_ref, sin_ref, query_ref, nope_ref):
    rows = jnp.zeros((TOK, 768), f32)
    for z in range(2):
        for group in range(4):
            place = (z * 4 + group) * 256
            rows = rows + nn(
                normed_ref[:, place : place + 256], weight_rows(attn_ref, z, group, 0, 768)
            )
    for h in range(HEADS):
        nope = rows[:, h * 192 : h * 192 + NOPE].astype(bf16)
        rope = turned(rows[:, h * 192 + NOPE : (h + 1) * 192], cos_ref[...], sin_ref[...])
        nope_ref[h] = nope
        for z in range(2):
            query_ref[h, :, z * 256 : (z + 1) * 256] = nt(
                nope, up_rows(attn_ref, z, h, 1280)
            ).astype(bf16)
        query_ref[h, :, RANK:] = rope.astype(bf16)


def attend_kernel(
    place_ref, q_ref, k_ref, attn_ref,
    out_ref, log_ref, flat_ref, own_ref, send_ref, top_ref, sum_ref, acc_ref,
):
    owner, chunk = pl.program_id(0), pl.program_id(1)
    place, core = place_ref[owner], place_ref[2]

    @pl.when(chunk == 0)
    def _():
        top_ref[...] = jnp.full(top_ref.shape, -1e30, f32)
        sum_ref[...] = jnp.zeros(sum_ref.shape, f32)
        acc_ref[...] = jnp.zeros(acc_ref.shape, f32)

    @pl.when(chunk * (CHUNK // BLOCK) <= place)
    def _():
        q = q_ref[...].reshape(HEADS * BLOCK, KEYS)
        k = k_ref[pl.ds(chunk * CHUNK, CHUNK), :]
        scores = nt(q, k) * SCALE
        column = lax.broadcasted_iota(jnp.int32, scores.shape, 1) + chunk * CHUNK
        scores = jnp.where(column < (place + 1) * BLOCK, scores, -1e30)
        top_old = top_ref[...][:, :1]
        top = jnp.maximum(top_old, jnp.max(scores, axis=1, keepdims=True))
        weights = jnp.exp(scores - top)
        fade = jnp.exp(top_old - top)
        total = sum_ref[...][:, :1] * fade + jnp.sum(weights, axis=1, keepdims=True)
        acc_ref[...] = acc_ref[...] * fade + nn(weights.astype(bf16), k[:, :RANK])
        top_ref[...] = jnp.broadcast_to(top, top_ref.shape)
        sum_ref[...] = jnp.broadcast_to(total, sum_ref.shape)

    @pl.when(chunk == pl.num_programs(1) - 1)
    def _():
        total = sum_ref[...][:, :1]
        value = acc_ref[...] / total
        out_ref[...] = value.reshape(out_ref.shape)
        log_ref[...] = (top_ref[...] + jnp.log(sum_ref[...])).reshape(log_ref.shape)
        value = value.astype(bf16)
        for h in range(HEADS):
            rows = value[h * BLOCK : (h + 1) * BLOCK]
            head = nn(rows[:, :256], up_rows(attn_ref, 0, h, 1408))
            head = head + nn(rows[:, 256:], up_rows(attn_ref, 1, h, 1408))
            flat_ref[:, h * VDIM : (h + 1) * VDIM] = head.astype(bf16)
        flat = flat_ref[...]
        for z in range(2):
            mine = slice(z * QUARTER, (z + 1) * QUARTER)
            weight = attn_ref[z, pl.ds(core * 8, 8), :, 768:1280].reshape(QUARTER, QUARTER)
            own_ref[:, mine] = nt(flat, weight)
            weight = attn_ref[z, pl.ds(8 - core * 8, 8), :, 768:1280].reshape(QUARTER, QUARTER)
            send_ref[:, mine] = nt(flat, weight).astype(bf16)


def attend(places, query, keys, attn_all):
    rows = HEADS * BLOCK
    tokens = pl.BlockSpec((BLOCK, HALF), lambda o, c, p: (o, 0))
    return pl.pallas_call(
        attend_kernel,
        grid_spec=pltpu.PrefetchScalarGridSpec(
            num_scalar_prefetch=1,
            grid=(2, SEQ_BLOCKS * BLOCK // CHUNK),
            in_specs=[
                pl.BlockSpec((HEADS, 1, BLOCK, KEYS), lambda o, c, p: (0, o, 0, 0)),
                pl.BlockSpec((SEQ_BLOCKS * BLOCK, KEYS), lambda o, c, p: (0, 0)),
                pl.BlockSpec((2, 16, 64, 1536), lambda o, c, p: (0, 0, 0, 0)),
            ],
            out_specs=[
                pl.BlockSpec((HEADS, 1, BLOCK, RANK), lambda o, c, p: (0, o, 0, 0)),
                pl.BlockSpec((HEADS, 1, BLOCK, BLOCK), lambda o, c, p: (0, o, 0, 0)),
                pl.BlockSpec((BLOCK, HEADS * VDIM), lambda o, c, p: (o, 0)),
                tokens,
                tokens,
            ],
            scratch_shapes=[
                pltpu.VMEM((rows, 128), f32),
                pltpu.VMEM((rows, 128), f32),
                pltpu.VMEM((rows, RANK), f32),
            ],
        ),
        out_shape=[
            out((HEADS, 2, BLOCK, RANK), f32),
            out((HEADS, 2, BLOCK, BLOCK), f32),
            out((TOK, HEADS * VDIM), bf16),
            out((TOK, HALF), f32),
            out((TOK, HALF), bf16),
        ],
        compiler_params=pltpu.CompilerParams(vmem_limit_bytes=56 * MIB),
        cost_estimate=pl.CostEstimate(
            flops=2 * 2 * rows * 1280 * (KEYS + RANK), bytes_accessed=16 * MIB, transcendentals=0
        ),
        name="attend",
    )(places, query, keys, attn_all)


def back_kernel(
    core, own_ref, other_ref, sum_own_ref, sum_other_ref, input_ref, root_ref, gain_ref,
    grad_ref, router_ref, probs_ref, prob_grad_ref, attn_ref,
    after_grad_ref, attn_grad_ref, logit_ref, gain_grad_ref, head_ref, latent_ref,
):
    probs, prob_grad = probs_ref[...], prob_grad_ref[...]
    inner = jnp.sum(probs * prob_grad, axis=0, keepdims=True)
    logit_grad = (probs * (prob_grad - inner)).astype(bf16)
    logit_ref[...] = logit_grad
    after = input_ref[...].astype(f32) + whole_value(sum_own_ref[...], sum_other_ref[...], core)
    normed_grad = whole_value(own_ref[...], other_ref[...], core)
    normed_grad = normed_grad + tn(logit_grad, router_ref[...])
    root = root_ref[:, :1]
    gain_grad_ref[...] = jnp.sum(normed_grad * after * root, axis=0, keepdims=True)
    scaled = normed_grad * gain_ref[...]
    mean = jnp.sum(scaled * after, axis=1, keepdims=True) * (1.0 / WIDTH)
    after_grad = grad_ref[...].astype(f32) + root * scaled - after * (root * root * root * mean)
    after_grad_ref[...] = after_grad
    attn_grad = after_grad.astype(bf16)
    attn_grad_ref[...] = attn_grad
    head = jnp.zeros((TOK, QUARTER), f32)
    for z in range(2):
        for group in range(4):
            place = (z * 4 + group) * 256
            head = head + nn(
                attn_grad[:, place : place + 256], weight_rows(attn_ref, z, group, 768, 1280)
            )
    head = head.astype(bf16)
    head_ref[...] = head
    for h in range(HEADS):
        for z in range(2):
            latent_ref[h, :, z * 256 : (z + 1) * 256] = nt(
                head[:, h * VDIM : (h + 1) * VDIM], up_rows(attn_ref, z, h, 1408)
            ).astype(bf16)


def query_back_kernel(
    core_ref, dq_ref, nope_ref, normed_ref, attn_ref, cos_ref, sin_ref,
    value_ref, head_ref, attn_grad_ref, flat_ref, sums_ref, back_ref,
):
    parts = []
    for h in range(HEADS):
        lat = dq_ref[h, :, :RANK].astype(bf16)
        nope = nn(lat[:, :256], up_rows(attn_ref, 0, h, 1280))
        nope = nope + nn(lat[:, 256:], up_rows(attn_ref, 1, h, 1280))
        parts += [nope, turned(dq_ref[h, :, RANK:], cos_ref[...], -sin_ref[...])]
        heads = slice(h * 16, h * 16 + 16)
        key_grad = tn(lat, nope_ref[h]).astype(bf16)
        value_grad = tn(value_ref[h].astype(bf16), head_ref[:, h * VDIM : (h + 1) * VDIM])
        value_grad = value_grad.astype(bf16)
        for z in range(2):
            rows = slice(z * 256, (z + 1) * 256)
            sums_ref[:, z, heads, 1280:1408] = key_grad[rows].reshape(16, 16, 128)
            sums_ref[:, z, heads, 1408:1536] = value_grad[rows].reshape(16, 16, 128)
    query_grad = jnp.concatenate(parts, axis=1).astype(bf16)
    flat = flat_ref[...]
    for z in range(2):
        for group in range(4):
            place = slice((z * 4 + group) * 256, (z * 4 + group + 1) * 256)
            where = slice(group * 4, group * 4 + 4)
            sums_ref[where, z, :, :768] = (
                tn(normed_ref[:, place], query_grad).astype(bf16).reshape(4, 64, 768)
            )
            sums_ref[where, z, :, 768:1280] = (
                tn(attn_grad_ref[:, place], flat).astype(bf16).reshape(4, 64, QUARTER)
            )
            back_ref[:, place] = nt(query_grad, weight_rows(attn_ref, z, group, 0, 768))


def attend_back_kernel(
    place_ref, in_own_ref, in_other_ref, sum_own_ref, sum_other_ref, input_ref, root_ref, gain_ref,
    grad_ref, router_ref, probs_ref, prob_grad_ref, attn_ref, q_ref, k_ref, out_ref, log_ref,
    after_grad_ref, attn_grad_ref, logit_ref, gain_grad_ref, head_ref,
    dq_ref, own_ref, send_ref, latent_ref, inner_ref, dk_ref,
):
    owner, chunk = pl.program_id(0), pl.program_id(1)
    place, core = place_ref[owner], place_ref[2]
    rows = HEADS * BLOCK

    @pl.when((owner == 0) & (chunk == 0))
    def _():
        dk_ref[...] = jnp.zeros(dk_ref.shape, f32)
        back_kernel(
            core, in_own_ref, in_other_ref, sum_own_ref, sum_other_ref, input_ref, root_ref,
            gain_ref, grad_ref, router_ref, probs_ref, prob_grad_ref, attn_ref,
            after_grad_ref, attn_grad_ref, logit_ref, gain_grad_ref, head_ref, latent_ref,
        )

    tokens = pl.ds(pl.multiple_of(owner * BLOCK, BLOCK), BLOCK)

    @pl.when(chunk == 0)
    def _():
        dq_ref[...] = jnp.zeros(dq_ref.shape, f32)
        grad = latent_ref[:, tokens, :].reshape(rows, RANK)
        inner = jnp.sum(
            grad.astype(f32) * out_ref[...].reshape(rows, RANK), axis=1, keepdims=True
        )
        inner_ref[...] = jnp.broadcast_to(inner, inner_ref.shape)

    @pl.when(chunk * (CHUNK // BLOCK) <= place)
    def _():
        q = q_ref[...].reshape(rows, KEYS)
        grad = latent_ref[:, tokens, :].reshape(rows, RANK)
        part = pl.ds(chunk * CHUNK, CHUNK)
        k = k_ref[part, :]
        scores = nt(q, k) * SCALE
        column = lax.broadcasted_iota(jnp.int32, scores.shape, 1) + chunk * CHUNK
        log_total = log_ref[...].reshape(rows, BLOCK)[:, :1]
        probs = jnp.where(column < (place + 1) * BLOCK, jnp.exp(scores - log_total), 0.0)
        prob_back = nt(grad, k[:, :RANK])
        score_grad = (probs * (prob_back - inner_ref[...][:, :1])).astype(bf16)
        dq_ref[...] += (nn(score_grad, k) * SCALE).reshape(dq_ref.shape)
        dk_ref[part, :] += tn(score_grad, q) * SCALE
        dk_ref[part, :RANK] += tn(probs.astype(bf16), grad)

    @pl.when((owner == 1) & (chunk == pl.num_programs(1) - 1))
    def _():
        def block(i, carry):
            start = i * BLOCK
            own_ref[i] = dk_ref[pl.ds(pl.multiple_of(start + core * 64, 64), 64), :].astype(bf16)
            send_ref[i] = dk_ref[
                pl.ds(pl.multiple_of(start + (1 - core) * 64, 64), 64), :
            ].astype(bf16)
            return carry

        lax.fori_loop(0, SEQ_BLOCKS, block, 0)


def attend_back(places, *arrays):
    rows = HEADS * BLOCK

    def whole(array):
        zeros = (0,) * len(array.shape)
        return pl.BlockSpec(
            array.shape, lambda o, c, p: zeros, pipeline_mode=pl.Buffered(buffer_count=1)
        )

    def per_owner(width):
        return pl.BlockSpec((HEADS, 1, BLOCK, width), lambda o, c, p: (0, o, 0, 0))

    results = [
        out((TOK, WIDTH), f32),
        out((TOK, WIDTH), bf16),
        out((EXPERTS, TOK), bf16),
        out((1, WIDTH), f32),
        out((TOK, QUARTER), bf16),
    ]
    halves = [out((SEQ_BLOCKS, 64, KEYS), bf16)] * 2
    return pl.pallas_call(
        attend_back_kernel,
        grid_spec=pltpu.PrefetchScalarGridSpec(
            num_scalar_prefetch=1,
            grid=(2, SEQ_BLOCKS * BLOCK // CHUNK),
            in_specs=[whole(a) for a in arrays[:12]]
            + [per_owner(KEYS), whole(arrays[13]), per_owner(RANK), per_owner(BLOCK)],
            out_specs=[whole(a) for a in results] + [per_owner(KEYS)] + [whole(a) for a in halves],
            scratch_shapes=[
                pltpu.VMEM((HEADS, TOK, RANK), bf16),
                pltpu.VMEM((rows, 128), f32),
                pltpu.VMEM((SEQ_BLOCKS * BLOCK, KEYS), f32),
            ],
        ),
        out_shape=results + [out((HEADS, 2, BLOCK, KEYS), f32)] + halves,
        compiler_params=pltpu.CompilerParams(vmem_limit_bytes=58 * MIB),
        cost_estimate=pl.CostEstimate(
            flops=2 * 2 * rows * 1280 * 5 * KEYS, bytes_accessed=36 * MIB, transcendentals=0
        ),
        name="attend_back",
    )(places, *arrays)


def on_device(
    hidden_in,
    grad_out,
    block_ids,
    expert_ids,
    claim_order,
    attn_gain,
    latent_gain,
    ffn_gain,
    query_weight,
    latent_down,
    latent_up,
    output_weight,
    router_weight,
    expert_gate,
    expert_up,
    expert_down,
    shared_gate,
    shared_up,
    shared_down,
):
    ctx = lax.axis_index(CTX)
    zl = lax.axis_index("zl")
    core = lax.axis_index("core")
    ws = zl * 2 + core
    column_start = ws * QUARTER

    gains = jnp.concatenate([attn_gain, latent_gain, ffn_gain])
    gains = gather_two(gather_two(gains, "core", 0), "zl", 0).reshape(-1)
    small = jnp.concatenate(
        [
            latent_down.T,
            router_weight.T,
            jnp.pad(gains, (0, QUARTER - gains.shape[0]))[None],
            jnp.zeros((3, QUARTER), bf16),
        ],
        axis=0,
    )
    small_all = share_ctx(small, "small_weights")
    down_t = small_all[:, :18].reshape(KEYS, QUARTER)
    gains_all = small_all[:, 20, : 4 * 36].reshape(N_CTX, 4, 36).astype(f32)
    gain_one = gains_all[..., :16].reshape(-1)
    gain_kv = gains_all[..., 16:20].reshape(-1)
    gain_two = gains_all[..., 20:].reshape(-1)
    router_mine = small_all[:, 18:20]

    shared_pair_mine = gather_two(
        jnp.concatenate([shared_gate, shared_up, shared_down.T], axis=1), "zh", 0
    )
    up_mine = latent_up.reshape(16, HEADS, NOPE + VDIM).transpose(1, 0, 2).reshape(64, NOPE + VDIM)
    attn_all = gather_ctx(
        jnp.concatenate([query_weight, output_weight.T, up_mine], axis=1), "attn_weights"
    )

    core_is = jnp.stack([core, ctx])
    slot_by, grad_sent = call(
        cotangents_kernel,
        [out((EXPERTS, TOK), f32), out((N_CTX, EXP_DEV, SLOTS, HALF), bf16)],
        "cotangents",
        4 * N_CTX * SLOTS * TOK * HALF,
    )(
        core_is,
        jnp.pad(expert_ids.T, ((0, 2), (0, 0)), constant_values=-1),
        claim_order.reshape(1, TOK),
        claim_order.reshape(TOK, 1),
        grad_out,
    )

    local_ids = lax.dynamic_slice_in_dim(block_ids, ctx * 2, 2)
    places = local_ids % SEQ_BLOCKS
    sequence = local_ids[0] // SEQ_BLOCKS
    positions = (places[:, None] * BLOCK + jnp.arange(BLOCK)[None, :]).reshape(-1)
    pair_ids = block_ids.reshape(N_CTX, 2)
    in_seq = (pair_ids[:, 0] // SEQ_BLOCKS) == sequence
    rank = jnp.cumsum(in_seq.astype(jnp.int32)) - 1
    is_pair = in_seq[None, :] & (rank[None, :] == jnp.arange(SEQ_PAIRS)[:, None])
    pairs = jnp.sum(jnp.where(is_pair, jnp.arange(N_CTX)[None, :], 0), axis=1)
    pair_places = pair_ids[pairs] % SEQ_BLOCKS
    place_of = pair_places.T.reshape(-1)
    slot_of = jnp.sum(
        jnp.where(
            place_of[None, :] == jnp.arange(SEQ_BLOCKS)[:, None],
            jnp.arange(SEQ_BLOCKS)[None, :],
            0,
        ),
        axis=1,
    )

    inputs = hidden_in.astype(f32)
    root_one = lax.rsqrt(jnp.mean(inputs * inputs, axis=-1, keepdims=True) + EPSILON)
    normed_one = (inputs * root_one * gain_one).astype(bf16)
    normed_quarter = lax.dynamic_slice_in_dim(normed_one, column_start, QUARTER, 1)
    compressed_part = nt(normed_quarter, down_t).reshape(2, 2, 64, KEYS)
    compressed_half = pick(compressed_part, core, 1) + swap(
        pick(compressed_part, 1 - core, 1), "core"
    )
    compressed = pick(compressed_half, zl, 0) + swap(pick(compressed_half, 1 - zl, 0), "zl")
    row_start = ws * 64
    my_positions = lax.dynamic_slice_in_dim(positions, row_start, 64)
    latent_pre = compressed[:, :RANK]
    root_kv = lax.rsqrt(jnp.mean(latent_pre * latent_pre, axis=-1, keepdims=True) + EPSILON)
    latent_rows = jnp.concatenate(
        [
            (latent_pre * root_kv * gain_kv).astype(bf16),
            rotate(compressed[:, RANK:], my_positions, 1.0).astype(bf16),
        ],
        axis=1,
    )
    latent_ctx = after(share_ctx(latent_rows, "latents"), grad_sent)
    latent_mine = latent_ctx[pairs]
    latent_zl = swap(latent_mine, "zl")
    latent_core = swap(jnp.stack([latent_mine, latent_zl]), "core")
    (keys,) = call(keys_kernel, [out((SEQ_BLOCKS * BLOCK, KEYS), bf16)], "keys", 1)(
        jnp.concatenate([slot_of, jnp.stack([zl, core])]), latent_mine, latent_zl, latent_core
    )

    frequency = ROPE_BASE ** (-2.0 * jnp.arange(ROPE // 2, dtype=f32) / ROPE)
    angles = positions.astype(f32)[:, None] * frequency[None, :]
    cos = jnp.cos(angles)
    sin = jnp.sin(angles)
    cos, sin = jnp.concatenate([cos, cos], axis=1), jnp.concatenate([-sin, sin], axis=1)
    query, query_nope = call(
        query_kernel,
        [out((HEADS, TOK, KEYS), bf16), out((HEADS, TOK, NOPE), bf16)],
        "queries",
        2 * TOK * 768 * (WIDTH + RANK),
    )(core_is, normed_one, attn_all, cos, sin)
    query = query.reshape(HEADS, 2, BLOCK, KEYS)
    grad_own = exchange_ctx(grad_sent, "cotangent_rows", latent_core)
    grad_other = swap(grad_own, "core")
    places_core = jnp.concatenate([places, core[None]])
    value, log_total, head_flat, attn_own, attn_send = attend(places_core, query, keys, attn_all)
    attn_half = zl_sum(attn_own + swap(attn_send, "core").astype(f32))
    attn_other = swap(attn_half, "core")

    router_t = gather_two(gather_two(after(router_mine, keys), "zl", 0), "core", 1)
    router_t = router_t.transpose(3, 2, 0, 1, 4).reshape(EXPERTS, WIDTH)

    gain_row = gain_two.reshape(1, WIDTH)
    buffer = out((N_CTX, SLOTS, HALF), bf16)
    normed_two, root_two, probs, sent_one, sent_two = call(
        middle_kernel,
        [
            out((TOK, WIDTH), bf16),
            out((TOK, 128), f32),
            out((EXPERTS, TOK), f32),
            buffer,
            buffer,
        ],
        "middle",
        4 * N_CTX * SLOTS * TOK * HALF,
    )(core_is, attn_half, attn_other, hidden_in, gain_row, router_t, slot_by)

    weights = (expert_gate.transpose(0, 2, 1), expert_up.transpose(0, 2, 1), expert_down)
    one = exchange_ctx(sent_one, "rows_to_experts", grad_own)
    two = exchange_ctx(sent_two, "rows_to_experts", one)
    one_other = swap(one, "core")
    back_own, back_send, y_one, y_one_send, dots, *units_one = expert(
        0, core_is, one, one_other, grad_own, grad_other, *weights
    )
    two = after(two, dots)
    two_other = swap(two, "core")
    (sent_one,) = call(finish_rows_kernel, [buffer], "finish_rows", 1)(
        core_is, after(back_own, two), swap(back_send, "core"), dots, swap(dots, "core")
    )
    back_one = exchange_ctx(sent_one, "row_grads_back", two)
    back_own, back_send, y_two, y_two_send, dots, *units_two = expert(
        1, core_is, two, two_other, grad_own, grad_other, *weights
    )
    (sent_two,) = call(finish_rows_kernel, [buffer], "finish_rows", 1)(
        core_is, back_own, swap(after(back_send, back_one), "core"), dots,
        swap(after(dots, back_one), "core"),
    )
    back_two = exchange_ctx(sent_two, "row_grads_back", back_one)

    with jax.named_scope("shared_weights"):
        shared_all = lax.all_gather(after(shared_pair_mine, one), ("y", "x"), tiled=False)
    shared_own, shared_send, in_own, in_send, shared_grads = shared(
        core_is, after(normed_two, sent_two), grad_out, shared_all
    )
    back_two = after(back_two, in_own)

    in_half, prob_grad = call(
        combine_kernel,
        [out((TOK, HALF), bf16), out((EXPERTS, TOK), f32)],
        "combine",
        4 * N_CTX * SLOTS * TOK * HALF,
    )(core_is, back_one, back_two, slot_by, in_own, swap(in_send, "core"))
    (outs_one,) = call(add_kernel, [buffer], "outputs_sum", 1)(
        core_is, after(y_one, in_half), swap(y_one_send, "core")
    )
    prob_grad = prob_grad + swap(prob_grad, "zl")
    in_half = in_half.astype(f32) + swap(in_half, "zl").astype(f32)
    in_other = swap(in_half, "core")
    outs_one = exchange_ctx(after(outs_one, (in_other, prob_grad)), "outputs_back")
    (
        after_grad, attn_grad, logit_grad, gain_two_part, head_grad,
        grad_query_lat, keys_own, keys_send,
    ) = attend_back(
        places_core, in_half, in_other, attn_half, attn_other, hidden_in, root_two, gain_row,
        grad_out, router_t, probs, prob_grad, attn_all, query, keys, value, log_total,
    )
    grad_query_lat = grad_query_lat.reshape(HEADS, TOK, KEYS)
    normed_two_quarter = lax.dynamic_slice_in_dim(normed_two, column_start, QUARTER, 1)
    router_part = nn(logit_grad, normed_two_quarter).reshape(EXP_DEV, N_CTX, QUARTER)
    router_part = router_part.transpose(1, 0, 2)
    gain_two_mine = pick(gain_two_part.reshape(N_CTX, 4, 16), ws, 1)

    keys_mine, keys_other = call(
        key_split_kernel,
        [out((SEQ_PAIRS, 64, KEYS), f32), out((SEQ_PAIRS, 64, KEYS), bf16)],
        "key_split",
        1,
    )(jnp.concatenate([place_of, zl[None]]), after(keys_own, outs_one), swap(keys_send, "core"))
    (keys_sent,) = call(key_spread_kernel, [out((N_CTX, 64, KEYS), bf16)], "key_spread", 1)(
        pairs, keys_mine, swap(keys_other, "zl")
    )
    keys_back = exchange_ctx(keys_sent, "key_grads")

    attn_parts, normed_one_part = call(
        query_back_kernel,
        [out((16, 2, 64, 1536), bf16), out((TOK, WIDTH), f32)],
        "query_back",
        2 * TOK * WIDTH * 2048 + 2 * TOK * RANK * 1536,
    )(
        core_is, after(grad_query_lat, keys_other), query_nope, normed_one, attn_all, cos, sin,
        value.reshape(HEADS, TOK, RANK), head_grad, attn_grad, head_flat,
    )

    half_out = out((TOK, HALF), f32)
    (routed_half,) = call(outputs_kernel, [half_out], "outputs", 1)(
        core_is, after(outs_one, keys_sent), slot_by[:N_CTX], probs[:N_CTX],
        shared_own, swap(shared_send, "core"),
    )
    (outs_two,) = call(add_kernel, [buffer], "outputs_sum", 1)(
        core_is, after(y_two, keys_sent), swap(y_two_send, "core")
    )

    filled = expert_grads(
        core_is, (one, one_other, two, two_other), (grad_own, grad_other),
        (after(units_one[0], keys_sent), *units_one[1:], *units_two),
    )
    grad_expert_gate = filled[0].transpose(0, 2, 1)
    grad_expert_up = filled[1].transpose(0, 2, 1)
    grad_expert_down = filled[2]
    keys_back = after(keys_back, (filled[0], normed_one_part, routed_half, outs_two))

    compressed_grad, gain_kv_part = call(
        latent_back_kernel, [out((64, KEYS), bf16), out((1, RANK), f32)], "latent_back", 1
    )(
        core_is, keys_back, latent_pre, root_kv, gain_kv.reshape(1, RANK),
        lax.dynamic_slice_in_dim(cos, row_start, 64), lax.dynamic_slice_in_dim(sin, row_start, 64),
    )
    compressed_grad = gather_two(gather_two(compressed_grad, "core", 0), "zl", 0).reshape(TOK, KEYS)
    input_own, input_send, gain_one_part, grad_down_part = call(
        input_back_kernel,
        [
            out((TOK, HALF), f32),
            out((TOK, HALF), bf16),
            out((1, WIDTH), f32),
            out((KEYS, QUARTER), bf16),
        ],
        "input_back",
        4 * TOK * KEYS * QUARTER,
        [pltpu.VMEM((TOK, WIDTH), f32)],
    )(
        jnp.stack([core, zl]), compressed_grad, down_t, normed_one, normed_one_part, hidden_in,
        root_one, gain_one.reshape(1, WIDTH),
    )
    grad_down_part = grad_down_part.reshape(N_CTX, 18, QUARTER)
    input_quarter = zl_quarter(input_own + swap(input_send, "core").astype(f32), zl)
    grad_in = lax.dynamic_slice_in_dim(after_grad, column_start, QUARTER, 1) + input_quarter
    gain_parts = jnp.concatenate(
        [gain_one_part.reshape(N_CTX, 2, 2, 16), gain_kv_part.reshape(N_CTX, 2, 2, 4)], axis=-1
    )
    gain_core = pick(gain_parts, core, 2) + swap(pick(gain_parts, 1 - core, 2), "core")
    gain_mine = pick(gain_core, zl, 1) + swap(pick(gain_core, 1 - zl, 1), "zl")

    shared_pair = scatter_yx(
        after(shared_grads, back_two).reshape(WIDTH, 3 * FF_SH), "shared_weight_grads"
    )
    attn_pair = scatter_yx(
        after(attn_parts, shared_pair).reshape(WIDTH, 1536), "attn_weight_grads"
    )
    shared_sum = scatter_zh(shared_pair, "shared_weight_grads")
    attn_sum = scatter_zh(attn_pair, "attn_weight_grads")
    gain_rows = jnp.concatenate([gain_mine, gain_two_mine], axis=1)
    gain_rows = jnp.pad(gain_rows, ((0, 0), (0, QUARTER - 36)))[:, None, :]
    small_parts = jnp.concatenate(
        [
            grad_down_part,
            router_part.astype(bf16),
            gain_rows.astype(bf16),
            jnp.zeros((N_CTX, 3, QUARTER), bf16),
        ],
        axis=1,
    )
    small_back = exchange_ctx(small_parts, "small_weight_grads", keys_back)
    small_sum = jnp.sum(small_back.astype(f32), axis=0)
    outs_two = exchange_ctx(outs_two, "outputs_back", small_back)
    (routed_half,) = call(outputs_kernel, [half_out], "outputs", 1)(
        core_is, outs_two, slot_by[N_CTX:], probs[N_CTX:], routed_half,
        jnp.zeros((TOK, HALF), bf16),
    )
    layer_out = (
        lax.dynamic_slice_in_dim(hidden_in, column_start, QUARTER, 1).astype(f32)
        + lax.dynamic_slice_in_dim(attn_half, zl * QUARTER, QUARTER, 1)
        + zl_quarter(routed_half, zl)
    ).astype(bf16)
    up_sum = (
        attn_sum[:, 768 + QUARTER :]
        .reshape(HEADS, 16, NOPE + VDIM)
        .transpose(1, 0, 2)
        .reshape(16, HEADS * (NOPE + VDIM))
    )
    return (
        layer_out,
        grad_in,
        small_sum[20, :16],
        small_sum[20, 16:20],
        small_sum[20, 20:36],
        attn_sum[:, :768],
        small_sum[:18].T,
        up_sum,
        attn_sum[:, 768 : 768 + QUARTER].T,
        small_sum[18:20].T,
        grad_expert_gate,
        grad_expert_up,
        grad_expert_down,
        shared_sum[:, :FF_SH],
        shared_sum[:, FF_SH : 2 * FF_SH],
        shared_sum[:, 2 * FF_SH :].T,
    )


def solution(mesh):
    grid = Mesh(mesh.devices.reshape(2, 4, 4, 2, 2), CTX + ("zl", "core"))
    ctx, ws, both = CTX, ("zl", "core"), CTX + ("zl", "core")
    placed = (
        P(ctx, None),
        P(ctx, None),
        P(),
        P(ctx, None),
        P(ctx),
        P(both),
        P(both),
        P(both),
        P(ctx, ws),
        P(ws, ctx),
        P(ctx, ws),
        P(ws, ctx),
        P(ws, ctx),
        P(ctx, None, ws),
        P(ctx, None, ws),
        P(ctx, ws, None),
        P(ctx, ws),
        P(ctx, ws),
        P(ws, ctx),
    )
    return jax.shard_map(
        on_device,
        mesh=grid,
        in_specs=placed,
        out_specs=(
            P(ctx, ws),
            P(ctx, ws),
            P(both),
            P(both),
            P(both),
            P(ctx, ws),
            P(ws, ctx),
            P(ctx, ws),
            P(ws, ctx),
            P(ws, ctx),
            P(ctx, None, ws),
            P(ctx, None, ws),
            P(ctx, ws, None),
            P(ctx, ws),
            P(ctx, ws),
            P(ws, ctx),
        ),
        check_vma=False,
    )
```

```python
import jax
import jax.numpy as jnp
from jax import lax
from jax.experimental import pallas as pl
from jax.experimental.pallas import tpu as pltpu
from jax.sharding import Mesh
from jax.sharding import PartitionSpec as P

WIDTH = 2048
NOPE = 128
ROPE = 64
VDIM = 128
RANK = 512
KEYS = RANK + ROPE
HEADS = 4
EXPERTS = 64
EXP_DEV = 2
CAP = 30
TOPK = 6
SLOTS = 32
BLOCK = 128
SEQ_BLOCKS = 16
SEQ_PAIRS = 8
TOK = 256
QUARTER = 512
HALF = 1024
FF_SH = 704
N_CTX = 32
CHUNK = 512
EPSILON = 1e-06
ROPE_BASE = 10000.0
SCALE = (NOPE + ROPE) ** (-0.5)
CTX = ("zh", "y", "x")
MIB = 1 << 20

bf16 = jnp.bfloat16
f32 = jnp.float32


def dot(a, b, contract):
    return lax.dot_general(a, b, ((contract[0], contract[1]), ((), ())), preferred_element_type=f32)


def nn(a, b):
    return dot(a, b, ((1,), (0,)))


def nt(a, b):
    return dot(a, b, ((1,), (1,)))


def tn(a, b):
    return dot(a, b, ((0,), (0,)))


def rotate(values, positions, direction):
    half_width = values.shape[-1] // 2
    frequency = ROPE_BASE ** (-2.0 * jnp.arange(half_width, dtype=f32) / values.shape[-1])
    angles = positions.astype(f32)[:, None] * frequency[None, :]
    target_shape = (angles.shape[0],) + (1,) * (values.ndim - 2) + (half_width,)
    cosine = jnp.cos(angles).reshape(target_shape)
    sine_part = direction * jnp.sin(angles).reshape(target_shape)
    first_half = values[..., :half_width]
    second_half = values[..., half_width:]
    return jnp.concatenate(
        [
            first_half * cosine - second_half * sine_part,
            second_half * cosine + first_half * sine_part,
        ],
        axis=-1,
    )


def silu_slope(pre_act):
    sigmoid_val = jax.nn.sigmoid(pre_act)
    return sigmoid_val * (1.0 + pre_act * (1.0 - sigmoid_val))


def norm_back(upstream, source, inverse_root, gain_vec):
    scaled = upstream * gain_vec
    return inverse_root * scaled - source * inverse_root**3 * jnp.mean(
        scaled * source, axis=-1, keepdims=True
    )


def shift(value, axis, size, step):
    return lax.ppermute(value, axis, [(i, (i + step) % size) for i in range(size)])


def swap(value, axis):
    return shift(value, axis, 2, 1)


def pick(value, index, dim):
    return lax.dynamic_index_in_dim(value, index, dim, keepdims=False)


def gather_two(value, axis, dim):
    other = swap(value, axis)
    first = lax.axis_index(axis) == 0
    return jnp.stack(
        [jnp.where(first, value, other), jnp.where(first, other, value)], axis=dim
    )


def scatter_yx(value, name):
    with jax.named_scope(name):
        pair = lax.psum_scatter(value, ("y", "x"), scatter_dimension=0, tiled=True)
        return pair.reshape(2, -1, pair.shape[1])


def scatter_zh(pair, name):
    with jax.named_scope(name):
        here = lax.axis_index("zh")
        arrived = swap(pick(pair, 1 - here, 0), "zh")
        return pick(pair, here, 0).astype(f32) + arrived.astype(f32)


def after(value, earlier):
    return lax.optimization_barrier((value, earlier))[0]


def exchange_ctx(value, name, earlier=None):
    with jax.named_scope(name):
        if earlier is not None:
            value = after(value, earlier)
        return lax.all_to_all(value, CTX, 0, 0, tiled=True)


def share_ctx(value, name):
    return exchange_ctx(jnp.broadcast_to(value[None], (N_CTX,) + value.shape), name)


def half_of(value, core, dim=1):
    return jnp.concatenate(
        [
            lax.dynamic_slice_in_dim(value, core * QUARTER, QUARTER, dim),
            lax.dynamic_slice_in_dim(value, HALF + core * QUARTER, QUARTER, dim),
        ],
        axis=dim,
    )


def whole_of(own, other, core):
    first = jnp.where(core == 0, own, other)
    second = jnp.where(core == 0, other, own)
    return jnp.concatenate(
        [first[:, :QUARTER], second[:, :QUARTER], first[:, QUARTER:], second[:, QUARTER:]], axis=1
    )


def core_half(partial, core):
    arrived = swap(half_of(partial, 1 - core).astype(bf16), "core")
    return half_of(partial, core) + arrived.astype(f32)


def zl_sum(half):
    mine = half.astype(bf16)
    return mine.astype(f32) + swap(mine, "zl").astype(f32)


def zl_quarter(half, zl):
    arrived = swap(
        lax.dynamic_slice_in_dim(half, (1 - zl) * QUARTER, QUARTER, 1).astype(bf16), "zl"
    )
    return lax.dynamic_slice_in_dim(half, zl * QUARTER, QUARTER, 1) + arrived.astype(f32)


def call(body, outs, name, flops, scratch=(), limit=26):
    def run(scalars, *arrays):
        spec = pl.BlockSpec(memory_space=pltpu.VMEM)
        moved = sum(a.size * a.dtype.itemsize for a in arrays)
        moved += sum(o.size * o.dtype.itemsize for o in outs)
        return pl.pallas_call(
            body,
            in_specs=[pl.BlockSpec(memory_space=pltpu.SMEM)] + [spec] * len(arrays),
            out_specs=[spec] * len(outs),
            out_shape=outs,
            scratch_shapes=scratch,
            compiler_params=pltpu.CompilerParams(vmem_limit_bytes=limit * MIB),
            cost_estimate=pl.CostEstimate(
                flops=int(flops), bytes_accessed=int(moved), transcendentals=0
            ),
            name=name,
        )(scalars, *arrays)

    return run


def out(shape, kind):
    return jax.ShapeDtypeStruct(shape, kind)


def quarter_at(zl, core):
    return pl.ds(pl.multiple_of(zl * HALF + core * QUARTER, QUARTER), QUARTER)


def whole_value(own, other, core):
    first = jnp.where(core == 0, own, other)
    second = jnp.where(core == 0, other, own)
    return jnp.concatenate(
        [first[:, :QUARTER], second[:, :QUARTER], first[:, QUARTER:], second[:, QUARTER:]], axis=1
    )


def one_hot(slots):
    number = lax.broadcasted_iota(jnp.int32, (N_CTX, SLOTS, TOK), 1).astype(f32)
    hot = jnp.where(slots[:, None, :] == number, 1.0, 0.0)
    return hot.reshape(N_CTX * SLOTS, TOK)


def cotangents_kernel(core_ref, ids_ref, row_ref, col_ref, grad_ref, slot_ref, sent_ref):
    core = core_ref[0]
    row = lax.broadcasted_iota(jnp.int32, (EXPERTS, TOK), 0)
    expert = (row & (N_CTX - 1)) * 2 + (row >> 5)
    chosen = jnp.zeros((EXPERTS, TOK), f32)
    for k in range(TOPK):
        chosen = chosen + jnp.where(ids_ref[k : k + 1, :] == expert, 1.0, 0.0)
    before = jnp.where(col_ref[...] < row_ref[...], 1.0, 0.0).astype(bf16)
    earlier = nn(chosen.astype(bf16), before)
    slots = jnp.where((chosen > 0.5) & (earlier < CAP - 0.5), earlier, 99.0)
    slot_ref[...] = slots
    grad = jnp.concatenate([grad_ref[:, quarter_at(0, core)], grad_ref[:, quarter_at(1, core)]], 1)
    for e in range(EXP_DEV):
        hot = one_hot(slots[e * N_CTX : (e + 1) * N_CTX]).astype(bf16)
        sent_ref[:, e] = nn(hot, grad).astype(bf16).reshape(N_CTX, SLOTS, HALF)


def middle_kernel(
    core_ref, own_ref, other_ref, input_ref, gain_ref, router_ref, slot_ref,
    normed_ref, root_ref, probs_ref, sent_one_ref, sent_two_ref,
):
    core = core_ref[0]
    after = input_ref[...].astype(f32) + whole_value(own_ref[...], other_ref[...], core)
    root = lax.rsqrt(jnp.sum(after * after, axis=1, keepdims=True) * (1.0 / WIDTH) + EPSILON)
    normed = (after * root * gain_ref[...]).astype(bf16)
    normed_ref[...] = normed
    root_ref[...] = jnp.broadcast_to(root, root_ref.shape)
    logits = nt(router_ref[...], normed)
    weights = jnp.exp(logits - jnp.max(logits, axis=0, keepdims=True))
    probs = weights / jnp.sum(weights, axis=0, keepdims=True)
    probs_ref[...] = probs
    half = jnp.concatenate(
        [normed_ref[:, quarter_at(0, core)], normed_ref[:, quarter_at(1, core)]], axis=1
    )
    slot_row = lax.broadcasted_iota(jnp.int32, (N_CTX, SLOTS, HALF), 1)
    for e, sent_ref in enumerate((sent_one_ref, sent_two_ref)):
        part = slice(e * N_CTX, (e + 1) * N_CTX)
        hot = one_hot(slot_ref[part])
        gated = (hot.reshape(N_CTX, SLOTS, TOK) * probs[part][:, None, :]).astype(bf16)
        gate_row = nt(jnp.ones((8, TOK), bf16), gated.reshape(N_CTX * SLOTS, TOK))[:1]
        rows = nn(hot.astype(bf16), half).reshape(N_CTX, SLOTS, HALF)
        sent_ref[...] = jnp.where(slot_row == CAP, gate_row[None], rows).astype(bf16)


def column_of(row, ctx):
    groups = row.shape[0]
    lane = lax.broadcasted_iota(jnp.int32, (HALF, SLOTS), 0) - ctx * SLOTS
    picked = jnp.where(lane == lax.broadcasted_iota(jnp.int32, (HALF, SLOTS), 1), 1.0, 0.0)
    mine = nn(row.astype(bf16), picked.astype(bf16))
    square = (groups, SLOTS, SLOTS)
    same = lax.broadcasted_iota(jnp.int32, square, 1) == lax.broadcasted_iota(jnp.int32, square, 2)
    spread = jnp.where(same, mine[:, None, :], 0.0).reshape(groups * SLOTS, SLOTS)
    return jnp.sum(spread, axis=1, keepdims=True)


def shared_kernel(
    core_ref, normed_ref, grad_ref, weight_ref,
    own_ref, send_ref, in_own_ref, in_send_ref, grads_ref, pre_ref, back_ref,
):
    core = core_ref[0]

    def block(step):
        z, group = step // 4, lax.rem(step, 4)
        place = pl.ds(pl.multiple_of(step * 256, 256), 256)
        return z, group, place, weight_ref[pl.ds(group * 4, 4), z].reshape(256, 3 * FF_SH)

    pre_ref[...] = jnp.zeros(pre_ref.shape, f32)
    back_ref[...] = jnp.zeros(back_ref.shape, f32)

    def forward(step, carry):
        _, _, place, weight = block(step)
        pre_ref[...] += nn(normed_ref[:, place], weight[:, : 2 * FF_SH])
        back_ref[...] += nn(grad_ref[:, place], weight[:, 2 * FF_SH :])
        return carry

    lax.fori_loop(0, 8, forward, 0)
    gate, up, back = pre_ref[:, :FF_SH], pre_ref[:, FF_SH:], back_ref[...]
    sigmoid = 1.0 / (1.0 + jnp.exp(-gate))
    act = gate * sigmoid
    hidden = (act * up).astype(bf16)
    grad_gate = back * up * (sigmoid * (1.0 + gate * (1.0 - sigmoid)))
    grad_pre = jnp.concatenate([grad_gate, back * act], axis=1).astype(bf16)

    def backward(step, carry):
        z, group, place, weight = block(step)
        grads_ref[pl.ds(group * 4, 4), z, :, : 2 * FF_SH] = (
            tn(normed_ref[:, place], grad_pre).astype(bf16).reshape(4, 64, 2 * FF_SH)
        )
        grads_ref[pl.ds(group * 4, 4), z, :, 2 * FF_SH :] = (
            tn(grad_ref[:, place], hidden).astype(bf16).reshape(4, 64, FF_SH)
        )
        shared = nt(hidden, weight[:, 2 * FF_SH :])
        inner = nt(grad_pre, weight[:, : 2 * FF_SH])
        column = pl.ds(pl.multiple_of(z * QUARTER + lax.rem(group, 2) * 256, 256), 256)

        @pl.when(group // 2 == core)
        def _():
            own_ref[:, column] = shared
            in_own_ref[:, column] = inner

        @pl.when(group // 2 != core)
        def _():
            send_ref[:, column] = shared.astype(bf16)
            in_send_ref[:, column] = inner.astype(bf16)

        return carry

    lax.fori_loop(0, 8, backward, 0)


def shared(core, normed_two, grad_out, weights):
    run = pl.pallas_call(
        shared_kernel,
        in_specs=[pl.BlockSpec(memory_space=pltpu.SMEM)]
        + [pl.BlockSpec(memory_space=pltpu.VMEM)] * 3,
        out_specs=[pl.BlockSpec(memory_space=pltpu.VMEM)] * 5,
        out_shape=[
            out((TOK, HALF), f32),
            out((TOK, HALF), bf16),
            out((TOK, HALF), f32),
            out((TOK, HALF), bf16),
            out((16, 2, 64, 3 * FF_SH), bf16),
        ],
        scratch_shapes=[pltpu.VMEM((TOK, 2 * FF_SH), f32), pltpu.VMEM((TOK, FF_SH), f32)],
        compiler_params=pltpu.CompilerParams(vmem_limit_bytes=56 * MIB),
        cost_estimate=pl.CostEstimate(
            flops=18 * TOK * WIDTH * FF_SH, bytes_accessed=24 * MIB, transcendentals=0
        ),
        name="shared_experts",
    )
    return run(core, normed_two, grad_out, weights)


def expert_kernel(
    core_ref, own_ref, other_ref, grad_own_ref, grad_other_ref, wg_ref, wu_ref, wd_ref,
    back_own_ref, back_send_ref, y_own_ref, y_send_ref, dot_ref, scaled_ref, dg_ref, du_ref,
):
    core = core_ref[0]
    groups = own_ref.shape[0]
    rows = groups * SLOTS
    gate = jnp.zeros((rows, 352), f32)
    up = jnp.zeros((rows, 352), f32)
    plain = jnp.zeros((rows, 352), f32)
    for z in range(2):
        mine = slice(z * QUARTER, (z + 1) * QUARTER)
        for x_ref, g_ref, which in (
            (own_ref, grad_own_ref, core), (other_ref, grad_other_ref, 1 - core),
        ):
            place = quarter_at(z, which)
            x = x_ref[:, :, mine].reshape(rows, QUARTER)
            gate = gate + nt(x, wg_ref[0, :, place])
            up = up + nt(x, wu_ref[0, :, place])
            plain = plain + nt(g_ref[:, 0, :, mine].reshape(rows, QUARTER), wd_ref[0, :, place])
    sigmoid = 1.0 / (1.0 + jnp.exp(-gate))
    act = gate * sigmoid
    hidden = (act * up).astype(bf16)
    weight = column_of(own_ref[:, CAP, :], core_ref[1])
    scaled_ref[...] = (hidden.astype(f32) * weight).astype(bf16)
    dot_ref[...] = nt(jnp.ones((8, 352), bf16), (hidden.astype(f32) * plain).astype(bf16))
    back = plain * weight
    dg = (back * up * (sigmoid * (1.0 + gate * (1.0 - sigmoid)))).astype(bf16)
    du = (back * act).astype(bf16)
    dg_ref[...] = dg
    du_ref[...] = du
    for z in range(2):
        mine = slice(z * QUARTER, (z + 1) * QUARTER)
        for back_ref, y_ref, which in (
            (back_own_ref, y_own_ref, core), (back_send_ref, y_send_ref, 1 - core),
        ):
            place = quarter_at(z, which)
            part = nn(dg, wg_ref[0, :, place]) + nn(du, wu_ref[0, :, place])
            back_ref[:, :, mine] = part.astype(bf16).reshape(groups, SLOTS, QUARTER)
            part = nn(hidden, wd_ref[0, :, place])
            y_ref[:, :, mine] = part.astype(bf16).reshape(groups, SLOTS, QUARTER)


def expert(e, core, own, other, grad_own, grad_other, wg, wu, wd):
    total, step = N_CTX * SLOTS, 512
    rows = pl.BlockSpec((step // SLOTS, SLOTS, HALF), lambda i: (i, 0, 0))
    grads = pl.BlockSpec((step // SLOTS, 1, SLOTS, HALF), lambda i: (i, e, 0, 0))
    weight = pl.BlockSpec((1, 352, WIDTH), lambda i: (e, 0, 0))
    units = pl.BlockSpec((step, 352), lambda i: (i, 0))
    return pl.pallas_call(
        expert_kernel,
        grid=(total // step,),
        in_specs=[pl.BlockSpec(memory_space=pltpu.SMEM), rows, rows, grads, grads]
        + [weight] * 3,
        out_specs=[rows] * 4 + [pl.BlockSpec((8, step), lambda i: (0, i))] + [units] * 3,
        out_shape=[out((N_CTX, SLOTS, HALF), bf16)] * 4
        + [out((8, total), f32)] + [out((total, 352), bf16)] * 3,
        compiler_params=pltpu.CompilerParams(vmem_limit_bytes=56 * MIB),
        cost_estimate=pl.CostEstimate(
            flops=12 * total * WIDTH * 352, bytes_accessed=24 * MIB, transcendentals=0
        ),
        name="expert",
    )(core, own, other, grad_own, grad_other, wg, wu, wd)


def finish_rows_kernel(core_ref, own_ref, arrived_ref, dot_ref, dot_arrived_ref, sent_ref):
    slot_row = lax.broadcasted_iota(jnp.int32, own_ref.shape, 1)
    rows = own_ref[...].astype(f32) + arrived_ref[...].astype(f32)
    dots = (dot_ref[:1] + dot_arrived_ref[:1]).reshape(1, 1, HALF)
    sent_ref[...] = jnp.where(slot_row == CAP, dots, rows).astype(bf16)


def add_kernel(core_ref, own_ref, arrived_ref, sum_ref):
    sum_ref[...] = (own_ref[...].astype(f32) + arrived_ref[...].astype(f32)).astype(bf16)


def keys_kernel(slot_ref, own_ref, zl_ref, core_ref, keys_ref):
    zl, core = slot_ref[SEQ_BLOCKS], slot_ref[SEQ_BLOCKS + 1]

    def block(place, carry):
        slot = slot_ref[place]
        half, pair = slot // SEQ_PAIRS, lax.rem(slot, SEQ_PAIRS)
        mine = jnp.where(half == zl, own_ref[pair], zl_ref[pair])
        other = core_ref[jnp.where(half == zl, 0, 1), pair]
        start = pl.multiple_of(place * BLOCK, BLOCK)
        here = pl.multiple_of(start + core * 64, 64)
        there = pl.multiple_of(start + (1 - core) * 64, 64)
        keys_ref[pl.ds(here, 64), :] = mine
        keys_ref[pl.ds(there, 64), :] = other
        return carry

    lax.fori_loop(0, SEQ_BLOCKS, block, 0)


def key_split_kernel(place_ref, own_ref, arrived_ref, mine_ref, sent_ref):
    zl = place_ref[SEQ_BLOCKS]

    def pair(i, carry):
        here, there = place_ref[zl * SEQ_PAIRS + i], place_ref[(1 - zl) * SEQ_PAIRS + i]
        mine_ref[i] = own_ref[here].astype(f32) + arrived_ref[here].astype(f32)
        sent_ref[i] = (own_ref[there].astype(f32) + arrived_ref[there].astype(f32)).astype(bf16)
        return carry

    lax.fori_loop(0, SEQ_PAIRS, pair, 0)


def key_spread_kernel(pair_ref, mine_ref, arrived_ref, sent_ref):
    sent_ref[...] = jnp.zeros(sent_ref.shape, bf16)

    def pair(i, carry):
        sent_ref[pair_ref[i]] = (mine_ref[i] + arrived_ref[i].astype(f32)).astype(bf16)
        return carry

    lax.fori_loop(0, SEQ_PAIRS, pair, 0)


def latent_back_kernel(
    core_ref, back_ref, pre_ref, root_ref, gain_ref, cos_ref, sin_ref, grad_ref, gain_grad_ref
):
    total = jnp.zeros((64, KEYS), f32)
    for i in range(N_CTX):
        total = total + back_ref[i].astype(f32)
    normed_grad, pre, root = total[:, :RANK], pre_ref[...], root_ref[...]
    gain_grad_ref[...] = jnp.sum(normed_grad * pre * root, axis=0, keepdims=True)
    scaled = normed_grad * gain_ref[...]
    mean = jnp.sum(scaled * pre, axis=1, keepdims=True) * (1.0 / RANK)
    grad_ref[:, :RANK] = (root * scaled - pre * (root * root * root * mean)).astype(bf16)
    grad_ref[:, RANK:] = turned(total[:, RANK:], cos_ref[...], -sin_ref[...]).astype(bf16)


def input_back_kernel(
    core_ref, compressed_ref, down_ref, normed_ref, part_ref, input_ref, root_ref, gain_ref,
    logit_ref, normed_two_ref, gain_two_ref, gain_kv_ref,
    own_ref, send_ref, small_ref, total_ref,
):
    core, zl = core_ref[0], core_ref[1]
    quarter = quarter_at(zl, core)
    compressed = compressed_ref[...]
    total_ref[...] = part_ref[...]
    total_ref[:, quarter] += nn(compressed, down_ref[...])
    grad, source, root = total_ref[...], input_ref[...].astype(f32), root_ref[...]
    gain_one = jnp.sum(grad * source * root, axis=0, keepdims=True)
    scaled = grad * gain_ref[...]
    mean = jnp.sum(scaled * source, axis=1, keepdims=True) * (1.0 / WIDTH)
    total_ref[...] = root * scaled - source * (root * root * root * mean)
    for z in range(2):
        mine = slice(z * QUARTER, (z + 1) * QUARTER)
        own_ref[:, mine] = total_ref[:, quarter_at(z, core)]
        send_ref[:, mine] = total_ref[:, quarter_at(z, 1 - core)].astype(bf16)
    column = lax.broadcasted_iota(jnp.int32, (KEYS, N_CTX * 32), 1)
    place = (column >> 5) * 18 + (column & 31)
    same = (place == lax.broadcasted_iota(jnp.int32, place.shape, 0)) & ((column & 31) < 18)
    spread = nn(compressed, jnp.where(same, 1.0, 0.0).astype(bf16)).astype(bf16)
    down = tn(spread, normed_ref[:, quarter]).reshape(N_CTX, 32, QUARTER)
    router = nn(logit_ref[...], normed_two_ref[:, quarter])
    row = lax.broadcasted_iota(jnp.int32, down.shape, 1)
    small = down
    for e in range(EXP_DEV):
        small = jnp.where(row == 18 + e, router[e * N_CTX : (e + 1) * N_CTX][:, None, :], small)
    for k in range(4):
        part = slice(k * QUARTER, (k + 1) * QUARTER)
        small = jnp.where(row == 20 + k, gain_one[:, part][None], small)
        small = jnp.where(row == 24 + k, gain_two_ref[:, part][None], small)
    small = jnp.where(row == 28, gain_kv_ref[...][None], small)
    small_ref[...] = small.astype(bf16)


def expert_grads_kernel(
    core_ref, one_ref, one_other_ref, two_ref, two_other_ref, ga_ref, gb_ref,
    scaled_one_ref, dg_one_ref, du_one_ref, scaled_two_ref, dg_two_ref, du_two_ref,
    wg_ref, wu_ref, wd_ref,
):
    mine = lax.rem(pl.program_id(1), 2) == core_ref[0]
    rows = N_CTX * SLOTS
    grad = jnp.where(mine, ga_ref[...], gb_ref[...]).reshape(rows, QUARTER)
    for e, (own_ref, other_ref, scaled_ref, dg_ref, du_ref) in enumerate(
        (
            (one_ref, one_other_ref, scaled_one_ref, dg_one_ref, du_one_ref),
            (two_ref, two_other_ref, scaled_two_ref, dg_two_ref, du_two_ref),
        )
    ):

        @pl.when(pl.program_id(0) == e)
        def _(own_ref=own_ref, other_ref=other_ref, scaled_ref=scaled_ref, dg_ref=dg_ref,
              du_ref=du_ref):
            x = jnp.where(mine, own_ref[...], other_ref[...]).reshape(rows, QUARTER)
            wg_ref[0] = tn(dg_ref[...], x)
            wu_ref[0] = tn(du_ref[...], x)
            wd_ref[0] = tn(scaled_ref[...], grad)


def expert_grads(core, rows, grads, units):
    total = N_CTX * SLOTS
    first = pl.BlockSpec(
        (N_CTX, SLOTS, QUARTER), lambda e, q: (0, 0, jnp.where(e == 0, q // 2, 1))
    )
    second = pl.BlockSpec(
        (N_CTX, SLOTS, QUARTER), lambda e, q: (0, 0, jnp.where(e == 0, 0, q // 2))
    )
    grad = pl.BlockSpec((N_CTX, 1, SLOTS, QUARTER), lambda e, q: (0, e, 0, q // 2))
    unit = pl.BlockSpec((total, 352), lambda e, q: (0, 0))
    result = pl.BlockSpec((1, 352, QUARTER), lambda e, q: (e, 0, q))
    return pl.pallas_call(
        expert_grads_kernel,
        grid=(EXP_DEV, 4),
        in_specs=[pl.BlockSpec(memory_space=pltpu.SMEM), first, first, second, second, grad, grad]
        + [unit] * 6,
        out_specs=[result] * 3,
        out_shape=[out((EXP_DEV, 352, WIDTH), f32)] * 3,
        compiler_params=pltpu.CompilerParams(vmem_limit_bytes=56 * MIB),
        cost_estimate=pl.CostEstimate(
            flops=12 * total * WIDTH * 352, bytes_accessed=36 * MIB, transcendentals=0
        ),
        name="expert_grads",
    )(core, *rows, *grads, *units)


def combine_kernel(
    core_ref, one_ref, two_ref, slot_ref, own_ref, arrived_ref, half_ref, prob_ref
):
    half = own_ref[...] + arrived_ref[...].astype(f32)
    for e, back_ref in enumerate((one_ref, two_ref)):
        part = slice(e * N_CTX, (e + 1) * N_CTX)
        hot = one_hot(slot_ref[part])
        half = half + tn(hot.astype(bf16), back_ref[...].reshape(N_CTX * SLOTS, HALF))
        dots = column_of(back_ref[:, CAP, :], core_ref[1])
        prob_ref[part] = jnp.sum((hot * dots).reshape(N_CTX, SLOTS, TOK), axis=1)
    half_ref[...] = half.astype(bf16)


def outputs_two_kernel(core_ref, back_ref, slot_ref, probs_ref, own_ref, half_ref):
    hot = one_hot(slot_ref[...]).reshape(N_CTX, SLOTS, TOK) * probs_ref[...][:, None, :]
    hot = hot.reshape(N_CTX * SLOTS, TOK).astype(bf16)
    half_ref[...] = own_ref[...] + tn(hot, back_ref[...].reshape(N_CTX * SLOTS, HALF))


def outputs_kernel(core_ref, back_ref, slot_ref, probs_ref, own_ref, arrived_ref, half_ref):
    hot = one_hot(slot_ref[...]).reshape(N_CTX, SLOTS, TOK) * probs_ref[...][:, None, :]
    half = own_ref[...] + arrived_ref[...].astype(f32)
    half_ref[...] = half + tn(
        hot.reshape(N_CTX * SLOTS, TOK).astype(bf16), back_ref[...].reshape(N_CTX * SLOTS, HALF)
    )


def weight_rows(attn_ref, z, group, first, last):
    return attn_ref[z, group * 4 : group * 4 + 4, :, first:last].reshape(256, last - first)


def up_rows(attn_ref, z, head, first):
    rows = attn_ref[z, :, head * 16 : head * 16 + 16, first : first + 128]
    return rows.reshape(256, 128)


def turned(values, cos, sin):
    flipped = jnp.concatenate([values[:, ROPE // 2 :], values[:, : ROPE // 2]], axis=1)
    return values * cos + flipped * sin


def query_kernel(core_ref, normed_ref, attn_ref, cos_ref, sin_ref, query_ref, nope_ref):
    rows = jnp.zeros((TOK, 768), f32)
    for z in range(2):
        for group in range(4):
            place = (z * 4 + group) * 256
            rows = rows + nn(
                normed_ref[:, place : place + 256], weight_rows(attn_ref, z, group, 0, 768)
            )
    for h in range(HEADS):
        nope = rows[:, h * 192 : h * 192 + NOPE].astype(bf16)
        rope = turned(rows[:, h * 192 + NOPE : (h + 1) * 192], cos_ref[...], sin_ref[...])
        nope_ref[h] = nope
        for z in range(2):
            query_ref[h, :, z * 256 : (z + 1) * 256] = nt(
                nope, up_rows(attn_ref, z, h, 1280)
            ).astype(bf16)
        query_ref[h, :, RANK:] = rope.astype(bf16)


def attend_kernel(
    place_ref, q_ref, k_ref, attn_ref,
    out_ref, log_ref, flat_ref, own_ref, send_ref, top_ref, sum_ref, acc_ref,
):
    owner, chunk = pl.program_id(0), pl.program_id(1)
    place, core = place_ref[owner], place_ref[2]

    @pl.when(chunk == 0)
    def _():
        top_ref[...] = jnp.full(top_ref.shape, -1e30, f32)
        sum_ref[...] = jnp.zeros(sum_ref.shape, f32)
        acc_ref[...] = jnp.zeros(acc_ref.shape, f32)

    @pl.when(chunk * (CHUNK // BLOCK) <= place)
    def _():
        q = q_ref[...].reshape(HEADS * BLOCK, KEYS)
        k = k_ref[pl.ds(chunk * CHUNK, CHUNK), :]
        scores = nt(q, k) * SCALE
        column = lax.broadcasted_iota(jnp.int32, scores.shape, 1) + chunk * CHUNK
        scores = jnp.where(column < (place + 1) * BLOCK, scores, -1e30)
        top_old = top_ref[...][:, :1]
        top = jnp.maximum(top_old, jnp.max(scores, axis=1, keepdims=True))
        weights = jnp.exp(scores - top)
        fade = jnp.exp(top_old - top)
        total = sum_ref[...][:, :1] * fade + jnp.sum(weights, axis=1, keepdims=True)
        acc_ref[...] = acc_ref[...] * fade + nn(weights.astype(bf16), k[:, :RANK])
        top_ref[...] = jnp.broadcast_to(top, top_ref.shape)
        sum_ref[...] = jnp.broadcast_to(total, sum_ref.shape)

    @pl.when(chunk == pl.num_programs(1) - 1)
    def _():
        total = sum_ref[...][:, :1]
        value = acc_ref[...] / total
        out_ref[...] = value.reshape(out_ref.shape)
        log_ref[...] = (top_ref[...] + jnp.log(sum_ref[...])).reshape(log_ref.shape)
        value = value.astype(bf16)
        for h in range(HEADS):
            rows = value[h * BLOCK : (h + 1) * BLOCK]
            head = nn(rows[:, :256], up_rows(attn_ref, 0, h, 1408))
            head = head + nn(rows[:, 256:], up_rows(attn_ref, 1, h, 1408))
            flat_ref[:, h * VDIM : (h + 1) * VDIM] = head.astype(bf16)
        flat = flat_ref[...]
        for z in range(2):
            mine = slice(z * QUARTER, (z + 1) * QUARTER)
            weight = attn_ref[z, pl.ds(core * 8, 8), :, 768:1280].reshape(QUARTER, QUARTER)
            own_ref[:, mine] = nt(flat, weight)
            weight = attn_ref[z, pl.ds(8 - core * 8, 8), :, 768:1280].reshape(QUARTER, QUARTER)
            send_ref[:, mine] = nt(flat, weight).astype(bf16)


def attend(places, query, keys, attn_all):
    rows = HEADS * BLOCK
    tokens = pl.BlockSpec((BLOCK, HALF), lambda o, c, p: (o, 0))
    return pl.pallas_call(
        attend_kernel,
        grid_spec=pltpu.PrefetchScalarGridSpec(
            num_scalar_prefetch=1,
            grid=(2, SEQ_BLOCKS * BLOCK // CHUNK),
            in_specs=[
                pl.BlockSpec((HEADS, 1, BLOCK, KEYS), lambda o, c, p: (0, o, 0, 0)),
                pl.BlockSpec((SEQ_BLOCKS * BLOCK, KEYS), lambda o, c, p: (0, 0)),
                pl.BlockSpec((2, 16, 64, 1536), lambda o, c, p: (0, 0, 0, 0)),
            ],
            out_specs=[
                pl.BlockSpec((HEADS, 1, BLOCK, RANK), lambda o, c, p: (0, o, 0, 0)),
                pl.BlockSpec((HEADS, 1, BLOCK, BLOCK), lambda o, c, p: (0, o, 0, 0)),
                pl.BlockSpec((BLOCK, HEADS * VDIM), lambda o, c, p: (o, 0)),
                tokens,
                tokens,
            ],
            scratch_shapes=[
                pltpu.VMEM((rows, 128), f32),
                pltpu.VMEM((rows, 128), f32),
                pltpu.VMEM((rows, RANK), f32),
            ],
        ),
        out_shape=[
            out((HEADS, 2, BLOCK, RANK), f32),
            out((HEADS, 2, BLOCK, BLOCK), f32),
            out((TOK, HEADS * VDIM), bf16),
            out((TOK, HALF), f32),
            out((TOK, HALF), bf16),
        ],
        compiler_params=pltpu.CompilerParams(vmem_limit_bytes=56 * MIB),
        cost_estimate=pl.CostEstimate(
            flops=2 * 2 * rows * 1280 * (KEYS + RANK), bytes_accessed=16 * MIB, transcendentals=0
        ),
        name="attend",
    )(places, query, keys, attn_all)


def back_kernel(
    core, own_ref, other_ref, sum_own_ref, sum_other_ref, input_ref, root_ref, gain_ref,
    grad_ref, router_ref, probs_ref, prob_grad_ref, attn_ref,
    after_grad_ref, attn_grad_ref, logit_ref, gain_grad_ref, head_ref, latent_ref,
):
    probs, prob_grad = probs_ref[...], prob_grad_ref[...]
    inner = jnp.sum(probs * prob_grad, axis=0, keepdims=True)
    logit_grad = (probs * (prob_grad - inner)).astype(bf16)
    logit_ref[...] = logit_grad
    after = input_ref[...].astype(f32) + whole_value(sum_own_ref[...], sum_other_ref[...], core)
    normed_grad = whole_value(own_ref[...], other_ref[...], core)
    normed_grad = normed_grad + tn(logit_grad, router_ref[...])
    root = root_ref[:, :1]
    gain_grad_ref[...] = jnp.sum(normed_grad * after * root, axis=0, keepdims=True)
    scaled = normed_grad * gain_ref[...]
    mean = jnp.sum(scaled * after, axis=1, keepdims=True) * (1.0 / WIDTH)
    after_grad = grad_ref[...].astype(f32) + root * scaled - after * (root * root * root * mean)
    after_grad_ref[...] = after_grad
    attn_grad = after_grad.astype(bf16)
    attn_grad_ref[...] = attn_grad
    head = jnp.zeros((TOK, QUARTER), f32)
    for z in range(2):
        for group in range(4):
            place = (z * 4 + group) * 256
            head = head + nn(
                attn_grad[:, place : place + 256], weight_rows(attn_ref, z, group, 768, 1280)
            )
    head = head.astype(bf16)
    head_ref[...] = head
    for h in range(HEADS):
        for z in range(2):
            latent_ref[h, :, z * 256 : (z + 1) * 256] = nt(
                head[:, h * VDIM : (h + 1) * VDIM], up_rows(attn_ref, z, h, 1408)
            ).astype(bf16)


def query_back_kernel(
    core_ref, dq_ref, nope_ref, normed_ref, attn_ref, cos_ref, sin_ref,
    value_ref, head_ref, attn_grad_ref, flat_ref, sums_ref, back_ref,
):
    parts = []
    for h in range(HEADS):
        lat = dq_ref[h, :, :RANK].astype(bf16)
        nope = nn(lat[:, :256], up_rows(attn_ref, 0, h, 1280))
        nope = nope + nn(lat[:, 256:], up_rows(attn_ref, 1, h, 1280))
        parts += [nope, turned(dq_ref[h, :, RANK:], cos_ref[...], -sin_ref[...])]
        heads = slice(h * 16, h * 16 + 16)
        key_grad = tn(lat, nope_ref[h]).astype(bf16)
        value_grad = tn(value_ref[h].astype(bf16), head_ref[:, h * VDIM : (h + 1) * VDIM])
        value_grad = value_grad.astype(bf16)
        for z in range(2):
            rows = slice(z * 256, (z + 1) * 256)
            sums_ref[:, z, heads, 1280:1408] = key_grad[rows].reshape(16, 16, 128)
            sums_ref[:, z, heads, 1408:1536] = value_grad[rows].reshape(16, 16, 128)
    query_grad = jnp.concatenate(parts, axis=1).astype(bf16)
    flat = flat_ref[...]
    for z in range(2):
        for group in range(4):
            place = slice((z * 4 + group) * 256, (z * 4 + group + 1) * 256)
            where = slice(group * 4, group * 4 + 4)
            sums_ref[where, z, :, :768] = (
                tn(normed_ref[:, place], query_grad).astype(bf16).reshape(4, 64, 768)
            )
            sums_ref[where, z, :, 768:1280] = (
                tn(attn_grad_ref[:, place], flat).astype(bf16).reshape(4, 64, QUARTER)
            )
            back_ref[:, place] = nt(query_grad, weight_rows(attn_ref, z, group, 0, 768))


def attend_back_kernel(
    place_ref, in_own_ref, in_other_ref, sum_own_ref, sum_other_ref, input_ref, root_ref, gain_ref,
    grad_ref, router_ref, probs_ref, prob_grad_ref, attn_ref, q_ref, k_ref, out_ref, log_ref,
    after_grad_ref, attn_grad_ref, logit_ref, gain_grad_ref, head_ref,
    dq_ref, own_ref, send_ref, latent_ref, inner_ref, dk_ref,
):
    owner, chunk = pl.program_id(0), pl.program_id(1)
    place, core = place_ref[owner], place_ref[2]
    rows = HEADS * BLOCK

    @pl.when((owner == 0) & (chunk == 0))
    def _():
        dk_ref[...] = jnp.zeros(dk_ref.shape, f32)
        back_kernel(
            core, in_own_ref, in_other_ref, sum_own_ref, sum_other_ref, input_ref, root_ref,
            gain_ref, grad_ref, router_ref, probs_ref, prob_grad_ref, attn_ref,
            after_grad_ref, attn_grad_ref, logit_ref, gain_grad_ref, head_ref, latent_ref,
        )

    tokens = pl.ds(pl.multiple_of(owner * BLOCK, BLOCK), BLOCK)

    @pl.when(chunk == 0)
    def _():
        dq_ref[...] = jnp.zeros(dq_ref.shape, f32)
        grad = latent_ref[:, tokens, :].reshape(rows, RANK)
        inner = jnp.sum(
            grad.astype(f32) * out_ref[...].reshape(rows, RANK), axis=1, keepdims=True
        )
        inner_ref[...] = jnp.broadcast_to(inner, inner_ref.shape)

    @pl.when(chunk * (CHUNK // BLOCK) <= place)
    def _():
        q = q_ref[...].reshape(rows, KEYS)
        grad = latent_ref[:, tokens, :].reshape(rows, RANK)
        part = pl.ds(chunk * CHUNK, CHUNK)
        k = k_ref[part, :]
        scores = nt(q, k) * SCALE
        column = lax.broadcasted_iota(jnp.int32, scores.shape, 1) + chunk * CHUNK
        log_total = log_ref[...].reshape(rows, BLOCK)[:, :1]
        probs = jnp.where(column < (place + 1) * BLOCK, jnp.exp(scores - log_total), 0.0)
        prob_back = nt(grad, k[:, :RANK])
        score_grad = (probs * (prob_back - inner_ref[...][:, :1])).astype(bf16)
        dq_ref[...] += (nn(score_grad, k) * SCALE).reshape(dq_ref.shape)
        dk_ref[part, :] += tn(score_grad, q) * SCALE
        dk_ref[part, :RANK] += tn(probs.astype(bf16), grad)

    @pl.when((owner == 1) & (chunk == pl.num_programs(1) - 1))
    def _():
        def block(i, carry):
            start = i * BLOCK
            own_ref[i] = dk_ref[pl.ds(pl.multiple_of(start + core * 64, 64), 64), :].astype(bf16)
            send_ref[i] = dk_ref[
                pl.ds(pl.multiple_of(start + (1 - core) * 64, 64), 64), :
            ].astype(bf16)
            return carry

        lax.fori_loop(0, SEQ_BLOCKS, block, 0)


def attend_back(places, *arrays):
    rows = HEADS * BLOCK

    def whole(array):
        zeros = (0,) * len(array.shape)
        return pl.BlockSpec(
            array.shape, lambda o, c, p: zeros, pipeline_mode=pl.Buffered(buffer_count=1)
        )

    def per_owner(width):
        return pl.BlockSpec((HEADS, 1, BLOCK, width), lambda o, c, p: (0, o, 0, 0))

    results = [
        out((TOK, WIDTH), f32),
        out((TOK, WIDTH), bf16),
        out((EXPERTS, TOK), bf16),
        out((1, WIDTH), f32),
        out((TOK, QUARTER), bf16),
    ]
    halves = [out((SEQ_BLOCKS, 64, KEYS), bf16)] * 2
    return pl.pallas_call(
        attend_back_kernel,
        grid_spec=pltpu.PrefetchScalarGridSpec(
            num_scalar_prefetch=1,
            grid=(2, SEQ_BLOCKS * BLOCK // CHUNK),
            in_specs=[whole(a) for a in arrays[:12]]
            + [per_owner(KEYS), whole(arrays[13]), per_owner(RANK), per_owner(BLOCK)],
            out_specs=[whole(a) for a in results] + [per_owner(KEYS)] + [whole(a) for a in halves],
            scratch_shapes=[
                pltpu.VMEM((HEADS, TOK, RANK), bf16),
                pltpu.VMEM((rows, 128), f32),
                pltpu.VMEM((SEQ_BLOCKS * BLOCK, KEYS), f32),
            ],
        ),
        out_shape=results + [out((HEADS, 2, BLOCK, KEYS), f32)] + halves,
        compiler_params=pltpu.CompilerParams(vmem_limit_bytes=58 * MIB),
        cost_estimate=pl.CostEstimate(
            flops=2 * 2 * rows * 1280 * 5 * KEYS, bytes_accessed=36 * MIB, transcendentals=0
        ),
        name="attend_back",
    )(places, *arrays)


def on_device(
    hidden_in,
    grad_out,
    block_ids,
    expert_ids,
    claim_order,
    attn_gain,
    latent_gain,
    ffn_gain,
    query_weight,
    latent_down,
    latent_up,
    output_weight,
    router_weight,
    expert_gate,
    expert_up,
    expert_down,
    shared_gate,
    shared_up,
    shared_down,
):
    ctx = lax.axis_index(CTX)
    zl = lax.axis_index("zl")
    core = lax.axis_index("core")
    ws = zl * 2 + core
    column_start = ws * QUARTER

    gains = jnp.concatenate([attn_gain, latent_gain, ffn_gain])
    gains = gather_two(gather_two(gains, "core", 0), "zl", 0).reshape(-1)
    small = jnp.concatenate(
        [
            latent_down.T,
            router_weight.T,
            jnp.pad(gains, (0, QUARTER - gains.shape[0]))[None],
            jnp.zeros((3, QUARTER), bf16),
        ],
        axis=0,
    )
    small_all = share_ctx(small, "small_weights")
    down_t = small_all[:, :18].reshape(KEYS, QUARTER)
    gains_all = small_all[:, 20, : 4 * 36].reshape(N_CTX, 4, 36).astype(f32)
    gain_one = gains_all[..., :16].reshape(-1)
    gain_kv = gains_all[..., 16:20].reshape(-1)
    gain_two = gains_all[..., 20:].reshape(-1)
    router_mine = small_all[:, 18:20]

    shared_pair_mine = gather_two(
        jnp.concatenate([shared_gate, shared_up, shared_down.T], axis=1), "zh", 0
    )
    up_mine = latent_up.reshape(16, HEADS, NOPE + VDIM).transpose(1, 0, 2).reshape(64, NOPE + VDIM)
    with jax.named_scope("attn_weights"):
        attn_mine = jnp.concatenate([query_weight, output_weight.T, up_mine], axis=1)
        attn_all = lax.all_gather(attn_mine, CTX, tiled=False).reshape(2, 16, 64, 1536)

    core_is = jnp.stack([core, ctx])
    slot_by, grad_sent = call(
        cotangents_kernel,
        [out((EXPERTS, TOK), f32), out((N_CTX, EXP_DEV, SLOTS, HALF), bf16)],
        "cotangents",
        4 * N_CTX * SLOTS * TOK * HALF,
    )(
        core_is,
        jnp.pad(expert_ids.T, ((0, 2), (0, 0)), constant_values=-1),
        claim_order.reshape(1, TOK),
        claim_order.reshape(TOK, 1),
        grad_out,
    )

    local_ids = lax.dynamic_slice_in_dim(block_ids, ctx * 2, 2)
    places = local_ids % SEQ_BLOCKS
    sequence = local_ids[0] // SEQ_BLOCKS
    positions = (places[:, None] * BLOCK + jnp.arange(BLOCK)[None, :]).reshape(-1)
    pair_ids = block_ids.reshape(N_CTX, 2)
    in_seq = (pair_ids[:, 0] // SEQ_BLOCKS) == sequence
    rank = jnp.cumsum(in_seq.astype(jnp.int32)) - 1
    is_pair = in_seq[None, :] & (rank[None, :] == jnp.arange(SEQ_PAIRS)[:, None])
    pairs = jnp.sum(jnp.where(is_pair, jnp.arange(N_CTX)[None, :], 0), axis=1)
    pair_places = pair_ids[pairs] % SEQ_BLOCKS
    place_of = pair_places.T.reshape(-1)
    slot_of = jnp.sum(
        jnp.where(
            place_of[None, :] == jnp.arange(SEQ_BLOCKS)[:, None],
            jnp.arange(SEQ_BLOCKS)[None, :],
            0,
        ),
        axis=1,
    )

    inputs = hidden_in.astype(f32)
    root_one = lax.rsqrt(jnp.mean(inputs * inputs, axis=-1, keepdims=True) + EPSILON)
    normed_one = (inputs * root_one * gain_one).astype(bf16)
    normed_quarter = lax.dynamic_slice_in_dim(normed_one, column_start, QUARTER, 1)
    compressed_part = nt(normed_quarter, down_t).reshape(2, 2, 64, KEYS)
    compressed_half = pick(compressed_part, core, 1) + swap(
        pick(compressed_part, 1 - core, 1), "core"
    )
    compressed = pick(compressed_half, zl, 0) + swap(pick(compressed_half, 1 - zl, 0), "zl")
    row_start = ws * 64
    my_positions = lax.dynamic_slice_in_dim(positions, row_start, 64)
    latent_pre = compressed[:, :RANK]
    root_kv = lax.rsqrt(jnp.mean(latent_pre * latent_pre, axis=-1, keepdims=True) + EPSILON)
    latent_rows = jnp.concatenate(
        [
            (latent_pre * root_kv * gain_kv).astype(bf16),
            rotate(compressed[:, RANK:], my_positions, 1.0).astype(bf16),
        ],
        axis=1,
    )
    latent_ctx = after(share_ctx(after(latent_rows, shared_pair_mine), "latents"), grad_sent)
    latent_mine = latent_ctx[pairs]
    latent_zl = swap(latent_mine, "zl")
    latent_core = swap(jnp.stack([latent_mine, latent_zl]), "core")
    (keys,) = call(keys_kernel, [out((SEQ_BLOCKS * BLOCK, KEYS), bf16)], "keys", 1)(
        jnp.concatenate([slot_of, jnp.stack([zl, core])]), latent_mine, latent_zl, latent_core
    )

    frequency = ROPE_BASE ** (-2.0 * jnp.arange(ROPE // 2, dtype=f32) / ROPE)
    angles = positions.astype(f32)[:, None] * frequency[None, :]
    cos = jnp.cos(angles)
    sin = jnp.sin(angles)
    cos, sin = jnp.concatenate([cos, cos], axis=1), jnp.concatenate([-sin, sin], axis=1)
    query, query_nope = call(
        query_kernel,
        [out((HEADS, TOK, KEYS), bf16), out((HEADS, TOK, NOPE), bf16)],
        "queries",
        2 * TOK * 768 * (WIDTH + RANK),
    )(core_is, normed_one, attn_all, cos, sin)
    query = query.reshape(HEADS, 2, BLOCK, KEYS)
    grad_own = exchange_ctx(grad_sent, "cotangent_rows", latent_core)
    grad_other = swap(grad_own, "core")
    places_core = jnp.concatenate([places, core[None]])
    value, log_total, head_flat, attn_own, attn_send = attend(places_core, query, keys, attn_all)
    attn_half = zl_sum(attn_own + swap(attn_send, "core").astype(f32))
    attn_other = swap(attn_half, "core")

    router_t = gather_two(gather_two(after(router_mine, keys), "zl", 0), "core", 1)
    router_t = router_t.transpose(3, 2, 0, 1, 4).reshape(EXPERTS, WIDTH)

    gain_row = gain_two.reshape(1, WIDTH)
    buffer = out((N_CTX, SLOTS, HALF), bf16)
    normed_two, root_two, probs, sent_one, sent_two = call(
        middle_kernel,
        [
            out((TOK, WIDTH), bf16),
            out((TOK, 128), f32),
            out((EXPERTS, TOK), f32),
            buffer,
            buffer,
        ],
        "middle",
        4 * N_CTX * SLOTS * TOK * HALF,
    )(core_is, attn_half, attn_other, hidden_in, gain_row, router_t, slot_by)

    weights = (expert_gate.transpose(0, 2, 1), expert_up.transpose(0, 2, 1), expert_down)
    one = exchange_ctx(sent_one, "rows_to_experts", grad_own)
    two = exchange_ctx(sent_two, "rows_to_experts", one)
    one_other = swap(one, "core")
    back_own, back_send, y_one, y_one_send, dots, *units_one = expert(
        0, core_is, one, one_other, grad_own, grad_other, *weights
    )
    two = after(two, dots)
    two_other = swap(two, "core")
    (sent_one,) = call(finish_rows_kernel, [buffer], "finish_rows", 1, limit=20)(
        core_is, after(back_own, two), swap(back_send, "core"), dots, swap(dots, "core")
    )
    back_one = exchange_ctx(sent_one, "row_grads_back", two)
    back_own, back_send, y_two, y_two_send, dots, *units_two = expert(
        1, core_is, two, two_other, grad_own, grad_other, *weights
    )
    (sent_two,) = call(finish_rows_kernel, [buffer], "finish_rows", 1, limit=20)(
        core_is, back_own, swap(after(back_send, back_one), "core"), dots,
        swap(after(dots, back_one), "core"),
    )
    back_two = exchange_ctx(sent_two, "row_grads_back", back_one)

    with jax.named_scope("shared_weights"):
        shared_all = lax.all_gather(after(shared_pair_mine, latent_core), ("y", "x"), tiled=False)
    shared_own, shared_send, in_own, in_send, shared_grads = shared(
        core_is, after(normed_two, sent_two), grad_out, shared_all
    )
    (outs_one,) = call(add_kernel, [buffer], "outputs_sum", 1)(
        core_is, after(y_one, sent_two), swap(y_one_send, "core")
    )
    back_two = after(back_two, (in_own, outs_one))

    in_half, prob_grad = call(
        combine_kernel,
        [out((TOK, HALF), bf16), out((EXPERTS, TOK), f32)],
        "combine",
        4 * N_CTX * SLOTS * TOK * HALF,
    )(core_is, back_one, back_two, slot_by, in_own, swap(in_send, "core"))
    prob_grad = prob_grad + swap(prob_grad, "zl")
    in_half = in_half.astype(f32) + swap(in_half, "zl").astype(f32)
    in_other = swap(in_half, "core")
    outs_one = exchange_ctx(after(outs_one, (in_other, prob_grad)), "outputs_back")
    (
        after_grad, attn_grad, logit_grad, gain_two_part, head_grad,
        grad_query_lat, keys_own, keys_send,
    ) = attend_back(
        places_core, in_half, in_other, attn_half, attn_other, hidden_in, root_two, gain_row,
        grad_out, router_t, probs, prob_grad, attn_all, query, keys, value, log_total,
    )
    grad_query_lat = grad_query_lat.reshape(HEADS, TOK, KEYS)

    attn_parts, normed_one_part = call(
        query_back_kernel,
        [out((16, 2, 64, 1536), bf16), out((TOK, WIDTH), f32)],
        "query_back",
        2 * TOK * WIDTH * 2048 + 2 * TOK * RANK * 1536,
        limit=48,
    )(
        core_is, after(grad_query_lat, outs_one), query_nope, normed_one, attn_all, cos, sin,
        value.reshape(HEADS, TOK, RANK), head_grad, attn_grad, head_flat,
    )

    keys_mine, keys_other = call(
        key_split_kernel,
        [out((SEQ_PAIRS, 64, KEYS), f32), out((SEQ_PAIRS, 64, KEYS), bf16)],
        "key_split",
        1,
    )(jnp.concatenate([place_of, zl[None]]), after(keys_own, outs_one), swap(keys_send, "core"))
    keys_arrived = swap(keys_other, "zl")
    (keys_sent,) = call(key_spread_kernel, [out((N_CTX, 64, KEYS), bf16)], "key_spread", 1)(
        pairs, keys_mine, after(keys_arrived, normed_one_part)
    )
    (outs_two,) = call(add_kernel, [buffer], "outputs_sum", 1)(
        core_is, after(y_two, keys_sent), swap(y_two_send, "core")
    )
    keys_back = exchange_ctx(keys_sent, "key_grads")

    half_out = out((TOK, HALF), f32)
    (routed_half,) = call(outputs_kernel, [half_out], "outputs", 1)(
        core_is, after(outs_one, keys_sent), slot_by[:N_CTX], probs[:N_CTX],
        shared_own, swap(shared_send, "core"),
    )
    shared_pair = scatter_yx(
        after(shared_grads, back_two).reshape(WIDTH, 3 * FF_SH), "shared_weight_grads"
    )
    attn_pair = scatter_yx(
        after(attn_parts, (shared_pair, keys_sent)).reshape(WIDTH, 1536), "attn_weight_grads"
    )
    shared_sum = scatter_zh(shared_pair, "shared_weight_grads")

    filled = expert_grads(
        core_is, (one, one_other, two, two_other), (grad_own, grad_other),
        (after(units_one[0], keys_sent), *units_one[1:], *units_two),
    )
    grad_expert_gate = filled[0].transpose(0, 2, 1)
    grad_expert_up = filled[1].transpose(0, 2, 1)
    grad_expert_down = filled[2]

    keys_back = after(keys_back, (routed_half, shared_sum, filled[0], outs_two))
    compressed_grad, gain_kv_part = call(
        latent_back_kernel, [out((64, KEYS), bf16), out((1, RANK), f32)], "latent_back", 1
    )(
        core_is, keys_back, latent_pre, root_kv, gain_kv.reshape(1, RANK),
        lax.dynamic_slice_in_dim(cos, row_start, 64), lax.dynamic_slice_in_dim(sin, row_start, 64),
    )
    compressed_grad = gather_two(gather_two(compressed_grad, "core", 0), "zl", 0).reshape(TOK, KEYS)
    outs_two = exchange_ctx(after(outs_two, compressed_grad), "outputs_back")
    input_own, input_send, small_parts = call(
        input_back_kernel,
        [
            out((TOK, HALF), f32),
            out((TOK, HALF), bf16),
            out((N_CTX, 32, QUARTER), bf16),
        ],
        "input_back",
        4 * TOK * KEYS * QUARTER,
        [pltpu.VMEM((TOK, WIDTH), f32)],
    )(
        jnp.stack([core, zl]), compressed_grad, down_t, normed_one, normed_one_part, hidden_in,
        root_one, gain_one.reshape(1, WIDTH), logit_grad, normed_two, gain_two_part, gain_kv_part,
    )
    input_quarter = zl_quarter(input_own + swap(input_send, "core").astype(f32), zl)
    grad_in = lax.dynamic_slice_in_dim(after_grad, column_start, QUARTER, 1) + input_quarter

    attn_sum = scatter_zh(attn_pair, "attn_weight_grads")
    (routed_half,) = call(outputs_two_kernel, [half_out], "outputs_two", 1)(
        core_is, outs_two, slot_by[N_CTX:], probs[N_CTX:], routed_half
    )
    layer_out = (
        lax.dynamic_slice_in_dim(hidden_in, column_start, QUARTER, 1).astype(f32)
        + lax.dynamic_slice_in_dim(attn_half, zl * QUARTER, QUARTER, 1)
        + zl_quarter(routed_half, zl)
    ).astype(bf16)
    small_back = exchange_ctx(small_parts, "small_weight_grads", outs_two)
    small_back = after(small_back, (attn_sum, layer_out, grad_in))
    small_sum = jnp.sum(small_back.astype(f32), axis=0)
    lane = lax.rem(ctx, 8) * 64
    gain_one_rows = lax.dynamic_slice(small_sum, (20 + ctx // 8, lane), (1, 64))
    gain_two_rows = lax.dynamic_slice(small_sum, (24 + ctx // 8, lane), (1, 64))
    gain_kv_rows = lax.dynamic_slice(small_sum, (28, ctx * 16), (1, 16))
    gain_parts = jnp.concatenate(
        [gain_one_rows.reshape(2, 2, 16), gain_kv_rows.reshape(2, 2, 4)], axis=-1
    )
    gain_core = pick(gain_parts, core, 1) + swap(pick(gain_parts, 1 - core, 1), "core")
    gain_mine = pick(gain_core, zl, 0) + swap(pick(gain_core, 1 - zl, 0), "zl")
    gain_two_mine = lax.dynamic_slice_in_dim(gain_two_rows[0], ws * 16, 16)

    up_sum = (
        attn_sum[:, 768 + QUARTER :]
        .reshape(HEADS, 16, NOPE + VDIM)
        .transpose(1, 0, 2)
        .reshape(16, HEADS * (NOPE + VDIM))
    )
    return (
        layer_out,
        grad_in,
        gain_mine[:16],
        gain_mine[16:],
        gain_two_mine,
        attn_sum[:, :768],
        small_sum[:18].T,
        up_sum,
        attn_sum[:, 768 : 768 + QUARTER].T,
        small_sum[18:20].T,
        grad_expert_gate,
        grad_expert_up,
        grad_expert_down,
        shared_sum[:, :FF_SH],
        shared_sum[:, FF_SH : 2 * FF_SH],
        shared_sum[:, 2 * FF_SH :].T,
    )


def solution(mesh):
    grid = Mesh(mesh.devices.reshape(2, 4, 4, 2, 2), CTX + ("zl", "core"))
    ctx, ws, both = CTX, ("zl", "core"), CTX + ("zl", "core")
    placed = (
        P(ctx, None),
        P(ctx, None),
        P(),
        P(ctx, None),
        P(ctx),
        P(both),
        P(both),
        P(both),
        P(ctx, ws),
        P(ws, ctx),
        P(ctx, ws),
        P(ws, ctx),
        P(ws, ctx),
        P(ctx, None, ws),
        P(ctx, None, ws),
        P(ctx, ws, None),
        P(ctx, ws),
        P(ctx, ws),
        P(ws, ctx),
    )
    return jax.shard_map(
        on_device,
        mesh=grid,
        in_specs=placed,
        out_specs=(
            P(ctx, ws),
            P(ctx, ws),
            P(both),
            P(both),
            P(both),
            P(ctx, ws),
            P(ws, ctx),
            P(ctx, ws),
            P(ws, ctx),
            P(ws, ctx),
            P(ctx, None, ws),
            P(ctx, None, ws),
            P(ctx, ws, None),
            P(ctx, ws),
            P(ctx, ws),
            P(ws, ctx),
        ),
        check_vma=False,
    )
```

```python
import jax
import jax.numpy as jnp
from jax import lax
from jax.experimental import pallas as pl
from jax.experimental.pallas import tpu as pltpu
from jax.sharding import Mesh
from jax.sharding import PartitionSpec as P

WIDTH = 2048
NOPE = 128
ROPE = 64
VDIM = 128
RANK = 512
KEYS = RANK + ROPE
HEADS = 4
EXPERTS = 64
EXP_DEV = 2
CAP = 30
TOPK = 6
SLOTS = 32
BLOCK = 128
SEQ_BLOCKS = 16
SEQ_PAIRS = 8
TOK = 256
QUARTER = 512
HALF = 1024
FF_SH = 704
N_CTX = 32
CHUNK = 512
EPSILON = 1e-06
ROPE_BASE = 10000.0
SCALE = (NOPE + ROPE) ** (-0.5)
SCALE_TWO = SCALE * 1.4426950408889634
CTX = ("zh", "y", "x")
MIB = 1 << 20

bf16 = jnp.bfloat16
f32 = jnp.float32


def dot(a, b, contract):
    return lax.dot_general(a, b, ((contract[0], contract[1]), ((), ())), preferred_element_type=f32)


def nn(a, b):
    return dot(a, b, ((1,), (0,)))


def nt(a, b):
    return dot(a, b, ((1,), (1,)))


def tn(a, b):
    return dot(a, b, ((0,), (0,)))


def rotate(values, positions, direction):
    half_width = values.shape[-1] // 2
    frequency = ROPE_BASE ** (-2.0 * jnp.arange(half_width, dtype=f32) / values.shape[-1])
    angles = positions.astype(f32)[:, None] * frequency[None, :]
    target_shape = (angles.shape[0],) + (1,) * (values.ndim - 2) + (half_width,)
    cosine = jnp.cos(angles).reshape(target_shape)
    sine_part = direction * jnp.sin(angles).reshape(target_shape)
    first_half = values[..., :half_width]
    second_half = values[..., half_width:]
    return jnp.concatenate(
        [
            first_half * cosine - second_half * sine_part,
            second_half * cosine + first_half * sine_part,
        ],
        axis=-1,
    )


def silu_slope(pre_act):
    sigmoid_val = jax.nn.sigmoid(pre_act)
    return sigmoid_val * (1.0 + pre_act * (1.0 - sigmoid_val))


def norm_back(upstream, source, inverse_root, gain_vec):
    scaled = upstream * gain_vec
    return inverse_root * scaled - source * inverse_root**3 * jnp.mean(
        scaled * source, axis=-1, keepdims=True
    )


def shift(value, axis, size, step):
    return lax.ppermute(value, axis, [(i, (i + step) % size) for i in range(size)])


def swap(value, axis):
    return shift(value, axis, 2, 1)


def pick(value, index, dim):
    return lax.dynamic_index_in_dim(value, index, dim, keepdims=False)


def gather_two(value, axis, dim):
    other = swap(value, axis)
    first = lax.axis_index(axis) == 0
    return jnp.stack(
        [jnp.where(first, value, other), jnp.where(first, other, value)], axis=dim
    )


def scatter_yx(value, name):
    with jax.named_scope(name):
        pair = lax.psum_scatter(value, ("y", "x"), scatter_dimension=0, tiled=True)
        return pair.reshape(2, -1, pair.shape[1])


def scatter_zh(pair, name):
    with jax.named_scope(name):
        here = lax.axis_index("zh")
        arrived = swap(pick(pair, 1 - here, 0), "zh")
        return pick(pair, here, 0).astype(f32) + arrived.astype(f32)


def after(value, earlier):
    return lax.optimization_barrier((value, earlier))[0]


def exchange_ctx(value, name, earlier=None):
    with jax.named_scope(name):
        if earlier is not None:
            value = after(value, earlier)
        return lax.all_to_all(value, CTX, 0, 0, tiled=True)


def share_ctx(value, name):
    return exchange_ctx(jnp.broadcast_to(value[None], (N_CTX,) + value.shape), name)


def half_of(value, core, dim=1):
    return jnp.concatenate(
        [
            lax.dynamic_slice_in_dim(value, core * QUARTER, QUARTER, dim),
            lax.dynamic_slice_in_dim(value, HALF + core * QUARTER, QUARTER, dim),
        ],
        axis=dim,
    )


def whole_of(own, other, core):
    first = jnp.where(core == 0, own, other)
    second = jnp.where(core == 0, other, own)
    return jnp.concatenate(
        [first[:, :QUARTER], second[:, :QUARTER], first[:, QUARTER:], second[:, QUARTER:]], axis=1
    )


def core_half(partial, core):
    arrived = swap(half_of(partial, 1 - core).astype(bf16), "core")
    return half_of(partial, core) + arrived.astype(f32)


def zl_sum(half):
    mine = half.astype(bf16)
    return mine.astype(f32) + swap(mine, "zl").astype(f32)


def zl_quarter(half, zl):
    arrived = swap(
        lax.dynamic_slice_in_dim(half, (1 - zl) * QUARTER, QUARTER, 1).astype(bf16), "zl"
    )
    return lax.dynamic_slice_in_dim(half, zl * QUARTER, QUARTER, 1) + arrived.astype(f32)


def call(body, outs, name, flops, scratch=(), limit=26):
    def run(scalars, *arrays):
        spec = pl.BlockSpec(memory_space=pltpu.VMEM)
        moved = sum(a.size * a.dtype.itemsize for a in arrays)
        moved += sum(o.size * o.dtype.itemsize for o in outs)
        return pl.pallas_call(
            body,
            in_specs=[pl.BlockSpec(memory_space=pltpu.SMEM)] + [spec] * len(arrays),
            out_specs=[spec] * len(outs),
            out_shape=outs,
            scratch_shapes=scratch,
            compiler_params=pltpu.CompilerParams(vmem_limit_bytes=limit * MIB),
            cost_estimate=pl.CostEstimate(
                flops=int(flops), bytes_accessed=int(moved), transcendentals=0
            ),
            name=name,
        )(scalars, *arrays)

    return run


def out(shape, kind):
    return jax.ShapeDtypeStruct(shape, kind)


def quarter_at(zl, core):
    return pl.ds(pl.multiple_of(zl * HALF + core * QUARTER, QUARTER), QUARTER)


def whole_value(own, other, core):
    first = jnp.where(core == 0, own, other)
    second = jnp.where(core == 0, other, own)
    return jnp.concatenate(
        [first[:, :QUARTER], second[:, :QUARTER], first[:, QUARTER:], second[:, QUARTER:]], axis=1
    )


def one_hot(slots):
    number = lax.broadcasted_iota(jnp.int32, (N_CTX, SLOTS, TOK), 1).astype(f32)
    hot = jnp.where(slots[:, None, :] == number, 1.0, 0.0)
    return hot.reshape(N_CTX * SLOTS, TOK)


def cotangents_kernel(core_ref, ids_ref, row_ref, col_ref, grad_ref, slot_ref, sent_ref):
    core = core_ref[0]
    row = lax.broadcasted_iota(jnp.int32, (EXPERTS, TOK), 0)
    expert = (row & (N_CTX - 1)) * 2 + (row >> 5)
    chosen = jnp.zeros((EXPERTS, TOK), f32)
    for k in range(TOPK):
        chosen = chosen + jnp.where(ids_ref[k : k + 1, :] == expert, 1.0, 0.0)
    before = jnp.where(col_ref[...] < row_ref[...], 1.0, 0.0).astype(bf16)
    earlier = nn(chosen.astype(bf16), before)
    slots = jnp.where((chosen > 0.5) & (earlier < CAP - 0.5), earlier, 99.0)
    slot_ref[...] = slots
    grad = jnp.concatenate([grad_ref[:, quarter_at(0, core)], grad_ref[:, quarter_at(1, core)]], 1)
    for e in range(EXP_DEV):
        hot = one_hot(slots[e * N_CTX : (e + 1) * N_CTX]).astype(bf16)
        sent_ref[:, e] = nn(hot, grad).astype(bf16).reshape(N_CTX, SLOTS, HALF)


def router_kernel(core_ref, own_ref, zl_ref, core_two_ref, router_ref):
    core, zl = core_ref[0], core_ref[1]
    for e in range(EXP_DEV):
        rows = slice(e * N_CTX, (e + 1) * N_CTX)
        router_ref[rows, quarter_at(zl, core)] = own_ref[:, e, :]
        router_ref[rows, quarter_at(1 - zl, core)] = zl_ref[:, e, :]
        router_ref[rows, quarter_at(zl, 1 - core)] = core_two_ref[:, e, :]
        router_ref[rows, quarter_at(1 - zl, 1 - core)] = core_two_ref[:, 2 + e, :]


def middle_kernel(
    core_ref, own_ref, other_ref, input_ref, gain_ref, router_ref, slot_ref,
    normed_ref, root_ref, probs_ref, sent_one_ref, sent_two_ref,
):
    core = core_ref[0]
    after = input_ref[...].astype(f32) + whole_value(own_ref[...], other_ref[...], core)
    root = lax.rsqrt(jnp.sum(after * after, axis=1, keepdims=True) * (1.0 / WIDTH) + EPSILON)
    normed = (after * root * gain_ref[...]).astype(bf16)
    normed_ref[...] = normed
    root_ref[...] = jnp.broadcast_to(root, root_ref.shape)
    logits = nt(router_ref[...], normed)
    weights = jnp.exp(logits - jnp.max(logits, axis=0, keepdims=True))
    probs = weights / jnp.sum(weights, axis=0, keepdims=True)
    probs_ref[...] = probs
    half = jnp.concatenate(
        [normed_ref[:, quarter_at(0, core)], normed_ref[:, quarter_at(1, core)]], axis=1
    )
    slot_row = lax.broadcasted_iota(jnp.int32, (N_CTX, SLOTS, HALF), 1)
    for e, sent_ref in enumerate((sent_one_ref, sent_two_ref)):
        part = slice(e * N_CTX, (e + 1) * N_CTX)
        hot = one_hot(slot_ref[part])
        gated = (hot.reshape(N_CTX, SLOTS, TOK) * probs[part][:, None, :]).astype(bf16)
        gate_row = nt(jnp.ones((8, TOK), bf16), gated.reshape(N_CTX * SLOTS, TOK))[:1]
        rows = nn(hot.astype(bf16), half).reshape(N_CTX, SLOTS, HALF)
        sent_ref[...] = jnp.where(slot_row == CAP, gate_row[None], rows).astype(bf16)


def column_of(row, ctx):
    groups = row.shape[0]
    lane = lax.broadcasted_iota(jnp.int32, (HALF, SLOTS), 0) - ctx * SLOTS
    picked = jnp.where(lane == lax.broadcasted_iota(jnp.int32, (HALF, SLOTS), 1), 1.0, 0.0)
    mine = nn(row.astype(bf16), picked.astype(bf16))
    square = (groups, SLOTS, SLOTS)
    same = lax.broadcasted_iota(jnp.int32, square, 1) == lax.broadcasted_iota(jnp.int32, square, 2)
    spread = jnp.where(same, mine[:, None, :], 0.0).reshape(groups * SLOTS, SLOTS)
    return jnp.sum(spread, axis=1, keepdims=True)


def shared_kernel(
    core_ref, normed_ref, grad_ref, weight_ref,
    own_ref, send_ref, in_own_ref, in_send_ref, grads_ref, pre_ref, back_ref,
):
    core = core_ref[0]

    def block(step):
        z, group = step // 4, lax.rem(step, 4)
        place = pl.ds(pl.multiple_of(step * 256, 256), 256)
        return z, group, place, weight_ref[pl.ds(group * 4, 4), z].reshape(256, 3 * FF_SH)

    pre_ref[...] = jnp.zeros(pre_ref.shape, f32)
    back_ref[...] = jnp.zeros(back_ref.shape, f32)

    def forward(step, carry):
        _, _, place, weight = block(step)
        pre_ref[...] += nn(normed_ref[:, place], weight[:, : 2 * FF_SH])
        back_ref[...] += nn(grad_ref[:, place], weight[:, 2 * FF_SH :])
        return carry

    lax.fori_loop(0, 8, forward, 0)
    gate, up, back = pre_ref[:, :FF_SH], pre_ref[:, FF_SH:], back_ref[...]
    sigmoid = 1.0 / (1.0 + jnp.exp(-gate))
    act = gate * sigmoid
    hidden = (act * up).astype(bf16)
    grad_gate = back * up * (sigmoid * (1.0 + gate * (1.0 - sigmoid)))
    grad_pre = jnp.concatenate([grad_gate, back * act], axis=1).astype(bf16)

    def backward(step, carry):
        z, group, place, weight = block(step)
        grads_ref[pl.ds(group * 4, 4), z, :, : 2 * FF_SH] = (
            tn(normed_ref[:, place], grad_pre).astype(bf16).reshape(4, 64, 2 * FF_SH)
        )
        grads_ref[pl.ds(group * 4, 4), z, :, 2 * FF_SH :] = (
            tn(grad_ref[:, place], hidden).astype(bf16).reshape(4, 64, FF_SH)
        )
        shared = nt(hidden, weight[:, 2 * FF_SH :])
        inner = nt(grad_pre, weight[:, : 2 * FF_SH])
        column = pl.ds(pl.multiple_of(z * QUARTER + lax.rem(group, 2) * 256, 256), 256)

        @pl.when(group // 2 == core)
        def _():
            own_ref[:, column] = shared
            in_own_ref[:, column] = inner

        @pl.when(group // 2 != core)
        def _():
            send_ref[:, column] = shared.astype(bf16)
            in_send_ref[:, column] = inner.astype(bf16)

        return carry

    lax.fori_loop(0, 8, backward, 0)


def shared(core, normed_two, grad_out, weights):
    run = pl.pallas_call(
        shared_kernel,
        in_specs=[pl.BlockSpec(memory_space=pltpu.SMEM)]
        + [pl.BlockSpec(memory_space=pltpu.VMEM)] * 3,
        out_specs=[pl.BlockSpec(memory_space=pltpu.VMEM)] * 5,
        out_shape=[
            out((TOK, HALF), f32),
            out((TOK, HALF), bf16),
            out((TOK, HALF), f32),
            out((TOK, HALF), bf16),
            out((16, 2, 64, 3 * FF_SH), bf16),
        ],
        scratch_shapes=[pltpu.VMEM((TOK, 2 * FF_SH), f32), pltpu.VMEM((TOK, FF_SH), f32)],
        compiler_params=pltpu.CompilerParams(vmem_limit_bytes=40 * MIB),
        cost_estimate=pl.CostEstimate(
            flops=18 * TOK * WIDTH * FF_SH, bytes_accessed=24 * MIB, transcendentals=0
        ),
        name="shared_experts",
    )
    return run(core, normed_two, grad_out, weights)


def expert_kernel(
    core_ref, own_ref, other_ref, grad_own_ref, grad_other_ref, wg_ref, wu_ref, wd_ref,
    back_own_ref, back_send_ref, y_own_ref, y_send_ref, scaled_ref, dg_ref, du_ref,
):
    core = core_ref[0]
    groups = own_ref.shape[0]
    rows = groups * SLOTS
    gate = jnp.zeros((rows, 352), f32)
    up = jnp.zeros((rows, 352), f32)
    plain = jnp.zeros((rows, 352), f32)
    for z in range(2):
        mine = slice(z * QUARTER, (z + 1) * QUARTER)
        for x_ref, g_ref, which in (
            (own_ref, grad_own_ref, core), (other_ref, grad_other_ref, 1 - core),
        ):
            place = quarter_at(z, which)
            x = x_ref[:, :, mine].reshape(rows, QUARTER)
            gate = gate + nt(x, wg_ref[0, :, place])
            up = up + nt(x, wu_ref[0, :, place])
            plain = plain + nt(g_ref[:, 0, :, mine].reshape(rows, QUARTER), wd_ref[0, :, place])
    sigmoid = 1.0 / (1.0 + jnp.exp(-gate))
    act = gate * sigmoid
    hidden = (act * up).astype(bf16)
    weight = column_of(own_ref[:, CAP, :], core_ref[1])
    scaled_ref[...] = (hidden.astype(f32) * weight).astype(bf16)
    dots = nt(jnp.ones((8, 352), bf16), (hidden.astype(f32) * plain).astype(bf16))[:1]
    back = plain * weight
    dg = (back * up * (sigmoid * (1.0 + gate * (1.0 - sigmoid)))).astype(bf16)
    du = (back * act).astype(bf16)
    dg_ref[...] = dg
    du_ref[...] = du
    for z in range(2):
        mine = slice(z * QUARTER, (z + 1) * QUARTER)
        for back_ref, y_ref, which in (
            (back_own_ref, y_own_ref, core), (back_send_ref, y_send_ref, 1 - core),
        ):
            place = quarter_at(z, which)
            part = nn(dg, wg_ref[0, :, place]) + nn(du, wu_ref[0, :, place])
            back_ref[:, :, mine] = part.astype(bf16).reshape(groups, SLOTS, QUARTER)
            part = nn(hidden, wd_ref[0, :, place])
            y_ref[:, :, mine] = part.astype(bf16).reshape(groups, SLOTS, QUARTER)
    lanes = pl.ds(pl.multiple_of(pl.program_id(0) * rows, rows), rows)
    for back_ref in (back_own_ref, back_send_ref):
        back_ref[:, CAP, lanes] = jnp.broadcast_to(dots.astype(bf16), (groups, rows))


def expert(e, core, own, other, grad_own, grad_other, wg, wu, wd):
    total, step = N_CTX * SLOTS, 512
    rows = pl.BlockSpec((step // SLOTS, SLOTS, HALF), lambda i: (i, 0, 0))
    grads = pl.BlockSpec((step // SLOTS, 1, SLOTS, HALF), lambda i: (i, e, 0, 0))
    weight = pl.BlockSpec((1, 352, WIDTH), lambda i: (e, 0, 0))
    units = pl.BlockSpec((step, 352), lambda i: (i, 0))
    return pl.pallas_call(
        expert_kernel,
        grid=(total // step,),
        in_specs=[pl.BlockSpec(memory_space=pltpu.SMEM), rows, rows, grads, grads]
        + [weight] * 3,
        out_specs=[rows] * 4 + [units] * 3,
        out_shape=[out((N_CTX, SLOTS, HALF), bf16)] * 4 + [out((total, 352), bf16)] * 3,
        compiler_params=pltpu.CompilerParams(vmem_limit_bytes=56 * MIB),
        cost_estimate=pl.CostEstimate(
            flops=12 * total * WIDTH * 352, bytes_accessed=24 * MIB, transcendentals=0
        ),
        name="expert",
    )(core, own, other, grad_own, grad_other, wg, wu, wd)


def add_kernel(core_ref, own_ref, arrived_ref, sum_ref):
    sum_ref[...] = (own_ref[...].astype(f32) + arrived_ref[...].astype(f32)).astype(bf16)


def keys_kernel(slot_ref, own_ref, zl_ref, core_ref, keys_ref):
    zl, core = slot_ref[SEQ_BLOCKS], slot_ref[SEQ_BLOCKS + 1]

    def block(place, carry):
        slot = slot_ref[place]
        half, pair = slot // SEQ_PAIRS, lax.rem(slot, SEQ_PAIRS)
        mine = jnp.where(half == zl, own_ref[pair], zl_ref[pair])
        other = core_ref[jnp.where(half == zl, 0, 1), pair]
        start = pl.multiple_of(place * BLOCK, BLOCK)
        here = pl.multiple_of(start + core * 64, 64)
        there = pl.multiple_of(start + (1 - core) * 64, 64)
        keys_ref[pl.ds(here, 64), :] = mine
        keys_ref[pl.ds(there, 64), :] = other
        return carry

    lax.fori_loop(0, SEQ_BLOCKS, block, 0)


def key_split_kernel(place_ref, own_ref, arrived_ref, mine_ref, sent_ref):
    zl = place_ref[SEQ_BLOCKS]

    def pair(i, carry):
        here, there = place_ref[zl * SEQ_PAIRS + i], place_ref[(1 - zl) * SEQ_PAIRS + i]
        mine_ref[i] = own_ref[here].astype(f32) + arrived_ref[here].astype(f32)
        sent_ref[i] = (own_ref[there].astype(f32) + arrived_ref[there].astype(f32)).astype(bf16)
        return carry

    lax.fori_loop(0, SEQ_PAIRS, pair, 0)


def key_spread_kernel(pair_ref, mine_ref, arrived_ref, sent_ref):
    sent_ref[...] = jnp.zeros(sent_ref.shape, bf16)

    def pair(i, carry):
        sent_ref[pair_ref[i]] = (mine_ref[i] + arrived_ref[i].astype(f32)).astype(bf16)
        return carry

    lax.fori_loop(0, SEQ_PAIRS, pair, 0)


def latent_back_kernel(
    core_ref, back_ref, pre_ref, root_ref, gain_ref, cos_ref, sin_ref, grad_ref, gain_grad_ref
):
    total = jnp.zeros((64, KEYS), f32)
    for i in range(N_CTX):
        total = total + back_ref[i].astype(f32)
    normed_grad, pre, root = total[:, :RANK], pre_ref[...], root_ref[...]
    gain_grad_ref[...] = jnp.sum(normed_grad * pre * root, axis=0, keepdims=True)
    scaled = normed_grad * gain_ref[...]
    mean = jnp.sum(scaled * pre, axis=1, keepdims=True) * (1.0 / RANK)
    grad_ref[:, :RANK] = (root * scaled - pre * (root * root * root * mean)).astype(bf16)
    grad_ref[:, RANK:] = turned(total[:, RANK:], cos_ref[...], -sin_ref[...]).astype(bf16)


def input_back_kernel(
    core_ref, compressed_ref, down_ref, normed_ref, part_ref, input_ref, root_ref, gain_ref,
    logit_ref, normed_two_ref, gain_two_ref, gain_kv_ref,
    own_ref, send_ref, small_ref, total_ref,
):
    core, zl = core_ref[0], core_ref[1]
    quarter = quarter_at(zl, core)
    compressed = compressed_ref[...]
    total_ref[...] = part_ref[...]
    total_ref[:, quarter] += nn(compressed, down_ref[...])
    grad, source, root = total_ref[...], input_ref[...].astype(f32), root_ref[...]
    gain_one = jnp.sum(grad * source * root, axis=0, keepdims=True)
    scaled = grad * gain_ref[...]
    mean = jnp.sum(scaled * source, axis=1, keepdims=True) * (1.0 / WIDTH)
    total_ref[...] = root * scaled - source * (root * root * root * mean)
    for z in range(2):
        mine = slice(z * QUARTER, (z + 1) * QUARTER)
        own_ref[:, mine] = total_ref[:, quarter_at(z, core)]
        send_ref[:, mine] = total_ref[:, quarter_at(z, 1 - core)].astype(bf16)
    column = lax.broadcasted_iota(jnp.int32, (KEYS, N_CTX * 32), 1)
    place = (column >> 5) * 18 + (column & 31)
    same = (place == lax.broadcasted_iota(jnp.int32, place.shape, 0)) & ((column & 31) < 18)
    spread = nn(compressed, jnp.where(same, 1.0, 0.0).astype(bf16)).astype(bf16)
    down = tn(spread, normed_ref[:, quarter]).reshape(N_CTX, 32, QUARTER)
    router = nn(logit_ref[...], normed_two_ref[:, quarter])
    row = lax.broadcasted_iota(jnp.int32, down.shape, 1)
    small = down
    for e in range(EXP_DEV):
        small = jnp.where(row == 18 + e, router[e * N_CTX : (e + 1) * N_CTX][:, None, :], small)
    for k in range(4):
        part = slice(k * QUARTER, (k + 1) * QUARTER)
        small = jnp.where(row == 20 + k, gain_one[:, part][None], small)
        small = jnp.where(row == 24 + k, gain_two_ref[:, part][None], small)
    small = jnp.where(row == 28, gain_kv_ref[...][None], small)
    small_ref[...] = small.astype(bf16)


def expert_grads_kernel(
    core_ref, one_ref, one_other_ref, two_ref, two_other_ref, ga_ref, gb_ref,
    scaled_one_ref, dg_one_ref, du_one_ref, scaled_two_ref, dg_two_ref, du_two_ref,
    wg_ref, wu_ref, wd_ref,
):
    mine = lax.rem(pl.program_id(1), 2) == core_ref[0]
    rows = N_CTX * SLOTS
    grad = jnp.where(mine, ga_ref[...], gb_ref[...]).reshape(rows, QUARTER)
    for e, (own_ref, other_ref, scaled_ref, dg_ref, du_ref) in enumerate(
        (
            (one_ref, one_other_ref, scaled_one_ref, dg_one_ref, du_one_ref),
            (two_ref, two_other_ref, scaled_two_ref, dg_two_ref, du_two_ref),
        )
    ):

        @pl.when(pl.program_id(0) == e)
        def _(own_ref=own_ref, other_ref=other_ref, scaled_ref=scaled_ref, dg_ref=dg_ref,
              du_ref=du_ref):
            x = jnp.where(mine, own_ref[...], other_ref[...]).reshape(rows, QUARTER)
            wg_ref[0] = tn(dg_ref[...], x)
            wu_ref[0] = tn(du_ref[...], x)
            wd_ref[0] = tn(scaled_ref[...], grad)


def expert_grads(core, rows, grads, units):
    total = N_CTX * SLOTS
    first = pl.BlockSpec(
        (N_CTX, SLOTS, QUARTER), lambda e, q: (0, 0, jnp.where(e == 0, q // 2, 1))
    )
    second = pl.BlockSpec(
        (N_CTX, SLOTS, QUARTER), lambda e, q: (0, 0, jnp.where(e == 0, 0, q // 2))
    )
    grad = pl.BlockSpec((N_CTX, 1, SLOTS, QUARTER), lambda e, q: (0, e, 0, q // 2))
    unit = pl.BlockSpec((total, 352), lambda e, q: (0, 0))
    result = pl.BlockSpec((1, 352, QUARTER), lambda e, q: (e, 0, q))
    return pl.pallas_call(
        expert_grads_kernel,
        grid=(EXP_DEV, 4),
        in_specs=[pl.BlockSpec(memory_space=pltpu.SMEM), first, first, second, second, grad, grad]
        + [unit] * 6,
        out_specs=[result] * 3,
        out_shape=[out((EXP_DEV, 352, WIDTH), f32)] * 3,
        compiler_params=pltpu.CompilerParams(vmem_limit_bytes=56 * MIB),
        cost_estimate=pl.CostEstimate(
            flops=12 * total * WIDTH * 352, bytes_accessed=36 * MIB, transcendentals=0
        ),
        name="expert_grads",
    )(core, *rows, *grads, *units)


def combine_kernel(
    core_ref, one_ref, two_ref, slot_ref, own_ref, arrived_ref, half_ref, prob_ref
):
    half = own_ref[...] + arrived_ref[...].astype(f32)
    for e, back_ref in enumerate((one_ref, two_ref)):
        part = slice(e * N_CTX, (e + 1) * N_CTX)
        hot = one_hot(slot_ref[part])
        half = half + tn(hot.astype(bf16), back_ref[...].reshape(N_CTX * SLOTS, HALF))
        dots = column_of(back_ref[:, CAP, :], core_ref[1])
        prob_ref[part] = jnp.sum((hot * dots).reshape(N_CTX, SLOTS, TOK), axis=1)
    half_ref[...] = half.astype(bf16)


def outputs_two_kernel(core_ref, back_ref, slot_ref, probs_ref, own_ref, half_ref):
    hot = one_hot(slot_ref[...]).reshape(N_CTX, SLOTS, TOK) * probs_ref[...][:, None, :]
    hot = hot.reshape(N_CTX * SLOTS, TOK).astype(bf16)
    half_ref[...] = own_ref[...] + tn(hot, back_ref[...].reshape(N_CTX * SLOTS, HALF))


def outputs_kernel(core_ref, back_ref, slot_ref, probs_ref, own_ref, arrived_ref, half_ref):
    hot = one_hot(slot_ref[...]).reshape(N_CTX, SLOTS, TOK) * probs_ref[...][:, None, :]
    half = own_ref[...] + arrived_ref[...].astype(f32)
    half_ref[...] = half + tn(
        hot.reshape(N_CTX * SLOTS, TOK).astype(bf16), back_ref[...].reshape(N_CTX * SLOTS, HALF)
    )


def weight_rows(attn_ref, z, group, first, last):
    return attn_ref[group * 4 : group * 4 + 4, z, :, first:last].reshape(256, last - first)


def up_rows(attn_ref, z, head, first):
    rows = attn_ref[:, z, head * 16 : head * 16 + 16, first : first + 128]
    return rows.reshape(256, 128)


def turned(values, cos, sin):
    flipped = jnp.concatenate([values[:, ROPE // 2 :], values[:, : ROPE // 2]], axis=1)
    return values * cos + flipped * sin


def query_kernel(core_ref, normed_ref, attn_ref, cos_ref, sin_ref, query_ref, nope_ref):
    rows = jnp.zeros((TOK, 768), f32)
    for z in range(2):
        for group in range(4):
            place = (z * 4 + group) * 256
            rows = rows + nn(
                normed_ref[:, place : place + 256], weight_rows(attn_ref, z, group, 0, 768)
            )
    for h in range(HEADS):
        nope = rows[:, h * 192 : h * 192 + NOPE].astype(bf16)
        rope = turned(rows[:, h * 192 + NOPE : (h + 1) * 192], cos_ref[...], sin_ref[...])
        nope_ref[h] = nope
        for z in range(2):
            query_ref[h, :, z * 256 : (z + 1) * 256] = nt(
                nope, up_rows(attn_ref, z, h, 1280)
            ).astype(bf16)
        query_ref[h, :, RANK:] = rope.astype(bf16)


def attend_kernel(
    place_ref, q_ref, k_ref, attn_ref,
    out_ref, log_ref, flat_ref, own_ref, send_ref, top_ref, sum_ref, acc_ref,
):
    owner, chunk = pl.program_id(0), pl.program_id(1)
    place, core = place_ref[owner], place_ref[2]

    @pl.when(chunk == 0)
    def _():
        top_ref[...] = jnp.full(top_ref.shape, -1e30, f32)
        sum_ref[...] = jnp.zeros(sum_ref.shape, f32)
        acc_ref[...] = jnp.zeros(acc_ref.shape, f32)

    def visit(masked):
        k = k_ref[pl.ds(chunk * CHUNK, CHUNK), :]
        for group in range(2):
            part = slice(group * 256, (group + 1) * 256)
            q = q_ref[2 * group : 2 * group + 2].reshape(256, KEYS)
            scores = nt(q, k) * SCALE_TWO
            if masked:
                column = lax.broadcasted_iota(jnp.int32, scores.shape, 1) + chunk * CHUNK
                scores = jnp.where(column < (place + 1) * BLOCK, scores, -1e30)
            top_old = top_ref[part, :1]
            top = jnp.maximum(top_old, jnp.max(scores, axis=1, keepdims=True))
            weights = jnp.exp2(scores - top)
            fade = jnp.exp2(top_old - top)
            total = sum_ref[part, :1] * fade + jnp.sum(weights, axis=1, keepdims=True)
            acc_ref[part] = acc_ref[part] * fade + nn(weights.astype(bf16), k[:, :RANK])
            top_ref[part] = jnp.broadcast_to(top, (256, 128))
            sum_ref[part] = jnp.broadcast_to(total, (256, 128))

    first = chunk * (CHUNK // BLOCK)
    whole = place >= first + CHUNK // BLOCK - 1
    pl.when(whole)(lambda: visit(False))
    pl.when((place >= first) & jnp.logical_not(whole))(lambda: visit(True))

    @pl.when(chunk == pl.num_programs(1) - 1)
    def _():
        total = sum_ref[...][:, :1]
        value = acc_ref[...] / total
        out_ref[...] = value.reshape(out_ref.shape)
        log_ref[...] = (top_ref[...] + jnp.log2(sum_ref[...])).reshape(log_ref.shape)
        value = value.astype(bf16)
        for h in range(HEADS):
            rows = value[h * BLOCK : (h + 1) * BLOCK]
            head = nn(rows[:, :256], up_rows(attn_ref, 0, h, 1408))
            head = head + nn(rows[:, 256:], up_rows(attn_ref, 1, h, 1408))
            flat_ref[:, h * VDIM : (h + 1) * VDIM] = head.astype(bf16)
        flat = flat_ref[...]
        for z in range(2):
            mine = slice(z * QUARTER, (z + 1) * QUARTER)
            weight = attn_ref[pl.ds(core * 8, 8), z, :, 768:1280].reshape(QUARTER, QUARTER)
            own_ref[:, mine] = nt(flat, weight)
            weight = attn_ref[pl.ds(8 - core * 8, 8), z, :, 768:1280].reshape(QUARTER, QUARTER)
            send_ref[:, mine] = nt(flat, weight).astype(bf16)


def attend(places, query, keys, attn_all):
    rows = HEADS * BLOCK
    tokens = pl.BlockSpec((BLOCK, HALF), lambda o, c, p: (o, 0))
    return pl.pallas_call(
        attend_kernel,
        grid_spec=pltpu.PrefetchScalarGridSpec(
            num_scalar_prefetch=1,
            grid=(2, SEQ_BLOCKS * BLOCK // CHUNK),
            in_specs=[
                pl.BlockSpec((HEADS, 1, BLOCK, KEYS), lambda o, c, p: (0, o, 0, 0)),
                pl.BlockSpec((SEQ_BLOCKS * BLOCK, KEYS), lambda o, c, p: (0, 0)),
                pl.BlockSpec((16, 2, 64, 1536), lambda o, c, p: (0, 0, 0, 0)),
            ],
            out_specs=[
                pl.BlockSpec((HEADS, 1, BLOCK, RANK), lambda o, c, p: (0, o, 0, 0)),
                pl.BlockSpec((HEADS, 1, BLOCK, BLOCK), lambda o, c, p: (0, o, 0, 0)),
                pl.BlockSpec((BLOCK, HEADS * VDIM), lambda o, c, p: (o, 0)),
                tokens,
                tokens,
            ],
            scratch_shapes=[
                pltpu.VMEM((rows, 128), f32),
                pltpu.VMEM((rows, 128), f32),
                pltpu.VMEM((rows, RANK), f32),
            ],
        ),
        out_shape=[
            out((HEADS, 2, BLOCK, RANK), f32),
            out((HEADS, 2, BLOCK, BLOCK), f32),
            out((TOK, HEADS * VDIM), bf16),
            out((TOK, HALF), f32),
            out((TOK, HALF), bf16),
        ],
        compiler_params=pltpu.CompilerParams(vmem_limit_bytes=40 * MIB),
        cost_estimate=pl.CostEstimate(
            flops=2 * 2 * rows * 1280 * (KEYS + RANK), bytes_accessed=16 * MIB, transcendentals=0
        ),
        name="attend",
    )(places, query, keys, attn_all)


def back_kernel(
    core, own_ref, other_ref, sum_own_ref, sum_other_ref, input_ref, root_ref, gain_ref,
    grad_ref, router_ref, probs_ref, prob_grad_ref, attn_ref,
    after_grad_ref, attn_grad_ref, logit_ref, gain_grad_ref, head_ref, latent_ref,
):
    probs, prob_grad = probs_ref[...], prob_grad_ref[...]
    inner = jnp.sum(probs * prob_grad, axis=0, keepdims=True)
    logit_grad = (probs * (prob_grad - inner)).astype(bf16)
    logit_ref[...] = logit_grad
    after = input_ref[...].astype(f32) + whole_value(sum_own_ref[...], sum_other_ref[...], core)
    normed_grad = whole_value(own_ref[...], other_ref[...], core)
    normed_grad = normed_grad + tn(logit_grad, router_ref[...])
    root = root_ref[:, :1]
    gain_grad_ref[...] = jnp.sum(normed_grad * after * root, axis=0, keepdims=True)
    scaled = normed_grad * gain_ref[...]
    mean = jnp.sum(scaled * after, axis=1, keepdims=True) * (1.0 / WIDTH)
    after_grad = grad_ref[...].astype(f32) + root * scaled - after * (root * root * root * mean)
    after_grad_ref[...] = after_grad
    attn_grad = after_grad.astype(bf16)
    attn_grad_ref[...] = attn_grad
    head = jnp.zeros((TOK, QUARTER), f32)
    for z in range(2):
        for group in range(4):
            place = (z * 4 + group) * 256
            head = head + nn(
                attn_grad[:, place : place + 256], weight_rows(attn_ref, z, group, 768, 1280)
            )
    head = head.astype(bf16)
    head_ref[...] = head
    for h in range(HEADS):
        for z in range(2):
            latent_ref[h, :, z * 256 : (z + 1) * 256] = nt(
                head[:, h * VDIM : (h + 1) * VDIM], up_rows(attn_ref, z, h, 1408)
            ).astype(bf16)


def query_back_kernel(
    core_ref, dq_ref, nope_ref, normed_ref, attn_ref, cos_ref, sin_ref,
    value_ref, head_ref, attn_grad_ref, flat_ref, sums_ref, back_ref,
):
    parts = []
    for h in range(HEADS):
        lat = dq_ref[h, :, :RANK].astype(bf16)
        nope = nn(lat[:, :256], up_rows(attn_ref, 0, h, 1280))
        nope = nope + nn(lat[:, 256:], up_rows(attn_ref, 1, h, 1280))
        parts += [nope, turned(dq_ref[h, :, RANK:], cos_ref[...], -sin_ref[...])]
        heads = slice(h * 16, h * 16 + 16)
        key_grad = tn(lat, nope_ref[h]).astype(bf16)
        value_grad = tn(value_ref[h].astype(bf16), head_ref[:, h * VDIM : (h + 1) * VDIM])
        value_grad = value_grad.astype(bf16)
        for z in range(2):
            rows = slice(z * 256, (z + 1) * 256)
            sums_ref[:, z, heads, 1280:1408] = key_grad[rows].reshape(16, 16, 128)
            sums_ref[:, z, heads, 1408:1536] = value_grad[rows].reshape(16, 16, 128)
    query_grad = jnp.concatenate(parts, axis=1).astype(bf16)
    flat = flat_ref[...]
    for z in range(2):
        for group in range(4):
            place = slice((z * 4 + group) * 256, (z * 4 + group + 1) * 256)
            where = slice(group * 4, group * 4 + 4)
            sums_ref[where, z, :, :768] = (
                tn(normed_ref[:, place], query_grad).astype(bf16).reshape(4, 64, 768)
            )
            sums_ref[where, z, :, 768:1280] = (
                tn(attn_grad_ref[:, place], flat).astype(bf16).reshape(4, 64, QUARTER)
            )
            back_ref[:, place] = nt(query_grad, weight_rows(attn_ref, z, group, 0, 768))


def attend_back_kernel(
    place_ref, in_own_ref, in_other_ref, sum_own_ref, sum_other_ref, input_ref, root_ref, gain_ref,
    grad_ref, router_ref, probs_ref, prob_grad_ref, attn_ref, q_ref, k_ref, out_ref, log_ref,
    after_grad_ref, attn_grad_ref, logit_ref, gain_grad_ref, head_ref,
    dq_ref, own_ref, send_ref, latent_ref, inner_ref, dk_ref,
):
    owner, chunk = pl.program_id(0), pl.program_id(1)
    place, core = place_ref[owner], place_ref[2]
    rows = HEADS * BLOCK

    @pl.when((owner == 0) & (chunk == 0))
    def _():
        dk_ref[...] = jnp.zeros(dk_ref.shape, f32)
        back_kernel(
            core, in_own_ref, in_other_ref, sum_own_ref, sum_other_ref, input_ref, root_ref,
            gain_ref, grad_ref, router_ref, probs_ref, prob_grad_ref, attn_ref,
            after_grad_ref, attn_grad_ref, logit_ref, gain_grad_ref, head_ref, latent_ref,
        )

    tokens = pl.ds(pl.multiple_of(owner * BLOCK, BLOCK), BLOCK)

    @pl.when(chunk == 0)
    def _():
        dq_ref[...] = jnp.zeros(dq_ref.shape, f32)
        grad = latent_ref[:, tokens, :].reshape(rows, RANK)
        inner = jnp.sum(
            grad.astype(f32) * out_ref[...].reshape(rows, RANK), axis=1, keepdims=True
        )
        inner_ref[...] = jnp.broadcast_to(inner, inner_ref.shape)

    def visit(masked):
        part = pl.ds(chunk * CHUNK, CHUNK)
        k = k_ref[part, :]
        q = q_ref[...].reshape(rows, KEYS)
        grad = latent_ref[:, tokens, :].reshape(rows, RANK)
        scores = nt(q, k) * SCALE_TWO
        probs = jnp.exp2(scores - log_ref[...].reshape(rows, BLOCK)[:, :1])
        if masked:
            column = lax.broadcasted_iota(jnp.int32, scores.shape, 1) + chunk * CHUNK
            probs = jnp.where(column < (place + 1) * BLOCK, probs, 0.0)
        prob_back = nt(grad, k[:, :RANK])
        score_grad = ((probs * SCALE) * (prob_back - inner_ref[...][:, :1])).astype(bf16)
        dq_ref[...] += nn(score_grad, k).reshape(dq_ref.shape)
        dk_ref[part, :] += tn(score_grad, q)
        dk_ref[part, :RANK] += tn(probs.astype(bf16), grad)

    first = chunk * (CHUNK // BLOCK)
    whole = place >= first + CHUNK // BLOCK - 1
    pl.when(whole)(lambda: visit(False))
    pl.when((place >= first) & jnp.logical_not(whole))(lambda: visit(True))

    @pl.when((owner == 1) & (chunk == pl.num_programs(1) - 1))
    def _():
        def block(i, carry):
            start = i * BLOCK
            own_ref[i] = dk_ref[pl.ds(pl.multiple_of(start + core * 64, 64), 64), :].astype(bf16)
            send_ref[i] = dk_ref[
                pl.ds(pl.multiple_of(start + (1 - core) * 64, 64), 64), :
            ].astype(bf16)
            return carry

        lax.fori_loop(0, SEQ_BLOCKS, block, 0)


def attend_back(places, *arrays):
    rows = HEADS * BLOCK

    def whole(array):
        zeros = (0,) * len(array.shape)
        return pl.BlockSpec(
            array.shape, lambda o, c, p: zeros, pipeline_mode=pl.Buffered(buffer_count=1)
        )

    def per_owner(width):
        return pl.BlockSpec((HEADS, 1, BLOCK, width), lambda o, c, p: (0, o, 0, 0))

    results = [
        out((TOK, WIDTH), f32),
        out((TOK, WIDTH), bf16),
        out((EXPERTS, TOK), bf16),
        out((1, WIDTH), f32),
        out((TOK, QUARTER), bf16),
    ]
    halves = [out((SEQ_BLOCKS, 64, KEYS), bf16)] * 2
    return pl.pallas_call(
        attend_back_kernel,
        grid_spec=pltpu.PrefetchScalarGridSpec(
            num_scalar_prefetch=1,
            grid=(2, SEQ_BLOCKS * BLOCK // CHUNK),
            in_specs=[whole(a) for a in arrays[:12]]
            + [per_owner(KEYS), whole(arrays[13]), per_owner(RANK), per_owner(BLOCK)],
            out_specs=[whole(a) for a in results] + [per_owner(KEYS)] + [whole(a) for a in halves],
            scratch_shapes=[
                pltpu.VMEM((HEADS, TOK, RANK), bf16),
                pltpu.VMEM((rows, 128), f32),
                pltpu.VMEM((SEQ_BLOCKS * BLOCK, KEYS), f32),
            ],
        ),
        out_shape=results + [out((HEADS, 2, BLOCK, KEYS), f32)] + halves,
        compiler_params=pltpu.CompilerParams(vmem_limit_bytes=58 * MIB),
        cost_estimate=pl.CostEstimate(
            flops=2 * 2 * rows * 1280 * 5 * KEYS, bytes_accessed=36 * MIB, transcendentals=0
        ),
        name="attend_back",
    )(places, *arrays)


def on_device(
    hidden_in,
    grad_out,
    block_ids,
    expert_ids,
    claim_order,
    attn_gain,
    latent_gain,
    ffn_gain,
    query_weight,
    latent_down,
    latent_up,
    output_weight,
    router_weight,
    expert_gate,
    expert_up,
    expert_down,
    shared_gate,
    shared_up,
    shared_down,
):
    ctx = lax.axis_index(CTX)
    zl = lax.axis_index("zl")
    core = lax.axis_index("core")
    ws = zl * 2 + core
    column_start = ws * QUARTER

    gains = jnp.concatenate([attn_gain, latent_gain, ffn_gain])
    gains = gather_two(gather_two(gains, "core", 0), "zl", 0).reshape(-1)
    small = jnp.concatenate(
        [
            latent_down.T,
            router_weight.T,
            jnp.pad(gains, (0, QUARTER - gains.shape[0]))[None],
            jnp.zeros((3, QUARTER), bf16),
        ],
        axis=0,
    )
    small_all = share_ctx(small, "small_weights")
    down_t = small_all[:, :18].reshape(KEYS, QUARTER)
    gains_all = small_all[:, 20, : 4 * 36].reshape(N_CTX, 4, 36).astype(f32)
    gain_one = gains_all[..., :16].reshape(-1)
    gain_kv = gains_all[..., 16:20].reshape(-1)
    gain_two = gains_all[..., 20:].reshape(-1)
    router_mine = small_all[:, 18:20]

    up_mine = latent_up.reshape(16, HEADS, NOPE + VDIM).transpose(1, 0, 2).reshape(64, NOPE + VDIM)
    dense_mine = jnp.concatenate(
        [query_weight, output_weight.T, up_mine, shared_gate, shared_up, shared_down.T], axis=1
    )
    dense_other = after(swap(dense_mine, "zh"), small)
    first = lax.axis_index("zh") == 0
    dense_mine = jnp.stack(
        [jnp.where(first, dense_mine, dense_other), jnp.where(first, dense_other, dense_mine)]
    )
    with jax.named_scope("dense_weights"):
        dense_all = lax.all_gather(dense_mine, ("y", "x"), tiled=False)
    attn_all, shared_all = dense_all[..., :1536], dense_all[..., 1536:]

    core_is = jnp.stack([core, ctx])
    slot_by, grad_sent = call(
        cotangents_kernel,
        [out((EXPERTS, TOK), f32), out((N_CTX, EXP_DEV, SLOTS, HALF), bf16)],
        "cotangents",
        4 * N_CTX * SLOTS * TOK * HALF,
    )(
        core_is,
        jnp.pad(expert_ids.T, ((0, 2), (0, 0)), constant_values=-1),
        claim_order.reshape(1, TOK),
        claim_order.reshape(TOK, 1),
        grad_out,
    )

    local_ids = lax.dynamic_slice_in_dim(block_ids, ctx * 2, 2)
    places = local_ids % SEQ_BLOCKS
    sequence = local_ids[0] // SEQ_BLOCKS
    positions = (places[:, None] * BLOCK + jnp.arange(BLOCK)[None, :]).reshape(-1)
    pair_ids = block_ids.reshape(N_CTX, 2)
    in_seq = (pair_ids[:, 0] // SEQ_BLOCKS) == sequence
    rank = jnp.cumsum(in_seq.astype(jnp.int32)) - 1
    is_pair = in_seq[None, :] & (rank[None, :] == jnp.arange(SEQ_PAIRS)[:, None])
    pairs = jnp.sum(jnp.where(is_pair, jnp.arange(N_CTX)[None, :], 0), axis=1)
    pair_places = pair_ids[pairs] % SEQ_BLOCKS
    place_of = pair_places.T.reshape(-1)
    slot_of = jnp.sum(
        jnp.where(
            place_of[None, :] == jnp.arange(SEQ_BLOCKS)[:, None],
            jnp.arange(SEQ_BLOCKS)[None, :],
            0,
        ),
        axis=1,
    )

    inputs = hidden_in.astype(f32)
    root_one = lax.rsqrt(jnp.mean(inputs * inputs, axis=-1, keepdims=True) + EPSILON)
    normed_one = (inputs * root_one * gain_one).astype(bf16)
    normed_quarter = lax.dynamic_slice_in_dim(normed_one, column_start, QUARTER, 1)
    compressed_part = nt(normed_quarter, down_t).reshape(2, 2, 64, KEYS)
    compressed_half = pick(compressed_part, core, 1) + swap(
        pick(compressed_part, 1 - core, 1), "core"
    )
    compressed = pick(compressed_half, zl, 0) + swap(pick(compressed_half, 1 - zl, 0), "zl")
    row_start = ws * 64
    my_positions = lax.dynamic_slice_in_dim(positions, row_start, 64)
    latent_pre = compressed[:, :RANK]
    root_kv = lax.rsqrt(jnp.mean(latent_pre * latent_pre, axis=-1, keepdims=True) + EPSILON)
    latent_rows = jnp.concatenate(
        [
            (latent_pre * root_kv * gain_kv).astype(bf16),
            rotate(compressed[:, RANK:], my_positions, 1.0).astype(bf16),
        ],
        axis=1,
    )
    frequency = ROPE_BASE ** (-2.0 * jnp.arange(ROPE // 2, dtype=f32) / ROPE)
    angles = positions.astype(f32)[:, None] * frequency[None, :]
    cos = jnp.cos(angles)
    sin = jnp.sin(angles)
    cos, sin = jnp.concatenate([cos, cos], axis=1), jnp.concatenate([-sin, sin], axis=1)
    key_slots = jnp.concatenate([slot_of, jnp.stack([zl, core])])
    latent_ctx = after(share_ctx(latent_rows, "latents"), (grad_sent, cos, sin, key_slots))
    latent_mine = latent_ctx[pairs]
    latent_zl = swap(latent_mine, "zl")
    latent_core = swap(jnp.stack([latent_mine, latent_zl]), "core")
    router_zl = swap(router_mine, "zl")
    router_core = swap(jnp.concatenate([router_mine, router_zl], axis=1), "core")
    (router_t,) = call(router_kernel, [out((EXPERTS, WIDTH), bf16)], "router", 1)(
        jnp.stack([core, zl]), router_mine, router_zl, router_core
    )
    (keys,) = call(keys_kernel, [out((SEQ_BLOCKS * BLOCK, KEYS), bf16)], "keys", 1)(
        key_slots, latent_mine, latent_zl, latent_core
    )

    query, query_nope = call(
        query_kernel,
        [out((HEADS, TOK, KEYS), bf16), out((HEADS, TOK, NOPE), bf16)],
        "queries",
        2 * TOK * 768 * (WIDTH + RANK),
    )(core_is, normed_one, attn_all, cos, sin)
    query = query.reshape(HEADS, 2, BLOCK, KEYS)
    grad_own = exchange_ctx(grad_sent, "cotangent_rows", (latent_core, router_core))
    grad_other = swap(grad_own, "core")
    places_core = jnp.concatenate([places, core[None]])
    value, log_total, head_flat, attn_own, attn_send = attend(places_core, after(query, router_t), keys, attn_all)
    attn_half = zl_sum(attn_own + swap(attn_send, "core").astype(f32))
    attn_other = swap(attn_half, "core")

    gain_row = gain_two.reshape(1, WIDTH)
    buffer = out((N_CTX, SLOTS, HALF), bf16)
    normed_two, root_two, probs, sent_one, sent_two = call(
        middle_kernel,
        [
            out((TOK, WIDTH), bf16),
            out((TOK, 128), f32),
            out((EXPERTS, TOK), f32),
            buffer,
            buffer,
        ],
        "middle",
        4 * N_CTX * SLOTS * TOK * HALF,
    )(core_is, attn_half, attn_other, hidden_in, gain_row, router_t, slot_by)

    weights = (expert_gate.transpose(0, 2, 1), expert_up.transpose(0, 2, 1), expert_down)
    one = exchange_ctx(sent_one, "rows_to_experts", grad_own)
    two = exchange_ctx(sent_two, "rows_to_experts", one)
    shared_own, shared_send, in_own, in_send, shared_grads = shared(
        core_is, normed_two, grad_out, shared_all
    )
    one = after(one, in_own)
    one_other = swap(one, "core")
    back_own, back_send, y_one, y_one_send, *units_one = expert(
        0, core_is, one, one_other, grad_own, grad_other, *weights
    )
    two = after(two, units_one[0])
    two_other = swap(two, "core")
    (sent_one,) = call(add_kernel, [buffer], "finish_rows", 1, limit=20)(
        core_is, after(back_own, two), swap(back_send, "core")
    )
    back_one = exchange_ctx(sent_one, "row_grads_back", two)
    back_own, back_send, y_two, y_two_send, *units_two = expert(
        1, core_is, two, two_other, grad_own, grad_other, *weights
    )
    (sent_two,) = call(add_kernel, [buffer], "finish_rows", 1, limit=20)(
        core_is, back_own, swap(after(back_send, back_one), "core")
    )
    back_two = exchange_ctx(sent_two, "row_grads_back", back_one)

    (outs_one,) = call(add_kernel, [buffer], "outputs_sum", 1)(
        core_is, after(y_one, sent_two), swap(y_one_send, "core")
    )
    back_two = after(back_two, outs_one)

    in_half, prob_grad = call(
        combine_kernel,
        [out((TOK, HALF), bf16), out((EXPERTS, TOK), f32)],
        "combine",
        4 * N_CTX * SLOTS * TOK * HALF,
    )(core_is, back_one, back_two, slot_by, in_own, swap(in_send, "core"))
    prob_grad = prob_grad + swap(prob_grad, "zl")
    in_half = in_half.astype(f32) + swap(in_half, "zl").astype(f32)
    in_other = swap(in_half, "core")
    outs_one = exchange_ctx(after(outs_one, (in_other, prob_grad)), "outputs_back")
    (
        after_grad, attn_grad, logit_grad, gain_two_part, head_grad,
        grad_query_lat, keys_own, keys_send,
    ) = attend_back(
        places_core, in_half, in_other, attn_half, attn_other, hidden_in, root_two, gain_row,
        grad_out, router_t, probs, prob_grad, attn_all, query, keys, value, log_total,
    )
    grad_query_lat = grad_query_lat.reshape(HEADS, TOK, KEYS)

    attn_parts, normed_one_part = call(
        query_back_kernel,
        [out((16, 2, 64, 1536), bf16), out((TOK, WIDTH), f32)],
        "query_back",
        2 * TOK * WIDTH * 2048 + 2 * TOK * RANK * 1536,
        limit=48,
    )(
        core_is, after(grad_query_lat, outs_one), query_nope, normed_one, attn_all, cos, sin,
        value.reshape(HEADS, TOK, RANK), head_grad, attn_grad, head_flat,
    )

    keys_mine, keys_other = call(
        key_split_kernel,
        [out((SEQ_PAIRS, 64, KEYS), f32), out((SEQ_PAIRS, 64, KEYS), bf16)],
        "key_split",
        1,
    )(jnp.concatenate([place_of, zl[None]]), after(keys_own, outs_one), swap(keys_send, "core"))
    keys_arrived = swap(keys_other, "zl")
    (keys_sent,) = call(key_spread_kernel, [out((N_CTX, 64, KEYS), bf16)], "key_spread", 1)(
        pairs, keys_mine, after(keys_arrived, normed_one_part)
    )
    (outs_two,) = call(add_kernel, [buffer], "outputs_sum", 1)(
        core_is, after(y_two, keys_sent), swap(y_two_send, "core")
    )
    keys_back = exchange_ctx(keys_sent, "key_grads")

    half_out = out((TOK, HALF), f32)
    (routed_half,) = call(outputs_kernel, [half_out], "outputs", 1)(
        core_is, after(outs_one, keys_sent), slot_by[:N_CTX], probs[:N_CTX],
        shared_own, swap(shared_send, "core"),
    )
    shared_pair = scatter_yx(
        after(shared_grads, sent_two).reshape(WIDTH, 3 * FF_SH), "shared_weight_grads"
    )
    attn_pair = scatter_yx(
        after(attn_parts, (shared_pair, keys_sent)).reshape(WIDTH, 1536), "attn_weight_grads"
    )
    shared_sum = scatter_zh(shared_pair, "shared_weight_grads")

    filled = expert_grads(
        core_is, (one, one_other, two, two_other), (grad_own, grad_other),
        (after(units_one[0], keys_sent), *units_one[1:], *units_two),
    )
    grad_expert_gate = filled[0].transpose(0, 2, 1)
    grad_expert_up = filled[1].transpose(0, 2, 1)
    grad_expert_down = filled[2]

    keys_back = after(keys_back, (routed_half, shared_sum, filled[0], outs_two))
    compressed_grad, gain_kv_part = call(
        latent_back_kernel, [out((64, KEYS), bf16), out((1, RANK), f32)], "latent_back", 1
    )(
        core_is, keys_back, latent_pre, root_kv, gain_kv.reshape(1, RANK),
        lax.dynamic_slice_in_dim(cos, row_start, 64), lax.dynamic_slice_in_dim(sin, row_start, 64),
    )
    compressed_grad = gather_two(gather_two(compressed_grad, "core", 0), "zl", 0).reshape(TOK, KEYS)
    outs_two = exchange_ctx(after(outs_two, compressed_grad), "outputs_back")
    input_own, input_send, small_parts = call(
        input_back_kernel,
        [
            out((TOK, HALF), f32),
            out((TOK, HALF), bf16),
            out((N_CTX, 32, QUARTER), bf16),
        ],
        "input_back",
        4 * TOK * KEYS * QUARTER,
        [pltpu.VMEM((TOK, WIDTH), f32)],
    )(
        jnp.stack([core, zl]), compressed_grad, down_t, normed_one, normed_one_part, hidden_in,
        root_one, gain_one.reshape(1, WIDTH), logit_grad, normed_two, gain_two_part, gain_kv_part,
    )
    input_quarter = zl_quarter(input_own + swap(input_send, "core").astype(f32), zl)
    grad_in = lax.dynamic_slice_in_dim(after_grad, column_start, QUARTER, 1) + input_quarter

    attn_sum = scatter_zh(attn_pair, "attn_weight_grads")
    (routed_half,) = call(outputs_two_kernel, [half_out], "outputs_two", 1)(
        core_is, outs_two, slot_by[N_CTX:], probs[N_CTX:], routed_half
    )
    layer_out = (
        lax.dynamic_slice_in_dim(hidden_in, column_start, QUARTER, 1).astype(f32)
        + lax.dynamic_slice_in_dim(attn_half, zl * QUARTER, QUARTER, 1)
        + zl_quarter(routed_half, zl)
    ).astype(bf16)
    small_back = exchange_ctx(small_parts, "small_weight_grads", outs_two)
    small_back = after(small_back, (attn_sum, layer_out, grad_in))
    small_sum = jnp.sum(small_back.astype(f32), axis=0)
    lane = lax.rem(ctx, 8) * 64
    gain_one_rows = lax.dynamic_slice(small_sum, (20 + ctx // 8, lane), (1, 64))
    gain_two_rows = lax.dynamic_slice(small_sum, (24 + ctx // 8, lane), (1, 64))
    gain_kv_rows = lax.dynamic_slice(small_sum, (28, ctx * 16), (1, 16))
    gain_parts = jnp.concatenate(
        [gain_one_rows.reshape(2, 2, 16), gain_kv_rows.reshape(2, 2, 4)], axis=-1
    )
    gain_core = pick(gain_parts, core, 1) + swap(pick(gain_parts, 1 - core, 1), "core")
    gain_mine = pick(gain_core, zl, 0) + swap(pick(gain_core, 1 - zl, 0), "zl")
    gain_two_mine = lax.dynamic_slice_in_dim(gain_two_rows[0], ws * 16, 16)

    up_sum = (
        attn_sum[:, 768 + QUARTER :]
        .reshape(HEADS, 16, NOPE + VDIM)
        .transpose(1, 0, 2)
        .reshape(16, HEADS * (NOPE + VDIM))
    )
    return (
        layer_out,
        grad_in,
        gain_mine[:16],
        gain_mine[16:],
        gain_two_mine,
        attn_sum[:, :768],
        small_sum[:18].T,
        up_sum,
        attn_sum[:, 768 : 768 + QUARTER].T,
        small_sum[18:20].T,
        grad_expert_gate,
        grad_expert_up,
        grad_expert_down,
        shared_sum[:, :FF_SH],
        shared_sum[:, FF_SH : 2 * FF_SH],
        shared_sum[:, 2 * FF_SH :].T,
    )


def solution(mesh):
    grid = Mesh(mesh.devices.reshape(2, 4, 4, 2, 2), CTX + ("zl", "core"))
    ctx, ws, both = CTX, ("zl", "core"), CTX + ("zl", "core")
    placed = (
        P(ctx, None),
        P(ctx, None),
        P(),
        P(ctx, None),
        P(ctx),
        P(both),
        P(both),
        P(both),
        P(ctx, ws),
        P(ws, ctx),
        P(ctx, ws),
        P(ws, ctx),
        P(ws, ctx),
        P(ctx, None, ws),
        P(ctx, None, ws),
        P(ctx, ws, None),
        P(ctx, ws),
        P(ctx, ws),
        P(ws, ctx),
    )
    return jax.shard_map(
        on_device,
        mesh=grid,
        in_specs=placed,
        out_specs=(
            P(ctx, ws),
            P(ctx, ws),
            P(both),
            P(both),
            P(both),
            P(ctx, ws),
            P(ws, ctx),
            P(ctx, ws),
            P(ws, ctx),
            P(ws, ctx),
            P(ctx, None, ws),
            P(ctx, None, ws),
            P(ctx, ws, None),
            P(ctx, ws),
            P(ctx, ws),
            P(ws, ctx),
        ),
        check_vma=False,
    )
```
